512 devices in a mesh: dp: 2 (over z_hi), context: 32 (over x, z_lo, core), tensor: 8 (over y).
Axes of the slice: x: 4, y: 8, z: 8 (z_hi: 2, z_lo: 4; z = z_hi * 4 + z_lo), core: 2. Of those that a mesh axis runs over, the one named last changes fastest.
Arguments:
- query_branch: bfloat16 [2, 4096, 4096], P('dp', 'context', 'tensor'), may hold values from -6 to 6
- key_branch: bfloat16 [2, 4096, 4096], P('dp', 'context', 'tensor'), may hold values from -6 to 6
- value_branch: bfloat16 [2, 4096, 4096], P('dp', 'context', 'tensor'), may hold values from -6 to 6
- cotangent: bfloat16 [2, 4096, 8192], P('dp', ('context', 'tensor')), may hold values from -6 to 6
- out_weight: bfloat16 [8192, 4096], P(('dp', 'context'), 'tensor'), may hold values from -0.0625 to 0.0625
- filters: bfloat16 [256, 128], P('tensor'), may hold values from -0.5 to 0.5
Outputs:
- query_grad: bfloat16 [2, 4096, 4096], P('dp', 'context', 'tensor')
- key_grad: bfloat16 [2, 4096, 4096], P('dp', 'context', 'tensor')
- value_grad: bfloat16 [2, 4096, 4096], P('dp', 'context', 'tensor')
- filter_grad: float32 [256, 128], P('tensor')
The draws below stay inside these ranges and needn't reach their ends.
All inputs are finite; a program needn't handle non-finite values.
Results may differ from the reference program's by a relative error of at most 0.0051.
Values may be sent and summed in bfloat16 or wider, within the bound.
No kernel may reach another device: no remote copies, remote signals or barrier semaphores. Data moves between devices by JAX's collectives and lax.ppermute only.
A program may use at most 64 MiB of HBM per device.

```python
import math
import jax
import jax.numpy as jnp
from jax import lax

D = 8192
C = 4096
GROUP = 16
TAPS = 128
LEN = 4096
SEQS = 2
FILTERS = 256


def level_of(rng, dims, split, smallest, top_value):
    gain = 1.0
    for dim, parts in split:
        steps = jax.random.uniform(jax.random.fold_in(jax.random.fold_in(rng, 6), dim), (parts,), jnp.float32, smallest / len(split), top_value / len(split))
        gain = gain * jnp.repeat(jnp.exp(steps), dims[dim] // parts).reshape((-1,) + (1,) * (len(dims) - 1 - dim))
    return gain


def bell_draw(stream_key, dims, spread, bound, split=(), kind=jnp.bfloat16):
    factor_of = level_of(stream_key, dims, split, -0.22, 0.18) if split else 1.0
    entries = jax.random.normal(stream_key, dims, jnp.float32) * spread * factor_of
    return jnp.minimum(jnp.maximum(entries, -bound), bound).astype(kind)


def setup_inputs(seed: int = 0) -> dict:
    seeds = jax.random.split(jax.random.key(seed), 7)
    return {
        "query_branch": bell_draw(seeds[0], (SEQS, LEN, C), 1.0, 6.0, ((0, 2), (1, 32), (2, 8))),
        "key_branch": bell_draw(seeds[1], (SEQS, LEN, C), 1.0, 6.0, ((0, 2), (1, 32), (2, 8))),
        "value_branch": bell_draw(seeds[2], (SEQS, LEN, C), 1.0, 6.0, ((0, 2), (1, 32), (2, 8))),
        "cotangent": bell_draw(seeds[3], (SEQS, LEN, D), 1.0, 6.0, ((0, 2), (1, 256))),
        "out_weight": bell_draw(seeds[4], (D, C), D ** -0.5, 0.0625, ((0, 64), (1, 8))),
        "filters": bell_draw(seeds[5], (FILTERS, TAPS), TAPS ** -0.5, 0.5, ((0, 8),)),
    }


def toeplitz_table(filters):
    taps = filters.shape[1]
    row_index = jnp.arange(taps, dtype=jnp.int32)[:, None]
    col_index = jnp.arange(2 * taps, dtype=jnp.int32)[None, :]
    lag_index = row_index + taps - col_index
    valid = (lag_index >= 0) & (lag_index < taps)
    padded = jnp.concatenate([filters, jnp.zeros((filters.shape[0], 1), filters.dtype)], 1)
    return jnp.take(padded, jnp.where(valid, lag_index, taps).astype(jnp.int32), axis=1)

def windows_of(rows, blocks, taps, groups, group):
    first = rows[:blocks * taps].reshape(blocks, taps, groups, group)
    second = rows[taps:].reshape(blocks, taps, groups, group)
    return jnp.concatenate([first, second], 1)

def reference(query_branch, key_branch, value_branch, cotangent, out_weight, filters):
    groups = filters.shape[0]
    table = toeplitz_table(filters)
    upper = jnp.concatenate([table[:, :, TAPS:], table[:, :, :TAPS]], 1)
    blocks = LEN // TAPS
    query_list, key_list, value_list = ([], [], [])
    outer = jnp.zeros((groups, TAPS, 2 * TAPS), jnp.float32)
    for seq in range(SEQS):
        keys = key_branch[seq].astype(jnp.float32)
        values = value_branch[seq].astype(jnp.float32)
        mixed = (keys * values).astype(jnp.bfloat16)
        rows = jnp.concatenate([jnp.zeros((TAPS, C), jnp.bfloat16), mixed], 0)
        windows = windows_of(rows, blocks, TAPS, groups, GROUP)
        conv = jnp.einsum('gim,bmgs->bigs', table.astype(jnp.float32), windows.astype(jnp.float32)).reshape(LEN, C)
        branch_grad = jnp.dot(cotangent[seq], out_weight, preferred_element_type=jnp.float32)
        query_list.append((branch_grad * conv).astype(jnp.bfloat16))
        conv_grad = (branch_grad * query_branch[seq].astype(jnp.float32)).astype(jnp.bfloat16)
        grad_rows = jnp.concatenate([conv_grad, jnp.zeros((TAPS, C), jnp.bfloat16)], 0)
        grad_windows = windows_of(grad_rows, blocks, TAPS, groups, GROUP)
        mixed_grad = jnp.einsum('gim,bigs->bmgs', upper.astype(jnp.float32), grad_windows.astype(jnp.float32)).reshape(LEN, C)
        key_list.append((mixed_grad * values).astype(jnp.bfloat16))
        value_list.append((mixed_grad * keys).astype(jnp.bfloat16))
        outer = outer + jnp.einsum('bigs,bmgs->gim', conv_grad.reshape(blocks, TAPS, groups, GROUP).astype(jnp.float32), windows.astype(jnp.float32))
    lag_index = (jnp.arange(TAPS, dtype=jnp.int32)[:, None] + TAPS - jnp.arange(TAPS, dtype=jnp.int32)[None, :]).astype(jnp.int32)
    lag_sum = lax.optimization_barrier(jnp.sum(jnp.take_along_axis(outer, jnp.broadcast_to(lag_index[None], (groups, TAPS, TAPS)), axis=2), axis=1))
    filter_grad = lag_sum / math.sqrt(SEQS * LEN * GROUP)
    return (jnp.stack(query_list), jnp.stack(key_list), jnp.stack(value_list), filter_grad)
```

```python
import math

import jax
import jax.numpy as jnp
from jax import lax
from jax.sharding import Mesh, PartitionSpec as P

GROUP = 16
TAPS = 128
F32 = jnp.float32
BF16 = jnp.bfloat16

X = ("xh", "xp")
Z = ("zh", "zl")
CONTEXT = ("xh", "xp", "zl", "co")


def swap(block, axis):
    return lax.ppermute(block, axis, [(0, 1), (1, 0)])


def from_behind(block, distance):
    n = lax.axis_size(CONTEXT)
    route = [(i - distance, i) for i in range(n) if 0 <= i - distance < n]
    return lax.ppermute(block, CONTEXT, route)


def exchange_copies(block, axes):
    n = lax.axis_size(axes)
    copies = jnp.broadcast_to(block[None], (n,) + block.shape)
    return lax.all_to_all(copies, axes, split_axis=0, concat_axis=0)


def toeplitz_table(filters):
    groups = filters.shape[0]
    taps = filters.shape[1]
    reversed_taps = filters[:, ::-1]
    period = jnp.concatenate([reversed_taps, jnp.zeros((groups, taps + 1), filters.dtype)], 1)
    tiled = jnp.tile(period, (1, taps))
    flat = jnp.concatenate([jnp.zeros((groups, 1), filters.dtype), tiled], 1)[:, : 2 * taps * taps]
    return flat.reshape(groups, taps, 2 * taps)


def lag_totals(outer):
    groups = outer.shape[0]
    taps = outer.shape[1]
    flat = outer.reshape(groups, taps * 2 * taps)
    flat = jnp.concatenate([flat, jnp.zeros((groups, taps), F32)], 1)
    skewed = flat.reshape(groups, taps, 2 * taps + 1)
    column_sums = jnp.sum(skewed, axis=1)
    return column_sums[:, taps:0:-1]


def windows_of(rows, blocks, taps, groups, group):
    first = rows[: blocks * taps].reshape(blocks, taps, groups, group)
    second = rows[taps:].reshape(blocks, taps, groups, group)
    return jnp.concatenate([first, second], 1)


def branch_gradient(cotangent, out_weight):
    rows = cotangent.shape[0]
    width = out_weight.shape[1]
    depth = out_weight.shape[0]
    parts = cotangent.reshape(rows, 2, 4, 4, 2, depth).transpose(2, 4, 0, 1, 3, 5)
    parts = parts.reshape(8, rows, 8 * depth)
    parts = lax.all_to_all(parts, X + ("co",), split_axis=0, concat_axis=0)
    gathered = lax.all_gather(parts, "y", axis=0)
    weights = exchange_copies(out_weight, Z).reshape(8 * depth, width)
    partial = jnp.einsum("ybrk,kn->byrn", gathered, weights, preferred_element_type=F32)
    partial = partial.reshape(4, 2, 8 * rows, width)
    co = lax.axis_index("co")
    mine = lax.dynamic_index_in_dim(partial, co, 1, keepdims=False)
    other = lax.dynamic_index_in_dim(partial, 1 - co, 1, keepdims=False)
    summed = (mine + swap(other, "co")).astype(BF16)
    terms = lax.all_to_all(summed, X, split_axis=0, concat_axis=0)
    return jnp.sum(terms.astype(F32), axis=0)


def local(query_branch, key_branch, value_branch, cotangent, out_weight, filters):
    tokens = query_branch.shape[1]
    width = query_branch.shape[2]
    groups = filters.shape[0]
    blocks = tokens // TAPS
    keys = key_branch[0].astype(F32)
    values = value_branch[0].astype(F32)
    mixed = (keys * values).astype(BF16)
    before = from_behind(mixed[tokens - (TAPS - 1) :], 1)
    rows = jnp.concatenate([jnp.zeros((1, width), BF16), before, mixed], 0)
    windows = windows_of(rows, blocks, TAPS, groups, GROUP)
    table = toeplitz_table(filters)
    conv = jnp.einsum("gim,bmgs->bigs", table, windows, preferred_element_type=F32).reshape(tokens, width)
    branch_grad = branch_gradient(cotangent[0], out_weight)
    query_grad = (branch_grad * conv).astype(BF16)
    conv_grad = (branch_grad * query_branch[0].astype(F32)).astype(BF16)
    after = from_behind(conv_grad[: TAPS - 1], -1)
    outer = jnp.einsum(
        "bigs,bmgs->gim",
        conv_grad.reshape(blocks, TAPS, groups, GROUP),
        windows,
        preferred_element_type=F32,
    )
    lags = lag_totals(outer)
    lags = lags + swap(lags, "co")
    lag_sum = jnp.sum(exchange_copies(lags, ("zh", "xh", "xp", "zl")), axis=0)
    grad_rows = jnp.concatenate([conv_grad, after, jnp.zeros((1, width), BF16)], 0)
    grad_windows = windows_of(grad_rows, blocks, TAPS, groups, GROUP)
    upper = jnp.concatenate([table[:, :, TAPS:], table[:, :, :TAPS]], 1)
    mixed_grad = jnp.einsum("gim,bigs->bmgs", upper, grad_windows, preferred_element_type=F32).reshape(tokens, width)
    key_grad = (mixed_grad * values).astype(BF16)
    value_grad = (mixed_grad * keys).astype(BF16)
    scale = 1.0 / math.sqrt(2 * lax.axis_size(CONTEXT) * tokens * GROUP)
    filter_grad = lag_sum * scale
    return (query_grad[None], key_grad[None], value_grad[None], filter_grad)


def solution(mesh):
    fine = Mesh(mesh.devices.reshape(2, 2, 2, 4, 2, 8), ("zh", "xh", "xp", "zl", "co", "y"))
    branch = P("zh", CONTEXT, "y")
    return jax.shard_map(
        local,
        mesh=fine,
        in_specs=(
            branch,
            branch,
            branch,
            P("zh", CONTEXT + ("y",), None),
            P(("zh",) + CONTEXT, "y"),
            P("y", None),
        ),
        out_specs=(branch, branch, branch, P("y", None)),
        check_vma=False,
    )
```

```python
import math

import jax
import jax.numpy as jnp
from jax import lax
from jax.experimental import pallas as pl
from jax.experimental.pallas import tpu as pltpu
from jax.sharding import Mesh, PartitionSpec as P

GROUP = 16
TAPS = 128
LANES = 128
PER = LANES // GROUP
F32 = jnp.float32
BF16 = jnp.bfloat16

X = ("xh", "xp")
Z = ("zh", "zl")
CONTEXT = ("xh", "xp", "zl", "co")
VMEM = pltpu.CompilerParams(vmem_limit_bytes=32 * 1024 * 1024)


def swap(block, axis):
    return lax.ppermute(block, axis, [(0, 1), (1, 0)])


def in_order(mine, theirs, axis):
    first = lax.axis_index(axis) == 0
    return jnp.stack([jnp.where(first, mine, theirs), jnp.where(first, theirs, mine)])


def from_behind(block, distance):
    n = lax.axis_size(CONTEXT)
    route = [(i - distance, i) for i in range(n) if 0 <= i - distance < n]
    return lax.ppermute(block, CONTEXT, route)


def sum_over(block, axes):
    n = lax.axis_size(axes)
    copies = jnp.broadcast_to(block[None], (n,) + block.shape)
    return jnp.sum(lax.all_to_all(copies, axes, split_axis=0, concat_axis=0), axis=0)


def shifted_rows(row):
    return pltpu.roll(jnp.broadcast_to(row, (TAPS, 2 * TAPS)), 0, 1, stride=1, stride_axis=0)


def lane_group(shape):
    return lax.broadcasted_iota(jnp.int32, shape, 1) >> 4


def filtered(rows_ref, window):
    owner = lane_group((TAPS, LANES))
    total = jnp.zeros((TAPS, LANES), F32)
    for g in range(PER):
        table = shifted_rows(rows_ref[g : g + 1, :]).astype(BF16)
        term = jnp.dot(table, window, preferred_element_type=F32)
        total = jnp.where(owner == g, term, total)
    return total


def conv_kernel(rows_ref, window_ref, conv_ref):
    conv_ref[...] = filtered(rows_ref, window_ref[...])


def mixed_grad_kernel(rows_ref, grad_ref, after_ref, key_ref, value_ref, key_grad_ref, value_grad_ref):
    window = jnp.concatenate([grad_ref[...], after_ref[...]], 0)
    mixed_grad = filtered(rows_ref, window)
    key_grad_ref[...] = (mixed_grad * value_ref[...].astype(F32)).astype(BF16)
    value_grad_ref[...] = (mixed_grad * key_ref[...].astype(F32)).astype(BF16)


def regroup(blocks):
    rows = blocks[0].shape[0]
    group = lane_group((rows, LANES))
    for bit in (1, 2):
        low = (group & bit) == 0
        out = list(blocks)
        for b in range(4):
            if b & bit:
                continue
            x0, x1 = blocks[b], blocks[b | bit]
            out[b] = jnp.where(low, x0, pltpu.roll(x1, GROUP * bit, 1))
            out[b | bit] = jnp.where(low, pltpu.roll(x0, LANES - GROUP * bit, 1), x1)
        blocks = out
    return blocks


def window_kernel(window_ref, out_ref):
    n = 2 * TAPS
    across = lax.broadcasted_iota(jnp.int32, (n, n), 0) + lax.broadcasted_iota(jnp.int32, (n, n), 1)
    turn = (across == n - 1).astype(F32).astype(BF16)
    turned = [jnp.dot(turn, window_ref[b], preferred_element_type=F32) for b in range(4)]
    for a, block in enumerate(regroup(turned)):
        out_ref[a] = block.astype(BF16)


def lag_kernel(mine_ref, other_ref, query_ref, window_ref, lag_ref):
    grads = [mine_ref[0], mine_ref[1], other_ref[0], other_ref[1]]
    grads = [g * query_ref[b].astype(F32) for b, g in enumerate(grads)]
    half = lax.broadcasted_iota(jnp.int32, (TAPS, LANES), 1) >> 6
    for a, block in enumerate(regroup(grads)):
        for h in range(2):
            part = jnp.where(half == h, block, 0.0).astype(BF16)
            outer = lax.dot_general(part, window_ref[a], (((1,), (1,)), ((), ())), preferred_element_type=F32)
            skewed = pltpu.roll(outer, 1, 1, stride=1, stride_axis=0)
            sums = jnp.sum(skewed, axis=0, keepdims=True)
            lag_ref[4 * h + a : 4 * h + a + 1, :] = sums[:, TAPS:]


def product_kernel(place_ref, cot_ref, *refs):
    weights, (mine_ref, other_ref) = refs[:-2], refs[-2:]
    start = place_ref[0]
    core = place_ref[1]
    depth = weights[0].shape[0]
    pieces = []
    for weight_ref, step, part in zip(weights, (0, 1, 7, 2, 6, 3, 5, 4, 4), (None,) * 7 + (0, 1)):
        column = lax.rem(start + step, 8) * depth
        size = depth
        if part is not None:
            size = depth // 2
            column = column + part * size
        pieces.append((pl.multiple_of(column, LANES), size, weight_ref))
    for out_ref, c in ((other_ref, 1 - core), (mine_ref, core)):
        for p in range(2):
            rows = pl.ds(pl.multiple_of((2 * p + c) * TAPS, TAPS), TAPS)
            total = jnp.zeros(out_ref.shape[1:], F32)
            for column, size, weight_ref in pieces:
                total += jnp.dot(cot_ref[rows, pl.ds(column, size)], weight_ref[...], preferred_element_type=F32)
            out_ref[p] = total


def lane_blocks(*lead):
    return pl.BlockSpec(lead + (LANES,), lambda l: (0,) * len(lead) + (l,))


def convolve(rows, window):
    width = window.shape[1]
    return pl.pallas_call(
        conv_kernel,
        grid=(width // LANES,),
        in_specs=[pl.BlockSpec((PER, 2 * TAPS), lambda l: (l, 0)), lane_blocks(2 * TAPS)],
        out_specs=lane_blocks(TAPS),
        out_shape=jax.ShapeDtypeStruct((TAPS, width), F32),
        compiler_params=VMEM,
        name="conv",
    )(rows, window)


def mixed_gradient(rows, grad, after, keys, values):
    width = grad.shape[1]
    tile = lane_blocks(TAPS)
    return pl.pallas_call(
        mixed_grad_kernel,
        grid=(width // LANES,),
        in_specs=[pl.BlockSpec((PER, 2 * TAPS), lambda l: (l, 0)), tile, tile, tile, tile],
        out_specs=[tile, tile],
        out_shape=[jax.ShapeDtypeStruct((TAPS, width), BF16)] * 2,
        compiler_params=VMEM,
        name="mixed_grad",
    )(rows, grad, after, keys, values)


def turned_windows(windows):
    width = windows.shape[2]
    return pl.pallas_call(
        window_kernel,
        grid=(width // LANES,),
        in_specs=[lane_blocks(4, 2 * TAPS)],
        out_specs=lane_blocks(4, 2 * TAPS),
        out_shape=jax.ShapeDtypeStruct(windows.shape, BF16),
        compiler_params=VMEM,
        name="windows",
    )(windows)


def lag_totals(mine, other, queries, windows):
    width = mine.shape[2]
    return pl.pallas_call(
        lag_kernel,
        grid=(width // LANES,),
        in_specs=[lane_blocks(2, TAPS), lane_blocks(2, TAPS), lane_blocks(4, TAPS), lane_blocks(4, 2 * TAPS)],
        out_specs=pl.BlockSpec((PER, TAPS), lambda l: (l, 0)),
        out_shape=jax.ShapeDtypeStruct((width // GROUP, TAPS), F32),
        compiler_params=VMEM,
        name="lags",
    )(mine, other, queries, windows)


def partial_products(cotangent, weights):
    width = weights[0].shape[1]
    place = jnp.stack([lax.axis_index(Z), lax.axis_index("co")]).astype(jnp.int32)
    whole = pl.BlockSpec(memory_space=pltpu.VMEM)
    out = jax.ShapeDtypeStruct((2, TAPS, width), F32)
    return pl.pallas_call(
        product_kernel,
        in_specs=[pl.BlockSpec(memory_space=pltpu.SMEM)] + [whole] * (1 + len(weights)),
        out_specs=[whole, whole],
        out_shape=[out, out],
        compiler_params=VMEM,
        name="product",
    )(place, cotangent, *weights)


def cotangent_columns(cotangent):
    rows, width = cotangent.shape
    depth = width // 64
    parts = cotangent.reshape(rows, 2, 2, 2, 4, 2, depth).transpose(3, 5, 0, 1, 4, 2, 6)
    parts = parts.reshape(4, 1, rows, 16 * depth)
    copies = jnp.broadcast_to(parts, (4, 8, rows, 16 * depth)).reshape(32, rows, 16 * depth)
    return lax.all_to_all(copies, ("xp", "co", "y"), split_axis=0, concat_axis=0).reshape(32 * rows, 16 * depth)


def weight_blocks(out_weight):
    depth, width = out_weight.shape
    own = in_order(out_weight, swap(out_weight, "xh"), "xh").reshape(2 * depth, width)
    n = 8
    up = [(i, (i + 1) % n) for i in range(n)]
    down = [(i, (i - 1) % n) for i in range(n)]
    blocks = [own]
    ahead = behind = own
    for _ in range(3):
        ahead = lax.ppermute(ahead, Z, down)
        behind = lax.ppermute(behind, Z, up)
        blocks += [ahead, behind]
    blocks.append(lax.ppermute(ahead[:depth], Z, down))
    blocks.append(lax.ppermute(behind[depth:], Z, up))
    return blocks


def local(query_branch, key_branch, value_branch, cotangent, out_weight, filters):
    query, keys, values = query_branch[0], key_branch[0], value_branch[0]
    tokens, width = query.shape
    groups = filters.shape[0]
    gathered = cotangent_columns(cotangent[0])
    weights = weight_blocks(out_weight)

    mixed = (keys.astype(F32) * values.astype(F32)).astype(BF16)
    before = from_behind(mixed, 1)
    window = jnp.concatenate([before, mixed], 0)
    taps = filters.astype(F32)
    zero = jnp.zeros((groups, TAPS), F32)
    rows = jnp.concatenate([taps, zero], 1)
    turned_rows = jnp.concatenate([zero[:, :1], taps[:, ::-1], zero[:, 1:]], 1)
    conv = convolve(turned_rows, window)

    saved = jnp.concatenate([query, window], 0)
    saved = in_order(saved, swap(saved, "xp"), "xp")
    saved = jnp.concatenate([saved, swap(saved, "co")], 0)
    queries = saved[:, :tokens]
    windows = turned_windows(saved[:, tokens:])

    mine, other = partial_products(gathered, weights)
    lags = lag_totals(mine, other, queries, windows)
    lag_sum = sum_over(sum_over(lags, X + ("co",)), Z)
    filter_grad = lag_sum * (1.0 / math.sqrt(2 * lax.axis_size(CONTEXT) * tokens * GROUP))

    summed = mine + swap(other, "co")
    xp = lax.axis_index("xp")
    keep = lax.dynamic_index_in_dim(summed, xp, 0, keepdims=False)
    give = lax.dynamic_index_in_dim(summed, 1 - xp, 0, keepdims=False)
    branch_grad = keep + swap(give.astype(BF16), "xp").astype(F32)
    query_grad = (branch_grad * conv).astype(BF16)
    conv_grad = (branch_grad * query.astype(F32)).astype(BF16)
    after = from_behind(conv_grad, -1)
    key_grad, value_grad = mixed_gradient(rows, conv_grad, after, keys, values)
    return (query_grad[None], key_grad[None], value_grad[None], filter_grad)


def solution(mesh):
    fine = Mesh(mesh.devices.reshape(2, 2, 2, 4, 2, 8), ("zh", "xh", "xp", "zl", "co", "y"))
    branch = P("zh", CONTEXT, "y")
    return jax.shard_map(
        local,
        mesh=fine,
        in_specs=(
            branch,
            branch,
            branch,
            P("zh", CONTEXT + ("y",), None),
            P(("zh",) + CONTEXT, "y"),
            P("y", None),
        ),
        out_specs=(branch, branch, branch, P("y", None)),
        check_vma=False,
    )
```

```python
import math

import jax
import jax.numpy as jnp
from jax import lax
from jax.experimental import pallas as pl
from jax.experimental.pallas import tpu as pltpu
from jax.sharding import Mesh, PartitionSpec as P

GROUP = 16
TAPS = 128
LANES = 128
PER = LANES // GROUP
F32 = jnp.float32
BF16 = jnp.bfloat16

Z = ("zh", "zm", "zp")
PAIRS = ("zh", "zm")
CONTEXT = ("x", "zm", "zp", "co")
VMEM = pltpu.CompilerParams(vmem_limit_bytes=32 * 1024 * 1024)


def swap(block, axis):
    return lax.ppermute(block, axis, [(0, 1), (1, 0)])


def in_order(mine, theirs, axis):
    first = lax.axis_index(axis) == 0
    return jnp.stack([jnp.where(first, mine, theirs), jnp.where(first, theirs, mine)])


def from_behind(block, distance):
    n = lax.axis_size(CONTEXT)
    route = [(i - distance, i) for i in range(n) if 0 <= i - distance < n]
    return lax.ppermute(block, CONTEXT, route)


def sum_over(block, axes):
    n = lax.axis_size(axes)
    copies = jnp.broadcast_to(block[None], (n,) + block.shape)
    return jnp.sum(lax.all_to_all(copies, axes, split_axis=0, concat_axis=0), axis=0)


def shifted_rows(row):
    return pltpu.roll(jnp.broadcast_to(row, (TAPS, 2 * TAPS)), 0, 1, stride=1, stride_axis=0)


def lane_group(shape):
    return lax.broadcasted_iota(jnp.int32, shape, 1) >> 4


def filtered(rows_ref, window):
    owner = lane_group((TAPS, LANES))
    total = jnp.zeros((TAPS, LANES), F32)
    for g in range(PER):
        table = shifted_rows(rows_ref[g : g + 1, :]).astype(BF16)
        term = jnp.dot(table, window, preferred_element_type=F32)
        total = jnp.where(owner == g, term, total)
    return total


def conv_kernel(rows_ref, window_ref, conv_ref):
    conv_ref[...] = filtered(rows_ref, window_ref[...])


def mixed_grad_kernel(rows_ref, grad_ref, after_ref, key_ref, value_ref, key_grad_ref, value_grad_ref):
    window = jnp.concatenate([grad_ref[...], after_ref[...]], 0)
    mixed_grad = filtered(rows_ref, window)
    key_grad_ref[...] = (mixed_grad * value_ref[...].astype(F32)).astype(BF16)
    value_grad_ref[...] = (mixed_grad * key_ref[...].astype(F32)).astype(BF16)


def regroup(blocks):
    rows = blocks[0].shape[0]
    group = lane_group((rows, LANES))
    for bit in (1, 2):
        low = (group & bit) == 0
        out = list(blocks)
        for b in range(4):
            if b & bit:
                continue
            x0, x1 = blocks[b], blocks[b | bit]
            out[b] = jnp.where(low, x0, pltpu.roll(x1, GROUP * bit, 1))
            out[b | bit] = jnp.where(low, pltpu.roll(x0, LANES - GROUP * bit, 1), x1)
        blocks = out
    return blocks


def window_kernel(window_ref, out_ref):
    n = 2 * TAPS
    across = lax.broadcasted_iota(jnp.int32, (n, n), 0) + lax.broadcasted_iota(jnp.int32, (n, n), 1)
    turn = (across == n - 1).astype(F32).astype(BF16)
    turned = [jnp.dot(turn, window_ref[b], preferred_element_type=F32) for b in range(4)]
    for a, block in enumerate(regroup(turned)):
        out_ref[a] = block.astype(BF16)


def lag_kernel(mine_ref, other_ref, query_ref, window_ref, lag_ref):
    grads = [mine_ref[0], mine_ref[1], other_ref[0], other_ref[1]]
    grads = [g * query_ref[b].astype(F32) for b, g in enumerate(grads)]
    half = lax.broadcasted_iota(jnp.int32, (TAPS, LANES), 1) >> 6
    for a, block in enumerate(regroup(grads)):
        for h in range(2):
            part = jnp.where(half == h, block, 0.0).astype(BF16)
            outer = lax.dot_general(part, window_ref[a], (((1,), (1,)), ((), ())), preferred_element_type=F32)
            skewed = pltpu.roll(outer, 1, 1, stride=1, stride_axis=0)
            sums = jnp.sum(skewed, axis=0, keepdims=True)
            lag_ref[4 * h + a : 4 * h + a + 1, :] = sums[:, TAPS:]


PIECES = ((0, (0, 1, 3, 2)), (1, (0, 1, 3, 2)), (3, (0, 1, 3, 2)), (2, (0, 1)), (2, (3, 2)))


def product_kernel(place_ref, cot_hbm, *refs):
    count = len(PIECES)
    weights_hbm, (mine_ref, other_ref, cot_ref), rest = refs[:count], refs[count : count + 3], refs[count + 3 :]
    weights, (cot_sem, weight_sems) = rest[:count], rest[count:]
    copies = [pltpu.make_async_copy(cot_hbm, cot_ref, cot_sem)]
    for i in range(count):
        copies.append(pltpu.make_async_copy(weights_hbm[i], weights[i], weight_sems.at[i]))
    for copy in copies:
        copy.start()
    x, pair, core = place_ref[0], place_ref[1], place_ref[2]
    copies[0].wait()
    for i, (x_step, z_steps) in enumerate(PIECES):
        copies[1 + i].wait()
        weight = weights[i][...]
        first = lax.rem(x + x_step, 4) * 4
        columns = [pl.multiple_of((first + lax.rem(pair + z, 4)) * TAPS, TAPS) for z in z_steps]
        for out_ref, c in ((other_ref, 1 - core), (mine_ref, core)):
            for p in range(2):
                rows = pl.ds(pl.multiple_of((2 * p + c) * TAPS, TAPS), TAPS)
                part = jnp.concatenate([cot_ref[rows, pl.ds(column, TAPS)] for column in columns], 1)
                term = jnp.dot(part, weight, preferred_element_type=F32)
                out_ref[p] = term if i == 0 else out_ref[p] + term


def lane_blocks(*lead):
    return pl.BlockSpec(lead + (LANES,), lambda l: (0,) * len(lead) + (l,))


def convolve(rows, window):
    width = window.shape[1]
    return pl.pallas_call(
        conv_kernel,
        grid=(width // LANES,),
        in_specs=[pl.BlockSpec((PER, 2 * TAPS), lambda l: (l, 0)), lane_blocks(2 * TAPS)],
        out_specs=lane_blocks(TAPS),
        out_shape=jax.ShapeDtypeStruct((TAPS, width), F32),
        compiler_params=VMEM,
        name="conv",
    )(rows, window)


def mixed_gradient(rows, grad, after, keys, values):
    width = grad.shape[1]
    tile = lane_blocks(TAPS)
    return pl.pallas_call(
        mixed_grad_kernel,
        grid=(width // LANES,),
        in_specs=[pl.BlockSpec((PER, 2 * TAPS), lambda l: (l, 0)), tile, tile, tile, tile],
        out_specs=[tile, tile],
        out_shape=[jax.ShapeDtypeStruct((TAPS, width), BF16)] * 2,
        compiler_params=VMEM,
        name="mixed_grad",
    )(rows, grad, after, keys, values)


def turned_windows(windows):
    width = windows.shape[2]
    return pl.pallas_call(
        window_kernel,
        grid=(width // LANES,),
        in_specs=[lane_blocks(4, 2 * TAPS)],
        out_specs=lane_blocks(4, 2 * TAPS),
        out_shape=jax.ShapeDtypeStruct(windows.shape, BF16),
        compiler_params=VMEM,
        name="windows",
    )(windows)


def lag_totals(mine, other, queries, windows):
    width = mine.shape[2]
    return pl.pallas_call(
        lag_kernel,
        grid=(width // LANES,),
        in_specs=[lane_blocks(2, TAPS), lane_blocks(2, TAPS), lane_blocks(4, TAPS), lane_blocks(4, 2 * TAPS)],
        out_specs=pl.BlockSpec((PER, TAPS), lambda l: (l, 0)),
        out_shape=jax.ShapeDtypeStruct((width // GROUP, TAPS), F32),
        compiler_params=VMEM,
        name="lags",
    )(mine, other, queries, windows)


def partial_products(cotangent, weights):
    width = weights[0].shape[1]
    place = [lax.axis_index("x"), lax.axis_index(PAIRS), lax.axis_index("co")]
    place = jnp.stack(place).astype(jnp.int32)
    whole = pl.BlockSpec(memory_space=pltpu.VMEM)
    out = jax.ShapeDtypeStruct((2, TAPS, width), F32)
    return pl.pallas_call(
        product_kernel,
        in_specs=[pl.BlockSpec(memory_space=pltpu.SMEM)] + [pl.BlockSpec(memory_space=pl.ANY)] * (1 + len(weights)),
        out_specs=[whole, whole],
        out_shape=[out, out],
        scratch_shapes=[pltpu.VMEM(a.shape, a.dtype) for a in (cotangent, *weights)]
        + [pltpu.SemaphoreType.DMA, pltpu.SemaphoreType.DMA((len(weights),))],
        compiler_params=VMEM,
        name="product",
    )(place, cotangent, *weights)


def cotangent_columns(cotangent):
    rows, width = cotangent.shape
    depth = width // 64
    parts = cotangent.reshape(rows, 2, 4, 2, 2, 2, depth).transpose(4, 5, 0, 2, 1, 3, 6)
    parts = parts.reshape(4, 1, rows, 16 * depth)
    copies = jnp.broadcast_to(parts, (4, 8, rows, 16 * depth)).reshape(32, rows, 16 * depth)
    gathered = lax.all_to_all(copies, ("zp", "co", "y"), split_axis=0, concat_axis=0)
    return copies, gathered.reshape(32 * rows, 16 * depth)


def turn(block, axes, distance):
    n = lax.axis_size(axes)
    return lax.ppermute(block, axes, [((i + distance) % n, i) for i in range(n)])


def weight_blocks(out_weight):
    near = [out_weight, turn(out_weight, PAIRS, 1), turn(out_weight, PAIRS, -1), turn(out_weight, PAIRS, 2)]
    near = jnp.concatenate(near, 0)
    half = near.shape[0] // 2
    ahead, behind = turn(near, "x", 1), turn(near, "x", -1)
    return near, [near, ahead, behind, turn(ahead[:half], "x", 1), turn(behind[half:], "x", -1)]


def local(query_branch, key_branch, value_branch, cotangent, out_weight, filters):
    query, keys, values = query_branch[0], key_branch[0], value_branch[0]
    tokens, width = query.shape
    groups = filters.shape[0]
    copies, gathered = cotangent_columns(cotangent[0])
    out_weight, _ = lax.optimization_barrier((out_weight, copies))
    near, weights = weight_blocks(out_weight)

    keys, near = lax.optimization_barrier((keys, near))
    mixed = (keys.astype(F32) * values.astype(F32)).astype(BF16)
    before = from_behind(mixed, 1)
    window = jnp.concatenate([before, mixed], 0)
    taps = filters.astype(F32)
    zero = jnp.zeros((groups, TAPS), F32)
    rows = jnp.concatenate([taps, zero], 1)
    turned_rows = jnp.concatenate([zero[:, :1], taps[:, ::-1], zero[:, 1:]], 1)
    conv = convolve(turned_rows, window)

    saved = jnp.concatenate([query, window], 0)
    saved = in_order(saved, swap(saved, "zp"), "zp")
    saved = jnp.concatenate([saved, swap(saved, "co")], 0)
    queries = saved[:, :tokens]
    windows = turned_windows(saved[:, tokens:])

    gathered, conv, windows, queries, rows = lax.optimization_barrier((gathered, conv, windows, queries, rows))
    mine, other = partial_products(gathered, weights)
    lags = lag_totals(mine, other, queries, windows)
    summed = mine + swap(other, "co")
    zp = lax.axis_index("zp")
    keep = lax.dynamic_index_in_dim(summed, zp, 0, keepdims=False)
    give = lax.dynamic_index_in_dim(summed, 1 - zp, 0, keepdims=False).astype(BF16)

    lag_sum = sum_over(lags, ("x", "co"))
    lag_sum, give = lax.optimization_barrier((lag_sum, give))
    lag_sum = sum_over(lag_sum, Z)
    filter_grad = lag_sum * (1.0 / math.sqrt(2 * lax.axis_size(CONTEXT) * tokens * GROUP))

    branch_grad = keep + swap(give, "zp").astype(F32)
    query_grad = (branch_grad * conv).astype(BF16)
    conv_grad = (branch_grad * query.astype(F32)).astype(BF16)
    after = from_behind(conv_grad, -1)
    key_grad, value_grad = mixed_gradient(rows, conv_grad, after, keys, values)
    return (query_grad[None], key_grad[None], value_grad[None], filter_grad)


def solution(mesh):
    fine = Mesh(mesh.devices.reshape(2, 4, 2, 2, 2, 8), ("zh", "x", "zm", "zp", "co", "y"))
    branch = P("zh", CONTEXT, "y")
    return jax.shard_map(
        local,
        mesh=fine,
        in_specs=(
            branch,
            branch,
            branch,
            P("zh", CONTEXT + ("y",), None),
            P(("zh",) + CONTEXT, "y"),
            P("y", None),
        ),
        out_specs=(branch, branch, branch, P("y", None)),
        check_vma=False,
    )
```

```python
import math

import jax
import jax.numpy as jnp
from jax import lax
from jax.experimental import pallas as pl
from jax.experimental.pallas import tpu as pltpu
from jax.sharding import Mesh, PartitionSpec as P

GROUP = 16
TAPS = 128
LANES = 128
PER = LANES // GROUP
F32 = jnp.float32
BF16 = jnp.bfloat16

Z = ("zh", "zl")
CONTEXT = ("xh", "xp", "zl", "co")
VMEM = pltpu.CompilerParams(vmem_limit_bytes=8 * 1024 * 1024)


def swap(block, axis):
    return lax.ppermute(block, axis, [(0, 1), (1, 0)])


def in_order(mine, theirs, axis):
    first = lax.axis_index(axis) == 0
    return jnp.stack([jnp.where(first, mine, theirs), jnp.where(first, theirs, mine)])


def from_behind(block, distance):
    n = lax.axis_size(CONTEXT)
    route = [(i - distance, i) for i in range(n) if 0 <= i - distance < n]
    return lax.ppermute(block, CONTEXT, route)


def sum_over(block, axes):
    n = lax.axis_size(axes)
    copies = jnp.broadcast_to(block[None], (n,) + block.shape)
    return jnp.sum(lax.all_to_all(copies, axes, split_axis=0, concat_axis=0), axis=0)


def shifted_rows(row):
    return pltpu.roll(jnp.broadcast_to(row, (TAPS, 2 * TAPS)), 0, 1, stride=1, stride_axis=0)


def lane_group(shape):
    return lax.broadcasted_iota(jnp.int32, shape, 1) >> 4


def filtered(rows_ref, window):
    owner = lane_group((TAPS, LANES))
    total = jnp.zeros((TAPS, LANES), F32)
    for g in range(PER):
        table = shifted_rows(rows_ref[g : g + 1, :]).astype(BF16)
        term = jnp.dot(table, window, preferred_element_type=F32)
        total = jnp.where(owner == g, term, total)
    return total


def conv_kernel(rows_ref, window_ref, conv_ref):
    conv_ref[...] = filtered(rows_ref, window_ref[...])


def mixed_grad_kernel(rows_ref, grad_ref, after_ref, key_ref, value_ref, key_grad_ref, value_grad_ref):
    window = jnp.concatenate([grad_ref[...], after_ref[...]], 0)
    mixed_grad = filtered(rows_ref, window)
    key_grad_ref[...] = (mixed_grad * value_ref[...].astype(F32)).astype(BF16)
    value_grad_ref[...] = (mixed_grad * key_ref[...].astype(F32)).astype(BF16)


def regroup(first, second):
    low = (lane_group(first.shape) & 1) == 0
    even = jnp.where(low, first, pltpu.roll(second, GROUP, 1))
    odd = jnp.where(low, pltpu.roll(first, LANES - GROUP, 1), second)
    return even, odd


def window_kernel(window_ref, out_ref):
    n = 2 * TAPS
    across = lax.broadcasted_iota(jnp.int32, (n, n), 0) + lax.broadcasted_iota(jnp.int32, (n, n), 1)
    turn = (across == n - 1).astype(F32).astype(BF16)
    turned = [jnp.dot(turn, window_ref[b], preferred_element_type=F32) for b in range(2)]
    for a, block in enumerate(regroup(*turned)):
        out_ref[a] = block.astype(BF16)


def lag_kernel(keep_ref, give_ref, query_ref, window_ref, lag_ref):
    keep = keep_ref[...] * query_ref[0].astype(F32)
    give = give_ref[...].astype(F32) * query_ref[1].astype(F32)
    quarter = lax.broadcasted_iota(jnp.int32, (TAPS, LANES), 1) >> 5
    for a, block in enumerate(regroup(keep, give)):
        for q in range(4):
            part = jnp.where(quarter == q, block, 0.0).astype(BF16)
            outer = lax.dot_general(part, window_ref[a], (((1,), (1,)), ((), ())), preferred_element_type=F32)
            skewed = pltpu.roll(outer, 1, 1, stride=1, stride_axis=0)
            sums = jnp.sum(skewed, axis=0, keepdims=True)
            lag_ref[2 * q + a : 2 * q + a + 1, :] = sums[:, TAPS:]


def product_kernel(place_ref, cot_ref, *refs):
    weights, (keep_ref, give_ref) = refs[:-2], refs[-2:]
    z, core, xp = place_ref[0], place_ref[1], place_ref[2]
    depth = weights[0].shape[0]
    pieces = [(z, 0)]
    for step in (1, 2, 3):
        below, above = lax.rem(z + 8 - step, 8), lax.rem(z + step, 8)
        pieces += [(jnp.where(core == 0, below, above), 0), (jnp.where(core == 0, above, below), 0)]
    far = lax.rem(z + 4, 8)
    pieces += [(far, jnp.where(core == 0, 0, depth // 2)), (far, jnp.where(core == 0, depth // 2, 0))]
    for out_ref, p in ((give_ref, 1 - xp), (keep_ref, xp)):
        rows = pl.ds(pl.multiple_of(p * TAPS, TAPS), TAPS)
        total = jnp.zeros(out_ref.shape, F32)
        for weight_ref, (place, offset) in zip(weights, pieces):
            columns = pl.ds(pl.multiple_of(place * depth + offset, LANES), weight_ref.shape[0])
            total += jnp.dot(cot_ref[rows, columns], weight_ref[...], preferred_element_type=F32)
        out_ref[...] = total.astype(out_ref.dtype)


def lane_blocks(*lead):
    return pl.BlockSpec(lead + (LANES,), lambda l: (0,) * len(lead) + (l,))


def convolve(rows, window):
    width = window.shape[1]
    return pl.pallas_call(
        conv_kernel,
        grid=(width // LANES,),
        in_specs=[pl.BlockSpec((PER, 2 * TAPS), lambda l: (l, 0)), lane_blocks(2 * TAPS)],
        out_specs=lane_blocks(TAPS),
        out_shape=jax.ShapeDtypeStruct((TAPS, width), F32),
        compiler_params=VMEM,
        name="conv",
    )(rows, window)


def mixed_gradient(rows, grad, after, keys, values):
    width = grad.shape[1]
    tile = lane_blocks(TAPS)
    return pl.pallas_call(
        mixed_grad_kernel,
        grid=(width // LANES,),
        in_specs=[pl.BlockSpec((PER, 2 * TAPS), lambda l: (l, 0)), tile, tile, tile, tile],
        out_specs=[tile, tile],
        out_shape=[jax.ShapeDtypeStruct((TAPS, width), BF16)] * 2,
        compiler_params=VMEM,
        name="mixed_grad",
    )(rows, grad, after, keys, values)


def turned_windows(windows):
    width = windows.shape[2]
    return pl.pallas_call(
        window_kernel,
        grid=(width // LANES,),
        in_specs=[lane_blocks(2, 2 * TAPS)],
        out_specs=lane_blocks(2, 2 * TAPS),
        out_shape=jax.ShapeDtypeStruct(windows.shape, BF16),
        compiler_params=VMEM,
        name="windows",
    )(windows)


def lag_totals(keep, give, queries, windows):
    width = keep.shape[1]
    return pl.pallas_call(
        lag_kernel,
        grid=(width // LANES,),
        in_specs=[lane_blocks(TAPS), lane_blocks(TAPS), lane_blocks(2, TAPS), lane_blocks(2, 2 * TAPS)],
        out_specs=pl.BlockSpec((PER, TAPS), lambda l: (l, 0)),
        out_shape=jax.ShapeDtypeStruct((width // GROUP, TAPS), F32),
        compiler_params=VMEM,
        name="lags",
    )(keep, give, queries, windows)


def partial_products(cotangent, weights):
    width = weights[0].shape[1]
    place = jnp.stack([lax.axis_index(Z), lax.axis_index("co"), lax.axis_index("xp")]).astype(jnp.int32)
    whole = pl.BlockSpec(memory_space=pltpu.VMEM)
    return pl.pallas_call(
        product_kernel,
        in_specs=[pl.BlockSpec(memory_space=pltpu.SMEM)] + [whole] * (1 + len(weights)),
        out_specs=[whole, whole],
        out_shape=[jax.ShapeDtypeStruct((TAPS, width), F32), jax.ShapeDtypeStruct((TAPS, width), BF16)],
        compiler_params=VMEM,
        name="product",
    )(place, cotangent, *weights)


def cotangent_columns(cotangent, after):
    rows, width = cotangent.shape
    depth = width // 64
    parts = cotangent.reshape(rows, 2, 2, 2, 4, 2, depth).transpose(3, 0, 1, 4, 5, 2, 6)
    parts, _ = lax.optimization_barrier((parts.reshape(2, 1, rows, 32 * depth), after))
    copies = jnp.broadcast_to(parts, (2, 8, rows, 32 * depth)).reshape(16, rows, 32 * depth)
    return lax.all_to_all(copies, ("xp", "y"), split_axis=0, concat_axis=0).reshape(16 * rows, 32 * depth)


def chip_weights(both):
    rows, width = both.shape[0] * both.shape[1], both.shape[2]
    both = both.reshape(rows, width)
    return in_order(both, swap(both, "co"), "co").reshape(2 * rows, width)


def weight_blocks(chip):
    n = lax.axis_size(Z)
    route = [(2 * i, 2 * ((i + 1) % n)) for i in range(n)] + [(2 * i + 1, 2 * ((i - 1) % n) + 1) for i in range(n)]
    blocks = [chip]
    got = chip
    for _ in range(3):
        got = lax.ppermute(got, Z + ("co",), route)
        blocks += [got, swap(got, "co")]
    half = got.shape[0] // 2
    got = jnp.where(lax.axis_index("co") == 0, got[:half], got[half:])
    got = lax.ppermute(got, Z + ("co",), route)
    return blocks + [got, swap(got, "co")]


def local(query_branch, key_branch, value_branch, cotangent, out_weight, filters):
    query, keys, values = query_branch[0], key_branch[0], value_branch[0]
    tokens, width = query.shape
    groups = filters.shape[0]
    both = in_order(out_weight, swap(out_weight, "xh"), "xh")
    gathered = cotangent_columns(cotangent[0], both)
    chip = chip_weights(both)
    weights = weight_blocks(chip)

    keys, _ = lax.optimization_barrier((keys, chip))
    mixed = (keys.astype(F32) * values.astype(F32)).astype(BF16)
    before = from_behind(mixed, 1)
    window = jnp.concatenate([before, mixed], 0)
    taps = filters.astype(F32)
    zero = jnp.zeros((groups, TAPS), F32)
    rows = jnp.concatenate([taps, zero], 1)
    turned_rows = jnp.concatenate([zero[:, :1], taps[:, ::-1], zero[:, 1:]], 1)
    conv = convolve(turned_rows, window)

    saved = jnp.concatenate([query, window], 0)
    saved = jnp.stack([saved, swap(saved, "xp")])
    queries = saved[:, :tokens]
    windows = turned_windows(saved[:, tokens:])

    gathered, conv, windows, queries, rows = lax.optimization_barrier((gathered, conv, windows, queries, rows))
    keep, give = partial_products(gathered, weights)
    lags = lag_totals(keep, give, queries, windows)
    lag_sum = sum_over(lags, ("xh", "xp", "co"))
    branch_grad = keep + swap(give, "xp").astype(F32)
    query_grad = (branch_grad * conv).astype(BF16)
    conv_grad = (branch_grad * query.astype(F32)).astype(BF16)
    lag_sum, conv_grad = lax.optimization_barrier((lag_sum, conv_grad))
    lag_sum = sum_over(lag_sum, Z)
    filter_grad = lag_sum * (1.0 / math.sqrt(2 * lax.axis_size(CONTEXT) * tokens * GROUP))
    after = from_behind(conv_grad, -1)
    key_grad, value_grad = mixed_gradient(rows, conv_grad, after, keys, values)
    return (query_grad[None], key_grad[None], value_grad[None], filter_grad)


def solution(mesh):
    fine = Mesh(mesh.devices.reshape(2, 2, 2, 4, 2, 8), ("zh", "xh", "xp", "zl", "co", "y"))
    branch = P("zh", CONTEXT, "y")
    return jax.shard_map(
        local,
        mesh=fine,
        in_specs=(
            branch,
            branch,
            branch,
            P("zh", CONTEXT + ("y",), None),
            P(("zh",) + CONTEXT, "y"),
            P("y", None),
        ),
        out_specs=(branch, branch, branch, P("y", None)),
        check_vma=False,
    )
```

```python
import math

import jax
import jax.numpy as jnp
from jax import lax
from jax.experimental import pallas as pl
from jax.experimental.pallas import tpu as pltpu
from jax.sharding import Mesh, PartitionSpec as P

GROUP = 16
TAPS = 128
LANES = 128
PER = LANES // GROUP
F32 = jnp.float32
BF16 = jnp.bfloat16

Z = ("zh", "zl")
CONTEXT = ("xh", "xp", "zl", "co")
VMEM = pltpu.CompilerParams(vmem_limit_bytes=8 * 1024 * 1024)


def swap(block, axis):
    return lax.ppermute(block, axis, [(0, 1), (1, 0)])


def in_order(mine, theirs, axis):
    first = lax.axis_index(axis) == 0
    return jnp.stack([jnp.where(first, mine, theirs), jnp.where(first, theirs, mine)])


def from_behind(block, distance):
    n = lax.axis_size(CONTEXT)
    route = [(i - distance, i) for i in range(n) if 0 <= i - distance < n]
    return lax.ppermute(block, CONTEXT, route)


def sum_over(block, axes):
    n = lax.axis_size(axes)
    copies = jnp.broadcast_to(block[None], (n,) + block.shape)
    return jnp.sum(lax.all_to_all(copies, axes, split_axis=0, concat_axis=0), axis=0)


def shifted_rows(row):
    return pltpu.roll(jnp.broadcast_to(row, (TAPS, 2 * TAPS)), 0, 1, stride=1, stride_axis=0)


def lane_group(shape):
    return lax.broadcasted_iota(jnp.int32, shape, 1) >> 4


def filtered(rows_ref, window):
    owner = lane_group((TAPS, LANES))
    total = jnp.zeros((TAPS, LANES), F32)
    for g in range(PER):
        table = shifted_rows(rows_ref[g : g + 1, :]).astype(BF16)
        term = jnp.dot(table, window, preferred_element_type=F32)
        total = jnp.where(owner == g, term, total)
    return total


def conv_kernel(rows_ref, window_ref, conv_ref):
    conv_ref[...] = filtered(rows_ref, window_ref[...])


def mixed_grad_kernel(rows_ref, grad_ref, after_ref, key_ref, value_ref, key_grad_ref, value_grad_ref):
    window = jnp.concatenate([grad_ref[...], after_ref[...]], 0)
    mixed_grad = filtered(rows_ref, window)
    key_grad_ref[...] = (mixed_grad * value_ref[...].astype(F32)).astype(BF16)
    value_grad_ref[...] = (mixed_grad * key_ref[...].astype(F32)).astype(BF16)


def regroup(first, second):
    low = (lane_group(first.shape) & 1) == 0
    even = jnp.where(low, first, pltpu.roll(second, GROUP, 1))
    odd = jnp.where(low, pltpu.roll(first, LANES - GROUP, 1), second)
    return even, odd


def window_kernel(window_ref, out_ref):
    n = 2 * TAPS
    across = lax.broadcasted_iota(jnp.int32, (n, n), 0) + lax.broadcasted_iota(jnp.int32, (n, n), 1)
    turn = (across == n - 1).astype(F32).astype(BF16)
    turned = [jnp.dot(turn, window_ref[b], preferred_element_type=F32) for b in range(2)]
    for a, block in enumerate(regroup(*turned)):
        out_ref[a] = block.astype(BF16)


def lag_kernel(keep_ref, give_ref, query_ref, window_ref, lag_ref):
    keep = keep_ref[...] * query_ref[0].astype(F32)
    give = give_ref[...].astype(F32) * query_ref[1].astype(F32)
    quarter = lax.broadcasted_iota(jnp.int32, (TAPS, LANES), 1) >> 5
    for a, block in enumerate(regroup(keep, give)):
        for q in range(4):
            part = jnp.where(quarter == q, block, 0.0).astype(BF16)
            outer = lax.dot_general(part, window_ref[a], (((1,), (1,)), ((), ())), preferred_element_type=F32)
            skewed = pltpu.roll(outer, 1, 1, stride=1, stride_axis=0)
            sums = jnp.sum(skewed, axis=0, keepdims=True)
            lag_ref[2 * q + a : 2 * q + a + 1, :] = sums[:, TAPS:]


def product_kernel(place_ref, cot_ref, *refs):
    weights, (keep_ref, give_ref) = refs[:-2], refs[-2:]
    z, core, xp = place_ref[0], place_ref[1], place_ref[2]
    depth = weights[0].shape[0]
    pieces = [(z, 0)]
    for step in (1, 2, 3):
        below, above = lax.rem(z + 8 - step, 8), lax.rem(z + step, 8)
        pieces += [(jnp.where(core == 0, below, above), 0), (jnp.where(core == 0, above, below), 0)]
    far = lax.rem(z + 4, 8)
    pieces += [(far, jnp.where(core == 0, 0, depth // 2)), (far, jnp.where(core == 0, depth // 2, 0))]
    for out_ref, p in ((give_ref, 1 - xp), (keep_ref, xp)):
        total = jnp.zeros(out_ref.shape, F32)
        for weight_ref, (place, offset) in zip(weights, pieces):
            size = weight_ref.shape[0]
            columns = pl.ds(pl.multiple_of(place * depth + offset, LANES), size)
            part = cot_ref[:, p, :, columns].reshape(TAPS, size)
            total += jnp.dot(part, weight_ref[...], preferred_element_type=F32)
        out_ref[...] = total.astype(out_ref.dtype)


def lane_blocks(*lead):
    return pl.BlockSpec(lead + (LANES,), lambda l: (0,) * len(lead) + (l,))


def convolve(rows, window):
    width = window.shape[1]
    return pl.pallas_call(
        conv_kernel,
        grid=(width // LANES,),
        in_specs=[pl.BlockSpec((PER, 2 * TAPS), lambda l: (l, 0)), lane_blocks(2 * TAPS)],
        out_specs=lane_blocks(TAPS),
        out_shape=jax.ShapeDtypeStruct((TAPS, width), F32),
        compiler_params=VMEM,
        name="conv",
    )(rows, window)


def mixed_gradient(rows, grad, after, keys, values):
    width = grad.shape[1]
    tile = lane_blocks(TAPS)
    return pl.pallas_call(
        mixed_grad_kernel,
        grid=(width // LANES,),
        in_specs=[pl.BlockSpec((PER, 2 * TAPS), lambda l: (l, 0)), tile, tile, tile, tile],
        out_specs=[tile, tile],
        out_shape=[jax.ShapeDtypeStruct((TAPS, width), BF16)] * 2,
        compiler_params=VMEM,
        name="mixed_grad",
    )(rows, grad, after, keys, values)


def turned_windows(windows):
    width = windows.shape[2]
    return pl.pallas_call(
        window_kernel,
        grid=(width // LANES,),
        in_specs=[lane_blocks(2, 2 * TAPS)],
        out_specs=lane_blocks(2, 2 * TAPS),
        out_shape=jax.ShapeDtypeStruct(windows.shape, BF16),
        compiler_params=VMEM,
        name="windows",
    )(windows)


def lag_totals(keep, give, queries, windows):
    width = keep.shape[1]
    return pl.pallas_call(
        lag_kernel,
        grid=(width // LANES,),
        in_specs=[lane_blocks(TAPS), lane_blocks(TAPS), lane_blocks(2, TAPS), lane_blocks(2, 2 * TAPS)],
        out_specs=pl.BlockSpec((PER, TAPS), lambda l: (l, 0)),
        out_shape=jax.ShapeDtypeStruct((width // GROUP, TAPS), F32),
        compiler_params=VMEM,
        name="lags",
    )(keep, give, queries, windows)


def partial_products(cotangent, weights):
    width = weights[0].shape[1]
    place = jnp.stack([lax.axis_index(Z), lax.axis_index("co"), lax.axis_index("xp")]).astype(jnp.int32)
    whole = pl.BlockSpec(memory_space=pltpu.VMEM)
    return pl.pallas_call(
        product_kernel,
        in_specs=[pl.BlockSpec(memory_space=pltpu.SMEM)] + [whole] * (1 + len(weights)),
        out_specs=[whole, whole],
        out_shape=[jax.ShapeDtypeStruct((TAPS, width), F32), jax.ShapeDtypeStruct((TAPS, width), BF16)],
        compiler_params=VMEM,
        name="product",
    )(place, cotangent, *weights)


def cotangent_columns(cotangent):
    rows, width = cotangent.shape
    depth = width // 64
    parts = cotangent.reshape(rows, 2, 2, 2, 4, 2, depth).transpose(3, 0, 1, 4, 5, 2, 6)
    parts = parts.reshape(2, rows, 32 * depth)
    xp = lax.axis_index("xp")
    keep = lax.dynamic_index_in_dim(parts, xp, 0, keepdims=False)
    give = lax.dynamic_index_in_dim(parts, 1 - xp, 0, keepdims=False)
    ready = in_order(keep, swap(give, "xp"), "xp")
    return ready, lax.all_gather(ready, "y", axis=0)


def chip_weights(both):
    rows, width = both.shape[0] * both.shape[1], both.shape[2]
    both = both.reshape(rows, width)
    return in_order(both, swap(both, "co"), "co").reshape(2 * rows, width)


def weight_blocks(chip):
    n = lax.axis_size(Z)
    route = [(2 * i, 2 * ((i + 1) % n)) for i in range(n)] + [(2 * i + 1, 2 * ((i - 1) % n) + 1) for i in range(n)]
    blocks = [chip]
    got = chip
    for _ in range(3):
        got = lax.ppermute(got, Z + ("co",), route)
        blocks += [got, swap(got, "co")]
    half = got.shape[0] // 2
    got = jnp.where(lax.axis_index("co") == 0, got[:half], got[half:])
    got = lax.ppermute(got, Z + ("co",), route)
    return blocks + [got, swap(got, "co")]


def local(query_branch, key_branch, value_branch, cotangent, out_weight, filters):
    query, keys, values = query_branch[0], key_branch[0], value_branch[0]
    tokens, width = query.shape
    groups = filters.shape[0]
    ready, gathered = cotangent_columns(cotangent[0])
    both = in_order(out_weight, swap(out_weight, "xh"), "xh")
    both, _ = lax.optimization_barrier((both, ready))
    chip = chip_weights(both)
    weights = weight_blocks(chip)

    keys, _ = lax.optimization_barrier((keys, chip))
    mixed = (keys.astype(F32) * values.astype(F32)).astype(BF16)
    before = from_behind(mixed, 1)
    window = jnp.concatenate([before, mixed], 0)
    taps = filters.astype(F32)
    zero = jnp.zeros((groups, TAPS), F32)
    rows = jnp.concatenate([taps, zero], 1)
    turned_rows = jnp.concatenate([zero[:, :1], taps[:, ::-1], zero[:, 1:]], 1)
    conv = convolve(turned_rows, window)

    saved = jnp.concatenate([query, window], 0)
    saved = jnp.stack([saved, swap(saved, "xp")])
    queries = saved[:, :tokens]
    windows = turned_windows(saved[:, tokens:])

    gathered, conv, windows, queries, rows = lax.optimization_barrier((gathered, conv, windows, queries, rows))
    keep, give = partial_products(gathered, weights)
    lags = lag_totals(keep, give, queries, windows)
    lag_sum = sum_over(lags, ("xh", "xp", "co"))
    branch_grad = keep + swap(give, "xp").astype(F32)
    query_grad = (branch_grad * conv).astype(BF16)
    conv_grad = (branch_grad * query.astype(F32)).astype(BF16)
    lag_sum, conv_grad = lax.optimization_barrier((lag_sum, conv_grad))
    lag_sum = sum_over(lag_sum, Z)
    filter_grad = lag_sum * (1.0 / math.sqrt(2 * lax.axis_size(CONTEXT) * tokens * GROUP))
    after = from_behind(conv_grad, -1)
    key_grad, value_grad = mixed_gradient(rows, conv_grad, after, keys, values)
    return (query_grad[None], key_grad[None], value_grad[None], filter_grad)


def solution(mesh):
    fine = Mesh(mesh.devices.reshape(2, 2, 2, 4, 2, 8), ("zh", "xh", "xp", "zl", "co", "y"))
    branch = P("zh", CONTEXT, "y")
    return jax.shard_map(
        local,
        mesh=fine,
        in_specs=(
            branch,
            branch,
            branch,
            P("zh", CONTEXT + ("y",), None),
            P(("zh",) + CONTEXT, "y"),
            P("y", None),
        ),
        out_specs=(branch, branch, branch, P("y", None)),
        check_vma=False,
    )
```

```python
import math

import jax
import jax.numpy as jnp
from jax import lax
from jax.experimental import pallas as pl
from jax.experimental.pallas import tpu as pltpu
from jax.sharding import Mesh, PartitionSpec as P

GROUP = 16
TAPS = 128
LANES = 128
PER = LANES // GROUP
F32 = jnp.float32
BF16 = jnp.bfloat16

Z = ("zh", "zl")
CONTEXT = ("x", "zl", "co")
TURNS = (0, 1, 2, 3)
VMEM = pltpu.CompilerParams(vmem_limit_bytes=8 * 1024 * 1024)


def swap(block, axis):
    return lax.ppermute(block, axis, [(0, 1), (1, 0)])


def in_order(mine, theirs, axis):
    first = lax.axis_index(axis) == 0
    return jnp.stack([jnp.where(first, mine, theirs), jnp.where(first, theirs, mine)])


def from_behind(block, distance):
    n = lax.axis_size(CONTEXT)
    route = [(i - distance, i) for i in range(n) if 0 <= i - distance < n]
    return lax.ppermute(block, CONTEXT, route)


def sum_over(block, axes):
    n = lax.axis_size(axes)
    copies = jnp.broadcast_to(block[None], (n,) + block.shape)
    return jnp.sum(lax.all_to_all(copies, axes, split_axis=0, concat_axis=0), axis=0)


def shifted_rows(row):
    return pltpu.roll(jnp.broadcast_to(row, (TAPS, 2 * TAPS)), 0, 1, stride=1, stride_axis=0)


def lane_group(shape):
    return lax.broadcasted_iota(jnp.int32, shape, 1) >> 4


def filtered(rows_ref, window):
    owner = lane_group((TAPS, LANES))
    total = jnp.zeros((TAPS, LANES), F32)
    for g in range(PER):
        table = shifted_rows(rows_ref[g : g + 1, :]).astype(BF16)
        term = jnp.dot(table, window, preferred_element_type=F32)
        total = jnp.where(owner == g, term, total)
    return total


def conv_kernel(rows_ref, window_ref, conv_ref):
    conv_ref[...] = filtered(rows_ref, window_ref[...])


def mixed_grad_kernel(rows_ref, grad_ref, after_ref, key_ref, value_ref, key_grad_ref, value_grad_ref):
    window = jnp.concatenate([grad_ref[...], after_ref[...]], 0)
    mixed_grad = filtered(rows_ref, window)
    key_grad_ref[...] = (mixed_grad * value_ref[...].astype(F32)).astype(BF16)
    value_grad_ref[...] = (mixed_grad * key_ref[...].astype(F32)).astype(BF16)


def regroup(blocks):
    rows = blocks[0].shape[0]
    group = lane_group((rows, LANES))
    for bit in (1, 2):
        low = (group & bit) == 0
        out = list(blocks)
        for b in range(4):
            if b & bit:
                continue
            x0, x1 = blocks[b], blocks[b | bit]
            out[b] = jnp.where(low, x0, pltpu.roll(x1, GROUP * bit, 1))
            out[b | bit] = jnp.where(low, pltpu.roll(x0, LANES - GROUP * bit, 1), x1)
        blocks = out
    return blocks


def window_kernel(window_ref, out_ref):
    n = 2 * TAPS
    across = lax.broadcasted_iota(jnp.int32, (n, n), 0) + lax.broadcasted_iota(jnp.int32, (n, n), 1)
    turn = (across == n - 1).astype(F32).astype(BF16)
    turned = [jnp.dot(turn, window_ref[b], preferred_element_type=F32) for b in range(4)]
    for a, block in enumerate(regroup(turned)):
        out_ref[a] = block.astype(BF16)


def lag_kernel(keep_ref, give_ref, query_ref, window_ref, lag_ref):
    grads = [keep_ref[...]] + [give_ref[b].astype(F32) for b in range(3)]
    grads = [g * query_ref[b].astype(F32) for b, g in enumerate(grads)]
    half = lax.broadcasted_iota(jnp.int32, (TAPS, LANES), 1) >> 6
    for a, block in enumerate(regroup(grads)):
        for h in range(2):
            part = jnp.where(half == h, block, 0.0).astype(BF16)
            outer = lax.dot_general(part, window_ref[a], (((1,), (1,)), ((), ())), preferred_element_type=F32)
            skewed = pltpu.roll(outer, 1, 1, stride=1, stride_axis=0)
            sums = jnp.sum(skewed, axis=0, keepdims=True)
            lag_ref[4 * h + a : 4 * h + a + 1, :] = sums[:, TAPS:]


def product_kernel(place_ref, cot_ref, *refs):
    weights, (keep_ref, give_ref) = refs[:-2], refs[-2:]
    z, core, x = place_ref[0], place_ref[1], place_ref[2]
    depth = weights[0].shape[0]
    pieces = [(z, 0)]
    for step in (1, 2, 3):
        below, above = lax.rem(z + 8 - step, 8), lax.rem(z + step, 8)
        pieces += [(jnp.where(core == 0, below, above), 0), (jnp.where(core == 0, above, below), 0)]
    far = lax.rem(z + 4, 8)
    pieces += [(far, jnp.where(core == 0, 0, depth // 2)), (far, jnp.where(core == 0, depth // 2, 0))]
    for turned in (1, 2, 3, 0):
        rows = pl.ds(pl.multiple_of(lax.rem(x + turned, 4) * TAPS, TAPS), TAPS)
        total = jnp.zeros(keep_ref.shape, F32)
        for weight_ref, (place, offset) in zip(weights, pieces):
            columns = pl.ds(pl.multiple_of(place * depth + offset, LANES), weight_ref.shape[0])
            total += jnp.dot(cot_ref[rows, columns], weight_ref[...], preferred_element_type=F32)
        if turned:
            give_ref[turned - 1] = total.astype(BF16)
        else:
            keep_ref[...] = total


def lane_blocks(*lead):
    return pl.BlockSpec(lead + (LANES,), lambda l: (0,) * len(lead) + (l,))


def convolve(rows, window):
    width = window.shape[1]
    return pl.pallas_call(
        conv_kernel,
        grid=(width // LANES,),
        in_specs=[pl.BlockSpec((PER, 2 * TAPS), lambda l: (l, 0)), lane_blocks(2 * TAPS)],
        out_specs=lane_blocks(TAPS),
        out_shape=jax.ShapeDtypeStruct((TAPS, width), F32),
        compiler_params=VMEM,
        name="conv",
    )(rows, window)


def mixed_gradient(rows, grad, after, keys, values):
    width = grad.shape[1]
    tile = lane_blocks(TAPS)
    return pl.pallas_call(
        mixed_grad_kernel,
        grid=(width // LANES,),
        in_specs=[pl.BlockSpec((PER, 2 * TAPS), lambda l: (l, 0)), tile, tile, tile, tile],
        out_specs=[tile, tile],
        out_shape=[jax.ShapeDtypeStruct((TAPS, width), BF16)] * 2,
        compiler_params=VMEM,
        name="mixed_grad",
    )(rows, grad, after, keys, values)


def turned_windows(windows):
    width = windows.shape[2]
    return pl.pallas_call(
        window_kernel,
        grid=(width // LANES,),
        in_specs=[lane_blocks(4, 2 * TAPS)],
        out_specs=lane_blocks(4, 2 * TAPS),
        out_shape=jax.ShapeDtypeStruct(windows.shape, BF16),
        compiler_params=VMEM,
        name="windows",
    )(windows)


def lag_totals(keep, give, queries, windows):
    width = keep.shape[1]
    return pl.pallas_call(
        lag_kernel,
        grid=(width // LANES,),
        in_specs=[lane_blocks(TAPS), lane_blocks(3, TAPS), lane_blocks(4, TAPS), lane_blocks(4, 2 * TAPS)],
        out_specs=pl.BlockSpec((PER, TAPS), lambda l: (l, 0)),
        out_shape=jax.ShapeDtypeStruct((width // GROUP, TAPS), F32),
        compiler_params=VMEM,
        name="lags",
    )(keep, give, queries, windows)


def partial_products(cotangent, weights):
    width = weights[0].shape[1]
    place = jnp.stack([lax.axis_index(Z), lax.axis_index("co"), lax.axis_index("x")]).astype(jnp.int32)
    whole = pl.BlockSpec(memory_space=pltpu.VMEM)
    return pl.pallas_call(
        product_kernel,
        in_specs=[pl.BlockSpec(memory_space=pltpu.SMEM)] + [whole] * (1 + len(weights)),
        out_specs=[whole, whole],
        out_shape=[jax.ShapeDtypeStruct((TAPS, width), F32), jax.ShapeDtypeStruct((3, TAPS, width), BF16)],
        compiler_params=VMEM,
        name="product",
    )(place, cotangent, *weights)


def turn(block, axes, distance):
    n = lax.axis_size(axes)
    return lax.ppermute(block, axes, [((i + distance) % n, i) for i in range(n)])


def cotangent_columns(cotangent, after):
    rows, width = cotangent.shape
    depth = width // 64
    parts = cotangent.reshape(rows, 2, 4, 4, 2, depth).transpose(2, 0, 1, 3, 4, 5)
    parts, _ = lax.optimization_barrier((parts.reshape(4, 1, rows, 16 * depth), after))
    copies = jnp.broadcast_to(parts, (4, 8, rows, 16 * depth)).reshape(32, rows, 16 * depth)
    return lax.all_to_all(copies, ("x", "y"), split_axis=0, concat_axis=0).reshape(32 * rows, 16 * depth)


def weight_blocks(chip):
    n = lax.axis_size(Z)
    route = [(2 * i, 2 * ((i + 1) % n)) for i in range(n)] + [(2 * i + 1, 2 * ((i - 1) % n) + 1) for i in range(n)]
    blocks = [chip]
    got = chip
    for _ in range(3):
        got = lax.ppermute(got, Z + ("co",), route)
        blocks += [got, swap(got, "co")]
    half = got.shape[0] // 2
    got = jnp.where(lax.axis_index("co") == 0, got[:half], got[half:])
    got = lax.ppermute(got, Z + ("co",), route)
    return blocks + [got, swap(got, "co")]


def local(query_branch, key_branch, value_branch, cotangent, out_weight, filters):
    query, keys, values = query_branch[0], key_branch[0], value_branch[0]
    tokens, width = query.shape
    groups = filters.shape[0]
    chip = in_order(out_weight, swap(out_weight, "co"), "co").reshape(2 * out_weight.shape[0], width)
    gathered = cotangent_columns(cotangent[0], chip)
    weights = weight_blocks(chip)

    keys, _ = lax.optimization_barrier((keys, weights[1]))
    mixed = (keys.astype(F32) * values.astype(F32)).astype(BF16)
    before = from_behind(mixed, 1)
    window = jnp.concatenate([before, mixed], 0)
    taps = filters.astype(F32)
    zero = jnp.zeros((groups, TAPS), F32)
    rows = jnp.concatenate([taps, zero], 1)
    turned_rows = jnp.concatenate([zero[:, :1], taps[:, ::-1], zero[:, 1:]], 1)
    conv = convolve(turned_rows, window)

    saved = jnp.concatenate([query, window], 0)
    saved = jnp.stack([saved if t == 0 else turn(saved, "x", t) for t in TURNS])
    queries = saved[:, :tokens]
    windows = turned_windows(saved[:, tokens:])

    gathered, conv, windows, queries, rows = lax.optimization_barrier((gathered, conv, windows, queries, rows))
    keep, give = partial_products(gathered, weights)
    lags = lag_totals(keep, give, queries, windows)
    lag_sum = sum_over(lags, ("x", "co"))
    branch_grad = keep
    for t in TURNS[1:]:
        branch_grad = branch_grad + turn(give[t - 1], "x", -t).astype(F32)
    query_grad = (branch_grad * conv).astype(BF16)
    conv_grad = (branch_grad * query.astype(F32)).astype(BF16)
    lag_sum, conv_grad = lax.optimization_barrier((lag_sum, conv_grad))
    lag_sum = sum_over(lag_sum, Z)
    filter_grad = lag_sum * (1.0 / math.sqrt(2 * lax.axis_size(CONTEXT) * tokens * GROUP))
    after = from_behind(conv_grad, -1)
    key_grad, value_grad = mixed_gradient(rows, conv_grad, after, keys, values)
    return (query_grad[None], key_grad[None], value_grad[None], filter_grad)


def solution(mesh):
    fine = Mesh(mesh.devices.reshape(2, 4, 4, 2, 8), ("zh", "x", "zl", "co", "y"))
    branch = P("zh", CONTEXT, "y")
    return jax.shard_map(
        local,
        mesh=fine,
        in_specs=(
            branch,
            branch,
            branch,
            P("zh", CONTEXT + ("y",), None),
            P(("zh",) + CONTEXT, "y"),
            P("y", None),
        ),
        out_specs=(branch, branch, branch, P("y", None)),
        check_vma=False,
    )
```

```python
import math

import jax
import jax.numpy as jnp
from jax import lax
from jax.experimental import pallas as pl
from jax.experimental.pallas import tpu as pltpu
from jax.sharding import Mesh, PartitionSpec as P

GROUP = 16
TAPS = 128
LANES = 128
PER = LANES // GROUP
F32 = jnp.float32
BF16 = jnp.bfloat16

Z = ("zh", "zl")
CONTEXT = ("x", "zl", "co")
VMEM = pltpu.CompilerParams(vmem_limit_bytes=8 * 1024 * 1024)


def swap(block, axis):
    return lax.ppermute(block, axis, [(0, 1), (1, 0)])


def in_order(mine, theirs, axis):
    first = lax.axis_index(axis) == 0
    return jnp.stack([jnp.where(first, mine, theirs), jnp.where(first, theirs, mine)])


def from_behind(block, distance):
    n = lax.axis_size(CONTEXT)
    route = [(i - distance, i) for i in range(n) if 0 <= i - distance < n]
    return lax.ppermute(block, CONTEXT, route)


def sum_over(block, axes):
    n = lax.axis_size(axes)
    copies = jnp.broadcast_to(block[None], (n,) + block.shape)
    return jnp.sum(lax.all_to_all(copies, axes, split_axis=0, concat_axis=0), axis=0)


def shifted_rows(row):
    return pltpu.roll(jnp.broadcast_to(row, (TAPS, 2 * TAPS)), 0, 1, stride=1, stride_axis=0)


def lane_group(shape):
    return lax.broadcasted_iota(jnp.int32, shape, 1) >> 4


def filtered(rows_ref, window):
    owner = lane_group((TAPS, LANES))
    total = jnp.zeros((TAPS, LANES), F32)
    for g in range(PER):
        table = shifted_rows(rows_ref[g : g + 1, :]).astype(BF16)
        term = jnp.dot(table, window, preferred_element_type=F32)
        total = jnp.where(owner == g, term, total)
    return total


def conv_kernel(rows_ref, window_ref, conv_ref, turned_ref):
    window = window_ref[...]
    conv_ref[...] = filtered(rows_ref, window)
    n = window.shape[0]
    across = lax.broadcasted_iota(jnp.int32, (n, n), 0) + lax.broadcasted_iota(jnp.int32, (n, n), 1)
    turn_rows = (across == n - 1).astype(F32).astype(BF16)
    turned_ref[...] = jnp.dot(turn_rows, window, preferred_element_type=F32).astype(BF16)


def mixed_grad_kernel(rows_ref, grad_ref, after_ref, key_ref, value_ref, key_grad_ref, value_grad_ref):
    window = jnp.concatenate([grad_ref[...], after_ref[...]], 0)
    mixed_grad = filtered(rows_ref, window)
    key_grad_ref[...] = (mixed_grad * value_ref[...].astype(F32)).astype(BF16)
    value_grad_ref[...] = (mixed_grad * key_ref[...].astype(F32)).astype(BF16)


def branch_kernel(terms_ref, conv_ref, query_ref, turned_ref, query_grad_ref, conv_grad_ref, lag_ref):
    branch_grad = terms_ref[0].astype(F32)
    for x in range(1, terms_ref.shape[0]):
        branch_grad = branch_grad + terms_ref[x].astype(F32)
    query_grad_ref[...] = (branch_grad * conv_ref[...]).astype(BF16)
    conv_grad = (branch_grad * query_ref[...].astype(F32)).astype(BF16)
    conv_grad_ref[...] = conv_grad
    owner = lane_group((TAPS, LANES))
    wide = conv_grad.astype(F32)
    for g in range(PER):
        part = jnp.where(owner == g, wide, 0.0).astype(BF16)
        outer = lax.dot_general(part, turned_ref[...], (((1,), (1,)), ((), ())), preferred_element_type=F32)
        skewed = pltpu.roll(outer, 1, 1, stride=1, stride_axis=0)
        lag_ref[g : g + 1, :] = jnp.sum(skewed, axis=0, keepdims=True)[:, TAPS:]


def product_kernel(place_ref, cot_ref, *refs):
    count = (len(refs) - 3) // 2
    weights_hbm, out_ref, total_ref, weights, sems = refs[:count], refs[count], refs[count + 1], refs[count + 2 : -1], refs[-1]
    copies = [pltpu.make_async_copy(weights_hbm[i], weights[i], sems.at[i]) for i in range(count)]
    for copy in copies:
        copy.start()
    z, core = place_ref[0], place_ref[1]
    depth = weights[0].shape[0]
    pieces = [(z, 0)]
    for step in (1, 2, 3):
        below, above = lax.rem(z + 8 - step, 8), lax.rem(z + step, 8)
        pieces += [(jnp.where(core == 0, below, above), 0), (jnp.where(core == 0, above, below), 0)]
    far = lax.rem(z + 4, 8)
    pieces += [(far, jnp.where(core == 0, 0, depth // 2)), (far, jnp.where(core == 0, depth // 2, 0))]
    for i, (place, offset) in enumerate(pieces):
        copies[i].wait()
        columns = pl.ds(pl.multiple_of(place * depth + offset, LANES), weights[i].shape[0])
        for x in range(4):
            rows = slice(x * TAPS, (x + 1) * TAPS)
            term = jnp.dot(cot_ref[rows, columns], weights[i][...], preferred_element_type=F32)
            if i:
                term = total_ref[x] + term
            if i < count - 1:
                total_ref[x] = term
            else:
                out_ref[x] = term.astype(BF16)


def lane_blocks(*lead):
    return pl.BlockSpec(lead + (LANES,), lambda l: (0,) * len(lead) + (l,))


def convolve(rows, window):
    width = window.shape[1]
    return pl.pallas_call(
        conv_kernel,
        grid=(width // LANES,),
        in_specs=[pl.BlockSpec((PER, 2 * TAPS), lambda l: (l, 0)), lane_blocks(2 * TAPS)],
        out_specs=[lane_blocks(TAPS), lane_blocks(2 * TAPS)],
        out_shape=[jax.ShapeDtypeStruct((TAPS, width), F32), jax.ShapeDtypeStruct((2 * TAPS, width), BF16)],
        compiler_params=VMEM,
        name="conv",
    )(rows, window)


def mixed_gradient(rows, grad, after, keys, values):
    width = grad.shape[1]
    tile = lane_blocks(TAPS)
    return pl.pallas_call(
        mixed_grad_kernel,
        grid=(width // LANES,),
        in_specs=[pl.BlockSpec((PER, 2 * TAPS), lambda l: (l, 0)), tile, tile, tile, tile],
        out_specs=[tile, tile],
        out_shape=[jax.ShapeDtypeStruct((TAPS, width), BF16)] * 2,
        compiler_params=VMEM,
        name="mixed_grad",
    )(rows, grad, after, keys, values)


def branch_gradients(terms, conv, query, turned):
    width = query.shape[1]
    tile = lane_blocks(TAPS)
    return pl.pallas_call(
        branch_kernel,
        grid=(width // LANES,),
        in_specs=[lane_blocks(terms.shape[0], TAPS), tile, tile, lane_blocks(2 * TAPS)],
        out_specs=[tile, tile, pl.BlockSpec((PER, TAPS), lambda l: (l, 0))],
        out_shape=[jax.ShapeDtypeStruct((TAPS, width), BF16)] * 2 + [jax.ShapeDtypeStruct((width // GROUP, TAPS), F32)],
        compiler_params=VMEM,
        name="branch",
    )(terms, conv, query, turned)


def partial_products(cotangent, weights):
    width = weights[0].shape[1]
    place = jnp.stack([lax.axis_index(Z), lax.axis_index("co")]).astype(jnp.int32)
    whole = pl.BlockSpec(memory_space=pltpu.VMEM)
    return pl.pallas_call(
        product_kernel,
        in_specs=[pl.BlockSpec(memory_space=pltpu.SMEM), whole]
        + [pl.BlockSpec(memory_space=pltpu.HBM)] * len(weights),
        out_specs=whole,
        out_shape=jax.ShapeDtypeStruct((4, TAPS, width), BF16),
        scratch_shapes=[pltpu.VMEM((4, TAPS, width), F32)]
        + [pltpu.VMEM(a.shape, a.dtype) for a in weights]
        + [pltpu.SemaphoreType.DMA((len(weights),))],
        compiler_params=VMEM,
        name="product",
    )(place, cotangent, *weights)


def cotangent_columns(cotangent, after):
    rows, width = cotangent.shape
    depth = width // 64
    parts = cotangent.reshape(rows, 2, 4, 4, 2, depth).transpose(2, 0, 1, 3, 4, 5)
    parts, _ = lax.optimization_barrier((parts.reshape(4, 1, rows, 16 * depth), after))
    copies = jnp.broadcast_to(parts, (4, 8, rows, 16 * depth)).reshape(32, rows, 16 * depth)
    return lax.all_to_all(copies, ("x", "y"), split_axis=0, concat_axis=0).reshape(32 * rows, 16 * depth)


def weight_blocks(chip):
    n = lax.axis_size(Z)
    route = [(2 * i, 2 * ((i + 1) % n)) for i in range(n)] + [(2 * i + 1, 2 * ((i - 1) % n) + 1) for i in range(n)]
    blocks = [chip]
    got = chip
    for _ in range(3):
        got = lax.ppermute(got, Z + ("co",), route)
        blocks += [got, swap(got, "co")]
    half = got.shape[0] // 2
    got = jnp.where(lax.axis_index("co") == 0, got[:half], got[half:])
    got = lax.ppermute(got, Z + ("co",), route)
    return blocks + [got, swap(got, "co")]


def local(query_branch, key_branch, value_branch, cotangent, out_weight, filters):
    query, keys, values = query_branch[0], key_branch[0], value_branch[0]
    tokens, width = query.shape
    groups = filters.shape[0]
    chip = in_order(out_weight, swap(out_weight, "co"), "co").reshape(2 * out_weight.shape[0], width)
    gathered = cotangent_columns(cotangent[0], chip)
    weights = weight_blocks(chip)

    keys, _ = lax.optimization_barrier((keys, weights[1]))
    mixed = (keys.astype(F32) * values.astype(F32)).astype(BF16)
    before = from_behind(mixed, 1)
    window = jnp.concatenate([before, mixed], 0)
    taps = filters.astype(F32)
    zero = jnp.zeros((groups, TAPS), F32)
    rows = jnp.concatenate([taps, zero], 1)
    turned_rows = jnp.concatenate([zero[:, :1], taps[:, ::-1], zero[:, 1:]], 1)
    conv, turned = convolve(turned_rows, window)

    gathered, conv, turned, rows = lax.optimization_barrier((gathered, conv, turned, rows))
    partial = partial_products(gathered, weights)
    terms = lax.all_to_all(partial, "x", split_axis=0, concat_axis=0)
    query_grad, conv_grad, lags = branch_gradients(terms, conv, query, turned)
    lag_sum = sum_over(sum_over(lags, ("x", "co")), Z)
    filter_grad = lag_sum * (1.0 / math.sqrt(2 * lax.axis_size(CONTEXT) * tokens * GROUP))
    after = from_behind(conv_grad, -1)
    key_grad, value_grad = mixed_gradient(rows, conv_grad, after, keys, values)
    return (query_grad[None], key_grad[None], value_grad[None], filter_grad)


def solution(mesh):
    fine = Mesh(mesh.devices.reshape(2, 4, 4, 2, 8), ("zh", "x", "zl", "co", "y"))
    branch = P("zh", CONTEXT, "y")
    return jax.shard_map(
        local,
        mesh=fine,
        in_specs=(
            branch,
            branch,
            branch,
            P("zh", CONTEXT + ("y",), None),
            P(("zh",) + CONTEXT, "y"),
            P("y", None),
        ),
        out_specs=(branch, branch, branch, P("y", None)),
        check_vma=False,
    )
```

```python
import math

import jax
import jax.numpy as jnp
from jax import lax
from jax.experimental import pallas as pl
from jax.experimental.pallas import tpu as pltpu
from jax.sharding import Mesh, PartitionSpec as P

GROUP = 16
TAPS = 128
LANES = 128
PER = LANES // GROUP
F32 = jnp.float32
BF16 = jnp.bfloat16

Z = ("zh", "zl")
CONTEXT = ("x", "zl", "co")
VMEM = pltpu.CompilerParams(vmem_limit_bytes=8 * 1024 * 1024)


def swap(block, axis):
    return lax.ppermute(block, axis, [(0, 1), (1, 0)])


def in_order(mine, theirs, axis):
    first = lax.axis_index(axis) == 0
    return jnp.stack([jnp.where(first, mine, theirs), jnp.where(first, theirs, mine)])


def from_behind(block, distance):
    n = lax.axis_size(CONTEXT)
    route = [(i - distance, i) for i in range(n) if 0 <= i - distance < n]
    return lax.ppermute(block, CONTEXT, route)


def shifted_rows(row):
    return pltpu.roll(jnp.broadcast_to(row, (TAPS, 2 * TAPS)), 0, 1, stride=1, stride_axis=0)


def lane_group(shape):
    return lax.broadcasted_iota(jnp.int32, shape, 1) >> 4


def filtered(rows, window):
    owner = lane_group((TAPS, LANES))
    total = jnp.zeros((TAPS, LANES), F32)
    for g in range(PER):
        table = shifted_rows(rows[g : g + 1, :]).astype(BF16)
        term = jnp.dot(table, window, preferred_element_type=F32)
        total = jnp.where(owner == g, term, total)
    return total


def antidiagonal(rows, columns, total):
    across = lax.broadcasted_iota(jnp.int32, (rows, columns), 0) + lax.broadcasted_iota(jnp.int32, (rows, columns), 1)
    return (across == total).astype(F32).astype(BF16)


def conv_kernel(filters_ref, before_ref, mixed_ref, conv_ref, turned_ref):
    window = jnp.concatenate([before_ref[...], mixed_ref[...]], 0)
    n = 2 * TAPS
    rows = jnp.dot(filters_ref[...], antidiagonal(TAPS, n, TAPS), preferred_element_type=F32)
    conv_ref[...] = filtered(rows, window)
    turned_ref[...] = jnp.dot(antidiagonal(n, n, n - 1), window, preferred_element_type=F32).astype(BF16)


def mixed_grad_kernel(filters_ref, grad_ref, after_ref, key_ref, value_ref, key_grad_ref, value_grad_ref):
    window = jnp.concatenate([grad_ref[...], after_ref[...]], 0)
    taps = filters_ref[...].astype(F32)
    mixed_grad = filtered(jnp.concatenate([taps, jnp.zeros(taps.shape, F32)], 1), window)
    key_grad_ref[...] = (mixed_grad * value_ref[...].astype(F32)).astype(BF16)
    value_grad_ref[...] = (mixed_grad * key_ref[...].astype(F32)).astype(BF16)


def spread_kernel(cot_ref, out_ref):
    size = cot_ref.shape[1] // 8
    for x in range(4):
        for zh in range(2):
            out_ref[x, 0, :, zh * size : (zh + 1) * size] = cot_ref[:, (4 * zh + x) * size : (4 * zh + x + 1) * size]


def sum_kernel(parts_ref, out_ref):
    total = jnp.sum(parts_ref[...], axis=0)
    for i in range(out_ref.shape[0]):
        out_ref[i] = total


def branch_kernel(terms_ref, conv_ref, query_ref, turned_ref, query_grad_ref, conv_grad_ref, lag_ref):
    branch_grad = terms_ref[0].astype(F32)
    for x in range(1, terms_ref.shape[0]):
        branch_grad = branch_grad + terms_ref[x].astype(F32)
    query_grad_ref[...] = (branch_grad * conv_ref[...]).astype(BF16)
    conv_grad = (branch_grad * query_ref[...].astype(F32)).astype(BF16)
    conv_grad_ref[...] = conv_grad
    owner = lane_group((TAPS, LANES))
    wide = conv_grad.astype(F32)
    for g in range(PER):
        part = jnp.where(owner == g, wide, 0.0).astype(BF16)
        outer = lax.dot_general(part, turned_ref[...], (((1,), (1,)), ((), ())), preferred_element_type=F32)
        skewed = pltpu.roll(outer, 1, 1, stride=1, stride_axis=0)
        sums = jnp.sum(skewed, axis=0, keepdims=True)[:, TAPS:]
        for copy in range(lag_ref.shape[0]):
            lag_ref[copy, g : g + 1, :] = sums


def product_kernel(place_ref, cot_ref, *refs):
    count = (len(refs) - 3) // 2
    weights_hbm, out_ref, total_ref, weights, sems = refs[:count], refs[count], refs[count + 1], refs[count + 2 : -1], refs[-1]
    copies = [pltpu.make_async_copy(weights_hbm[i], weights[i], sems.at[i]) for i in range(count)]
    for copy in copies:
        copy.start()
    z, core = place_ref[0], place_ref[1]
    depth = weights[0].shape[0]
    pieces = [(z, 0)]
    for step in (1, 2, 3):
        below, above = lax.rem(z + 8 - step, 8), lax.rem(z + step, 8)
        pieces += [(jnp.where(core == 0, below, above), 0), (jnp.where(core == 0, above, below), 0)]
    far = lax.rem(z + 4, 8)
    pieces += [(far, jnp.where(core == 0, 0, depth // 2)), (far, jnp.where(core == 0, depth // 2, 0))]
    for i, (place, offset) in enumerate(pieces):
        copies[i].wait()
        columns = pl.ds(pl.multiple_of(place * depth + offset, LANES), weights[i].shape[0])
        for x in range(4):
            rows = slice(x * TAPS, (x + 1) * TAPS)
            term = jnp.dot(cot_ref[rows, columns], weights[i][...], preferred_element_type=F32)
            if i:
                term = total_ref[x] + term
            if i < count - 1:
                total_ref[x] = term
            else:
                out_ref[x] = term.astype(BF16)


def lane_blocks(*lead):
    return pl.BlockSpec(lead + (LANES,), lambda l: (0,) * len(lead) + (l,))


FILTER_BLOCK = pl.BlockSpec((PER, TAPS), lambda l: (l, 0))


def spread(cotangent):
    rows, width = cotangent.shape
    return pl.pallas_call(
        spread_kernel,
        grid=(8,),
        in_specs=[pl.BlockSpec((rows, width), lambda i: (0, 0))],
        out_specs=pl.BlockSpec((4, 1, rows, width // 4), lambda i: (0, i, 0, 0)),
        out_shape=jax.ShapeDtypeStruct((4, 8, rows, width // 4), cotangent.dtype),
        compiler_params=VMEM,
        name="spread",
    )(cotangent)


def summed_copies(parts):
    return pl.pallas_call(
        sum_kernel,
        out_shape=jax.ShapeDtypeStruct(parts.shape, parts.dtype),
        compiler_params=VMEM,
        name="sums",
    )(parts)


def convolve(filters, before, mixed):
    width = mixed.shape[1]
    tile = lane_blocks(TAPS)
    return pl.pallas_call(
        conv_kernel,
        grid=(width // LANES,),
        in_specs=[FILTER_BLOCK, tile, tile],
        out_specs=[tile, lane_blocks(2 * TAPS)],
        out_shape=[jax.ShapeDtypeStruct((TAPS, width), F32), jax.ShapeDtypeStruct((2 * TAPS, width), BF16)],
        compiler_params=VMEM,
        name="conv",
    )(filters, before, mixed)


def mixed_gradient(filters, grad, after, keys, values):
    width = grad.shape[1]
    tile = lane_blocks(TAPS)
    return pl.pallas_call(
        mixed_grad_kernel,
        grid=(width // LANES,),
        in_specs=[FILTER_BLOCK, tile, tile, tile, tile],
        out_specs=[tile, tile],
        out_shape=[jax.ShapeDtypeStruct((TAPS, width), BF16)] * 2,
        compiler_params=VMEM,
        name="mixed_grad",
    )(filters, grad, after, keys, values)


def branch_gradients(terms, conv, query, turned):
    width = query.shape[1]
    tile = lane_blocks(TAPS)
    return pl.pallas_call(
        branch_kernel,
        grid=(width // LANES,),
        in_specs=[lane_blocks(terms.shape[0], TAPS), tile, tile, lane_blocks(2 * TAPS)],
        out_specs=[tile, tile, pl.BlockSpec((8, PER, TAPS), lambda l: (0, l, 0))],
        out_shape=[jax.ShapeDtypeStruct((TAPS, width), BF16)] * 2
        + [jax.ShapeDtypeStruct((8, width // GROUP, TAPS), F32)],
        compiler_params=VMEM,
        name="branch",
    )(terms, conv, query, turned)


def partial_products(cotangent, weights):
    width = weights[0].shape[1]
    place = jnp.stack([lax.axis_index(Z), lax.axis_index("co")]).astype(jnp.int32)
    whole = pl.BlockSpec(memory_space=pltpu.VMEM)
    return pl.pallas_call(
        product_kernel,
        in_specs=[pl.BlockSpec(memory_space=pltpu.SMEM), whole]
        + [pl.BlockSpec(memory_space=pltpu.HBM)] * len(weights),
        out_specs=whole,
        out_shape=jax.ShapeDtypeStruct((4, TAPS, width), BF16),
        scratch_shapes=[pltpu.VMEM((4, TAPS, width), F32)]
        + [pltpu.VMEM(a.shape, a.dtype) for a in weights]
        + [pltpu.SemaphoreType.DMA((len(weights),))],
        compiler_params=VMEM,
        name="product",
    )(place, cotangent, *weights)


def exchange(copies, axes):
    return lax.all_to_all(copies, axes, split_axis=0, concat_axis=0)


def weight_blocks(chip, beside):
    n = lax.axis_size(Z)
    route = [(2 * i, 2 * ((i + 1) % n)) for i in range(n)] + [(2 * i + 1, 2 * ((i - 1) % n) + 1) for i in range(n)]
    blocks = [chip]
    got = chip
    for _ in range(3):
        got = lax.ppermute(got, Z + ("co",), route)
        blocks += [got, swap(got, "co")]
    half = got.shape[0] // 2
    got = jnp.where(lax.axis_index("co") == 0, got[:half], got[half:])
    got, _ = lax.optimization_barrier((got, beside))
    got = lax.ppermute(got, Z + ("co",), route)
    return blocks + [got, swap(got, "co")]


def local(query_branch, key_branch, value_branch, cotangent, out_weight, filters):
    query, keys, values = query_branch[0], key_branch[0], value_branch[0]
    tokens, width = query.shape
    chip = in_order(out_weight, swap(out_weight, "co"), "co").reshape(2 * out_weight.shape[0], width)
    copies, chip = lax.optimization_barrier((spread(cotangent[0]), chip))
    gathered = exchange(copies.reshape((32,) + copies.shape[2:]), ("x", "y")).reshape(4 * TAPS, -1)

    keys, values, chip = lax.optimization_barrier((keys, values, chip))
    mixed = (keys.astype(F32) * values.astype(F32)).astype(BF16)
    conv, turned = convolve(filters, from_behind(mixed, 1), mixed)
    weights = weight_blocks(chip, conv)

    gathered, conv, turned = lax.optimization_barrier((gathered, conv, turned))
    terms = exchange(partial_products(gathered, weights), "x")
    query_grad, conv_grad, lags = branch_gradients(terms, conv, query, turned)
    lags = summed_copies(exchange(lags, ("x", "co")))
    after = from_behind(conv_grad, -1)
    lags, after = lax.optimization_barrier((lags, after))
    scale = 1.0 / math.sqrt(2 * lax.axis_size(CONTEXT) * tokens * GROUP)
    filter_grad = jnp.sum(exchange(lags, Z), axis=0) * scale
    key_grad, value_grad = mixed_gradient(filters, conv_grad, after, keys, values)
    return (query_grad[None], key_grad[None], value_grad[None], filter_grad)


def solution(mesh):
    fine = Mesh(mesh.devices.reshape(2, 4, 4, 2, 8), ("zh", "x", "zl", "co", "y"))
    branch = P("zh", CONTEXT, "y")
    return jax.shard_map(
        local,
        mesh=fine,
        in_specs=(
            branch,
            branch,
            branch,
            P("zh", CONTEXT + ("y",), None),
            P(("zh",) + CONTEXT, "y"),
            P("y", None),
        ),
        out_specs=(branch, branch, branch, P("y", None)),
        check_vma=False,
    )
```

```python
import math

import jax
import jax.numpy as jnp
from jax import lax
from jax.experimental import pallas as pl
from jax.experimental.pallas import tpu as pltpu
from jax.sharding import Mesh, PartitionSpec as P

GROUP = 16
TAPS = 128
LANES = 128
PER = LANES // GROUP
F32 = jnp.float32
BF16 = jnp.bfloat16

Z = ("zh", "zl")
CONTEXT = ("x", "zl", "co")
VMEM = pltpu.CompilerParams(vmem_limit_bytes=8 * 1024 * 1024)


def swap(block, axis):
    return lax.ppermute(block, axis, [(0, 1), (1, 0)])


def in_order(mine, theirs, axis):
    first = lax.axis_index(axis) == 0
    return jnp.stack([jnp.where(first, mine, theirs), jnp.where(first, theirs, mine)])


def from_behind(block, distance):
    n = lax.axis_size(CONTEXT)
    route = [(i - distance, i) for i in range(n) if 0 <= i - distance < n]
    return lax.ppermute(block, CONTEXT, route)


def shifted_rows(row):
    return pltpu.roll(jnp.broadcast_to(row, (TAPS, 2 * TAPS)), 0, 1, stride=1, stride_axis=0)


def lane_group(shape):
    return lax.broadcasted_iota(jnp.int32, shape, 1) >> 4


def filtered(rows, window):
    owner = lane_group((TAPS, LANES))
    total = jnp.zeros((TAPS, LANES), F32)
    for g in range(PER):
        table = shifted_rows(rows[g : g + 1, :]).astype(BF16)
        term = jnp.dot(table, window, preferred_element_type=F32)
        total = jnp.where(owner == g, term, total)
    return total


def antidiagonal(rows, columns, total):
    across = lax.broadcasted_iota(jnp.int32, (rows, columns), 0) + lax.broadcasted_iota(jnp.int32, (rows, columns), 1)
    return (across == total).astype(F32).astype(BF16)


def conv_kernel(filters_ref, before_ref, mixed_ref, conv_ref, turned_ref):
    window = jnp.concatenate([before_ref[...], mixed_ref[...]], 0)
    n = 2 * TAPS
    rows = jnp.dot(filters_ref[...], antidiagonal(TAPS, n, TAPS), preferred_element_type=F32)
    conv_ref[...] = filtered(rows, window)
    turned_ref[...] = jnp.dot(antidiagonal(n, n, n - 1), window, preferred_element_type=F32).astype(BF16)


def mixed_grad_kernel(filters_ref, grad_ref, after_ref, key_ref, value_ref, key_grad_ref, value_grad_ref):
    window = jnp.concatenate([grad_ref[...], after_ref[...]], 0)
    taps = filters_ref[...].astype(F32)
    mixed_grad = filtered(jnp.concatenate([taps, jnp.zeros(taps.shape, F32)], 1), window)
    key_grad_ref[...] = (mixed_grad * value_ref[...].astype(F32)).astype(BF16)
    value_grad_ref[...] = (mixed_grad * key_ref[...].astype(F32)).astype(BF16)


def spread_kernel(cot_ref, out_ref):
    size = cot_ref.shape[1] // 8
    for x in range(4):
        for zh in range(2):
            out_ref[x, 0, :, zh * size : (zh + 1) * size] = cot_ref[:, (4 * zh + x) * size : (4 * zh + x + 1) * size]


def sum_kernel(parts_ref, out_ref):
    total = jnp.sum(parts_ref[...], axis=0)
    for i in range(out_ref.shape[0]):
        out_ref[i] = total


def branch_kernel(terms_ref, conv_ref, query_ref, turned_ref, query_grad_ref, conv_grad_ref, lag_ref):
    branch_grad = terms_ref[0].astype(F32)
    for x in range(1, terms_ref.shape[0]):
        branch_grad = branch_grad + terms_ref[x].astype(F32)
    query_grad_ref[...] = (branch_grad * conv_ref[...]).astype(BF16)
    conv_grad = (branch_grad * query_ref[...].astype(F32)).astype(BF16)
    conv_grad_ref[...] = conv_grad
    owner = lane_group((TAPS, LANES))
    wide = conv_grad.astype(F32)
    for g in range(PER):
        part = jnp.where(owner == g, wide, 0.0).astype(BF16)
        outer = lax.dot_general(part, turned_ref[...], (((1,), (1,)), ((), ())), preferred_element_type=F32)
        skewed = pltpu.roll(outer, 1, 1, stride=1, stride_axis=0)
        sums = jnp.sum(skewed, axis=0, keepdims=True)[:, TAPS:]
        for copy in range(lag_ref.shape[0]):
            lag_ref[copy, g : g + 1, :] = sums


def product_kernel(place_ref, cot_ref, *refs):
    count = (len(refs) - 3) // 2
    weights_hbm, out_ref, total_ref, weights, sems = refs[:count], refs[count], refs[count + 1], refs[count + 2 : -1], refs[-1]
    copies = [pltpu.make_async_copy(weights_hbm[i], weights[i], sems.at[i]) for i in range(count)]
    for copy in copies:
        copy.start()
    z, core = place_ref[0], place_ref[1]
    depth = weights[0].shape[0]
    pieces = [z]
    for step in (1, 2, 3):
        below, above = lax.rem(z + 8 - step, 8), lax.rem(z + step, 8)
        pieces += [jnp.where(core == 0, below, above), jnp.where(core == 0, above, below)]
    pieces.append(lax.rem(z + 4, 8))
    for i, place in enumerate(pieces):
        copies[i].wait()
        columns = pl.ds(pl.multiple_of(place * depth, LANES), depth)
        for x in range(4):
            rows = slice(x * TAPS, (x + 1) * TAPS)
            term = jnp.dot(cot_ref[rows, columns], weights[i][...], preferred_element_type=F32)
            if i:
                term = total_ref[x] + term
            if i < count - 1:
                total_ref[x] = term
            else:
                out_ref[x] = term.astype(BF16)


def lane_blocks(*lead):
    return pl.BlockSpec(lead + (LANES,), lambda l: (0,) * len(lead) + (l,))


FILTER_BLOCK = pl.BlockSpec((PER, TAPS), lambda l: (l, 0))


def spread(cotangent):
    rows, width = cotangent.shape
    return pl.pallas_call(
        spread_kernel,
        grid=(8,),
        in_specs=[pl.BlockSpec((rows, width), lambda i: (0, 0))],
        out_specs=pl.BlockSpec((4, 1, rows, width // 4), lambda i: (0, i, 0, 0)),
        out_shape=jax.ShapeDtypeStruct((4, 8, rows, width // 4), cotangent.dtype),
        compiler_params=VMEM,
        name="spread",
    )(cotangent)


def summed_copies(parts):
    return pl.pallas_call(
        sum_kernel,
        out_shape=jax.ShapeDtypeStruct(parts.shape, parts.dtype),
        compiler_params=VMEM,
        name="sums",
    )(parts)


def convolve(filters, before, mixed):
    width = mixed.shape[1]
    tile = lane_blocks(TAPS)
    return pl.pallas_call(
        conv_kernel,
        grid=(width // LANES,),
        in_specs=[FILTER_BLOCK, tile, tile],
        out_specs=[tile, lane_blocks(2 * TAPS)],
        out_shape=[jax.ShapeDtypeStruct((TAPS, width), F32), jax.ShapeDtypeStruct((2 * TAPS, width), BF16)],
        compiler_params=VMEM,
        name="conv",
    )(filters, before, mixed)


def mixed_gradient(filters, grad, after, keys, values):
    width = grad.shape[1]
    tile = lane_blocks(TAPS)
    return pl.pallas_call(
        mixed_grad_kernel,
        grid=(width // LANES,),
        in_specs=[FILTER_BLOCK, tile, tile, tile, tile],
        out_specs=[tile, tile],
        out_shape=[jax.ShapeDtypeStruct((TAPS, width), BF16)] * 2,
        compiler_params=VMEM,
        name="mixed_grad",
    )(filters, grad, after, keys, values)


def branch_gradients(terms, conv, query, turned):
    width = query.shape[1]
    tile = lane_blocks(TAPS)
    return pl.pallas_call(
        branch_kernel,
        grid=(width // LANES,),
        in_specs=[lane_blocks(terms.shape[0], TAPS), tile, tile, lane_blocks(2 * TAPS)],
        out_specs=[tile, tile, pl.BlockSpec((8, PER, TAPS), lambda l: (0, l, 0))],
        out_shape=[jax.ShapeDtypeStruct((TAPS, width), BF16)] * 2
        + [jax.ShapeDtypeStruct((8, width // GROUP, TAPS), F32)],
        compiler_params=VMEM,
        name="branch",
    )(terms, conv, query, turned)


def partial_products(cotangent, weights):
    width = weights[0].shape[1]
    place = jnp.stack([lax.axis_index(Z), lax.axis_index("co")]).astype(jnp.int32)
    whole = pl.BlockSpec(memory_space=pltpu.VMEM)
    return pl.pallas_call(
        product_kernel,
        in_specs=[pl.BlockSpec(memory_space=pltpu.SMEM), whole]
        + [pl.BlockSpec(memory_space=pltpu.HBM)] * len(weights),
        out_specs=whole,
        out_shape=jax.ShapeDtypeStruct((4, TAPS, width), BF16),
        scratch_shapes=[pltpu.VMEM((4, TAPS, width), F32)]
        + [pltpu.VMEM(a.shape, a.dtype) for a in weights]
        + [pltpu.SemaphoreType.DMA((len(weights),))],
        compiler_params=VMEM,
        name="product",
    )(place, cotangent, *weights)


def exchange(copies, axes):
    return lax.all_to_all(copies, axes, split_axis=0, concat_axis=0)


def weight_blocks(chip, beside):
    n = lax.axis_size(Z)
    route = [(2 * i, 2 * ((i + 1) % n)) for i in range(n)] + [(2 * i + 1, 2 * ((i - 1) % n) + 1) for i in range(n)]
    blocks = [chip]
    got = chip
    for _ in range(n // 2 - 1):
        got = lax.ppermute(got, Z + ("co",), route)
        got, beside = lax.optimization_barrier((got, beside))
        beside = swap(got, "co")
        blocks += [got, beside]
    return blocks + [lax.ppermute(got, Z + ("co",), route)]


def local(query_branch, key_branch, value_branch, cotangent, out_weight, filters):
    query, keys, values = query_branch[0], key_branch[0], value_branch[0]
    tokens, width = query.shape
    chip = in_order(out_weight, swap(out_weight, "co"), "co").reshape(2 * out_weight.shape[0], width)
    copies = spread(cotangent[0])
    gathered = exchange(copies.reshape((32,) + copies.shape[2:]), ("x", "y")).reshape(4 * TAPS, -1)

    keys, values, chip = lax.optimization_barrier((keys, values, chip))
    mixed = (keys.astype(F32) * values.astype(F32)).astype(BF16)
    conv, turned = convolve(filters, from_behind(mixed, 1), mixed)
    weights = weight_blocks(chip, conv)

    gathered, conv, turned = lax.optimization_barrier((gathered, conv, turned))
    terms = exchange(partial_products(gathered, weights), "x")
    query_grad, conv_grad, lags = branch_gradients(terms, conv, query, turned)
    lags = summed_copies(exchange(lags, ("x", "co")))
    after = from_behind(conv_grad, -1)
    lags, after = lax.optimization_barrier((lags, after))
    scale = 1.0 / math.sqrt(2 * lax.axis_size(CONTEXT) * tokens * GROUP)
    filter_grad = jnp.sum(exchange(lags, Z), axis=0) * scale
    key_grad, value_grad = mixed_gradient(filters, conv_grad, after, keys, values)
    return (query_grad[None], key_grad[None], value_grad[None], filter_grad)


def solution(mesh):
    fine = Mesh(mesh.devices.reshape(2, 4, 4, 2, 8), ("zh", "x", "zl", "co", "y"))
    branch = P("zh", CONTEXT, "y")
    return jax.shard_map(
        local,
        mesh=fine,
        in_specs=(
            branch,
            branch,
            branch,
            P("zh", CONTEXT + ("y",), None),
            P(("zh",) + CONTEXT, "y"),
            P("y", None),
        ),
        out_specs=(branch, branch, branch, P("y", None)),
        check_vma=False,
    )
```

```python
import math

import jax
import jax.numpy as jnp
from jax import lax
from jax.experimental import pallas as pl
from jax.experimental.pallas import tpu as pltpu
from jax.sharding import Mesh, PartitionSpec as P

GROUP = 16
TAPS = 128
LANES = 128
PER = LANES // GROUP
F32 = jnp.float32
BF16 = jnp.bfloat16

Z = ("zh", "zl")
CONTEXT = ("x", "zl", "co")
Y = ("yq", "yp")
VMEM = pltpu.CompilerParams(vmem_limit_bytes=8 * 1024 * 1024)


def swap(block, axis):
    return lax.ppermute(block, axis, [(0, 1), (1, 0)])


def in_order(mine, theirs, axis):
    first = lax.axis_index(axis) == 0
    return jnp.stack([jnp.where(first, mine, theirs), jnp.where(first, theirs, mine)])


def from_behind(block, distance):
    n = lax.axis_size(CONTEXT)
    route = [(i - distance, i) for i in range(n) if 0 <= i - distance < n]
    return lax.ppermute(block, CONTEXT, route)


def shifted_rows(row):
    return pltpu.roll(jnp.broadcast_to(row, (TAPS, 2 * TAPS)), 0, 1, stride=1, stride_axis=0)


def lane_group(shape):
    return lax.broadcasted_iota(jnp.int32, shape, 1) >> 4


def filtered(rows, window):
    owner = lane_group((TAPS, LANES))
    total = jnp.zeros((TAPS, LANES), F32)
    for g in range(PER):
        table = shifted_rows(rows[g : g + 1, :]).astype(BF16)
        term = jnp.dot(table, window, preferred_element_type=F32)
        total = jnp.where(owner == g, term, total)
    return total


def antidiagonal(rows, columns, total):
    across = lax.broadcasted_iota(jnp.int32, (rows, columns), 0) + lax.broadcasted_iota(jnp.int32, (rows, columns), 1)
    return (across == total).astype(F32).astype(BF16)


def conv_kernel(filters_ref, before_ref, mixed_ref, conv_ref, turned_ref):
    window = jnp.concatenate([before_ref[...], mixed_ref[...]], 0)
    n = 2 * TAPS
    rows = jnp.dot(filters_ref[...], antidiagonal(TAPS, n, TAPS), preferred_element_type=F32)
    conv_ref[...] = filtered(rows, window)
    turned_ref[...] = jnp.dot(antidiagonal(n, n, n - 1), window, preferred_element_type=F32).astype(BF16)


def mixed_grad_kernel(filters_ref, grad_ref, after_ref, key_ref, value_ref, key_grad_ref, value_grad_ref):
    window = jnp.concatenate([grad_ref[...], after_ref[...]], 0)
    taps = filters_ref[...].astype(F32)
    mixed_grad = filtered(jnp.concatenate([taps, jnp.zeros(taps.shape, F32)], 1), window)
    key_grad_ref[...] = (mixed_grad * value_ref[...].astype(F32)).astype(BF16)
    value_grad_ref[...] = (mixed_grad * key_ref[...].astype(F32)).astype(BF16)


def spread_kernel(cot_ref, out_ref):
    size = cot_ref.shape[1] // 8
    for x in range(4):
        for zh in range(2):
            out_ref[x, 0, :, zh * size : (zh + 1) * size] = cot_ref[:, (4 * zh + x) * size : (4 * zh + x + 1) * size]


def sum_kernel(parts_ref, out_ref):
    total = jnp.sum(parts_ref[...], axis=0)
    for i in range(out_ref.shape[0]):
        out_ref[i] = total


def branch_kernel(terms_ref, conv_ref, query_ref, turned_ref, query_grad_ref, conv_grad_ref, lag_ref):
    branch_grad = terms_ref[0].astype(F32)
    for x in range(1, terms_ref.shape[0]):
        branch_grad = branch_grad + terms_ref[x].astype(F32)
    query_grad_ref[...] = (branch_grad * conv_ref[...]).astype(BF16)
    conv_grad = (branch_grad * query_ref[...].astype(F32)).astype(BF16)
    conv_grad_ref[...] = conv_grad
    owner = lane_group((TAPS, LANES))
    wide = conv_grad.astype(F32)
    for g in range(PER):
        part = jnp.where(owner == g, wide, 0.0).astype(BF16)
        outer = lax.dot_general(part, turned_ref[...], (((1,), (1,)), ((), ())), preferred_element_type=F32)
        skewed = pltpu.roll(outer, 1, 1, stride=1, stride_axis=0)
        sums = jnp.sum(skewed, axis=0, keepdims=True)[:, TAPS:]
        for copy in range(lag_ref.shape[0]):
            lag_ref[copy, g : g + 1, :] = sums


def product_kernel(place_ref, own_ref, low_ref, high_ref, *refs):
    count = (len(refs) - 3) // 2
    weights_hbm, out_ref, total_ref, weights, sems = refs[:count], refs[count], refs[count + 1], refs[count + 2 : -1], refs[-1]
    copies = [pltpu.make_async_copy(weights_hbm[i], weights[i], sems.at[i]) for i in range(count)]
    for copy in copies:
        copy.start()
    z, core, odd = place_ref[0], place_ref[1], place_ref[2]
    depth = weights[0].shape[0]
    pieces = [z]
    for step in (1, 2, 3):
        below, above = lax.rem(z + 8 - step, 8), lax.rem(z + step, 8)
        pieces += [jnp.where(core == 0, below, above), jnp.where(core == 0, above, below)]
    pieces.append(lax.rem(z + 4, 8))
    half = own_ref.shape[0] // 2
    parts = ((own_ref, 0), (own_ref, half), (low_ref, 0), (high_ref, 0))
    for i, place in enumerate(pieces):
        copies[i].wait()
        columns = pl.ds(pl.multiple_of(place * depth, LANES), depth)
        for j, (cot_ref, first) in enumerate(parts):
            term = jnp.dot(cot_ref[first : first + half, columns], weights[i][...], preferred_element_type=F32)
            if i:
                term = total_ref[j] + term
            if i < count - 1:
                total_ref[j] = term
                continue
            term = term.astype(BF16).reshape(2, 4, 16, term.shape[1])
            for x in range(2):
                for pair in range(4):
                    out_ref[2 * (j % 2) + x, pair, odd if j < 2 else 1 - odd] = term[x, pair]


def lane_blocks(*lead):
    return pl.BlockSpec(lead + (LANES,), lambda l: (0,) * len(lead) + (l,))


FILTER_BLOCK = pl.BlockSpec((PER, TAPS), lambda l: (l, 0))


def spread(cotangent):
    rows, width = cotangent.shape
    return pl.pallas_call(
        spread_kernel,
        grid=(4,),
        in_specs=[pl.BlockSpec((rows, width), lambda i: (0, 0))],
        out_specs=pl.BlockSpec((4, 1, rows, width // 4), lambda i: (0, i, 0, 0)),
        out_shape=jax.ShapeDtypeStruct((4, 4, rows, width // 4), cotangent.dtype),
        compiler_params=VMEM,
        name="spread",
    )(cotangent)


def summed_copies(parts):
    return pl.pallas_call(
        sum_kernel,
        out_shape=jax.ShapeDtypeStruct(parts.shape, parts.dtype),
        compiler_params=VMEM,
        name="sums",
    )(parts)


def convolve(filters, before, mixed):
    width = mixed.shape[1]
    tile = lane_blocks(TAPS)
    return pl.pallas_call(
        conv_kernel,
        grid=(width // LANES,),
        in_specs=[FILTER_BLOCK, tile, tile],
        out_specs=[tile, lane_blocks(2 * TAPS)],
        out_shape=[jax.ShapeDtypeStruct((TAPS, width), F32), jax.ShapeDtypeStruct((2 * TAPS, width), BF16)],
        compiler_params=VMEM,
        name="conv",
    )(filters, before, mixed)


def mixed_gradient(filters, grad, after, keys, values):
    width = grad.shape[1]
    tile = lane_blocks(TAPS)
    return pl.pallas_call(
        mixed_grad_kernel,
        grid=(width // LANES,),
        in_specs=[FILTER_BLOCK, tile, tile, tile, tile],
        out_specs=[tile, tile],
        out_shape=[jax.ShapeDtypeStruct((TAPS, width), BF16)] * 2,
        compiler_params=VMEM,
        name="mixed_grad",
    )(filters, grad, after, keys, values)


def branch_gradients(terms, conv, query, turned):
    width = query.shape[1]
    tile = lane_blocks(TAPS)
    return pl.pallas_call(
        branch_kernel,
        grid=(width // LANES,),
        in_specs=[lane_blocks(terms.shape[0], TAPS), tile, tile, lane_blocks(2 * TAPS)],
        out_specs=[tile, tile, pl.BlockSpec((8, PER, TAPS), lambda l: (0, l, 0))],
        out_shape=[jax.ShapeDtypeStruct((TAPS, width), BF16)] * 2
        + [jax.ShapeDtypeStruct((8, width // GROUP, TAPS), F32)],
        compiler_params=VMEM,
        name="branch",
    )(terms, conv, query, turned)


def partial_products(parts, weights):
    width = weights[0].shape[1]
    place = jnp.stack([lax.axis_index(Z), lax.axis_index("co"), lax.axis_index("yp")]).astype(jnp.int32)
    whole = pl.BlockSpec(memory_space=pltpu.VMEM)
    out = pl.pallas_call(
        product_kernel,
        in_specs=[pl.BlockSpec(memory_space=pltpu.SMEM)]
        + [whole] * 3
        + [pl.BlockSpec(memory_space=pltpu.HBM)] * len(weights),
        out_specs=whole,
        out_shape=jax.ShapeDtypeStruct((4, 4, 2, 16, width), BF16),
        scratch_shapes=[pltpu.VMEM((4, TAPS, width), F32)]
        + [pltpu.VMEM(a.shape, a.dtype) for a in weights]
        + [pltpu.SemaphoreType.DMA((len(weights),))],
        compiler_params=VMEM,
        name="product",
    )(place, *parts, *weights)
    return out.reshape(4, TAPS, width)


def exchange(copies, axes):
    return lax.all_to_all(copies, axes, split_axis=0, concat_axis=0)


def ahead(block, axes, distance):
    n = lax.axis_size(axes)
    return lax.ppermute(block, axes, [((i + distance) % n, i) for i in range(n)])


def along_z(block, steps):
    n = lax.axis_size(Z)
    route = [(2 * i, 2 * ((i + steps) % n)) for i in range(n)]
    route += [(2 * i + 1, 2 * ((i - steps) % n) + 1) for i in range(n)]
    return lax.ppermute(block, Z + ("co",), route)


def weight_blocks(chip):
    one, two = along_z(chip, 1), along_z(chip, 2)
    three, four = along_z(two, 1), along_z(two, 2)
    return [chip, one, swap(one, "co"), two, swap(two, "co"), three, swap(three, "co"), four]


def cotangent_parts(cotangent):
    copies = spread(cotangent)
    rows, width = copies.shape[2:]
    own = exchange(copies.reshape(16, rows, width), ("x", "yq"))
    low, high = ahead(own[:8], Y, -1), ahead(own[8:], Y, 1)
    return [part.reshape(-1, width) for part in (own, low, high)]


def local(query_branch, key_branch, value_branch, cotangent, out_weight, filters):
    query, keys, values = query_branch[0], key_branch[0], value_branch[0]
    tokens, width = query.shape
    chip = in_order(out_weight, swap(out_weight, "co"), "co").reshape(2 * out_weight.shape[0], width)
    parts = cotangent_parts(cotangent[0])

    keys, values, chip = lax.optimization_barrier((keys, values, chip))
    mixed = (keys.astype(F32) * values.astype(F32)).astype(BF16)
    conv, turned = convolve(filters, from_behind(mixed, 1), mixed)
    weights = weight_blocks(chip)

    parts, conv, turned = lax.optimization_barrier((parts, conv, turned))
    terms = exchange(partial_products(parts, weights), "x")
    query_grad, conv_grad, lags = branch_gradients(terms, conv, query, turned)
    lags = summed_copies(exchange(lags, ("x", "co")))
    after = from_behind(conv_grad, -1)
    lags, after = lax.optimization_barrier((lags, after))
    scale = 1.0 / math.sqrt(2 * lax.axis_size(CONTEXT) * tokens * GROUP)
    filter_grad = jnp.sum(exchange(lags, Z), axis=0) * scale
    key_grad, value_grad = mixed_gradient(filters, conv_grad, after, keys, values)
    return (query_grad[None], key_grad[None], value_grad[None], filter_grad)


def solution(mesh):
    fine = Mesh(mesh.devices.reshape(2, 4, 4, 2, 4, 2), ("zh", "x", "zl", "co", "yq", "yp"))
    branch = P("zh", CONTEXT, Y)
    return jax.shard_map(
        local,
        mesh=fine,
        in_specs=(
            branch,
            branch,
            branch,
            P("zh", CONTEXT + Y, None),
            P(("zh",) + CONTEXT, Y),
            P(Y, None),
        ),
        out_specs=(branch, branch, branch, P(Y, None)),
        check_vma=False,
    )
```

```python
import math

import jax
import jax.numpy as jnp
from jax import lax
from jax.experimental import pallas as pl
from jax.experimental.pallas import tpu as pltpu
from jax.sharding import Mesh, PartitionSpec as P

GROUP = 16
TAPS = 128
LANES = 128
PER = LANES // GROUP
F32 = jnp.float32
BF16 = jnp.bfloat16

Z = ("zh", "zl")
CONTEXT = ("x", "zl", "co")
Y = ("yq", "yp")
VMEM = pltpu.CompilerParams(vmem_limit_bytes=8 * 1024 * 1024)


def swap(block, axis):
    return lax.ppermute(block, axis, [(0, 1), (1, 0)])


def in_order(mine, theirs, axis):
    first = lax.axis_index(axis) == 0
    return jnp.stack([jnp.where(first, mine, theirs), jnp.where(first, theirs, mine)])


def from_behind(block, distance):
    n = lax.axis_size(CONTEXT)
    route = [(i - distance, i) for i in range(n) if 0 <= i - distance < n]
    return lax.ppermute(block, CONTEXT, route)


def shifted_rows(row):
    rows = pltpu.roll(jnp.broadcast_to(row, (8, 2 * TAPS)), 0, 1, stride=1, stride_axis=0)
    while rows.shape[0] < TAPS:
        rows = jnp.concatenate([rows, pltpu.roll(rows, rows.shape[0], 1)], 0)
    return rows


def skewed_sum(rows):
    while rows.shape[0] > 8:
        half = rows.shape[0] // 2
        rows = rows[:half] + pltpu.roll(rows[half:], half, 1)
    return jnp.sum(pltpu.roll(rows, 1, 1, stride=1, stride_axis=0), axis=0, keepdims=True)


def lane_group(shape):
    return lax.broadcasted_iota(jnp.int32, shape, 1) >> 4


def filtered(rows, window):
    owner = lane_group((TAPS, LANES))
    total = jnp.zeros((TAPS, LANES), F32)
    for g in range(PER):
        table = shifted_rows(rows[g : g + 1, :]).astype(BF16)
        term = jnp.dot(table, window, preferred_element_type=F32)
        total = jnp.where(owner == g, term, total)
    return total


def antidiagonal(rows, columns, total):
    across = lax.broadcasted_iota(jnp.int32, (rows, columns), 0) + lax.broadcasted_iota(jnp.int32, (rows, columns), 1)
    return (across == total).astype(F32).astype(BF16)


def conv_kernel(filters_ref, before_ref, mixed_ref, conv_ref, turned_ref):
    window = jnp.concatenate([before_ref[...], mixed_ref[...]], 0)
    n = 2 * TAPS
    rows = jnp.dot(filters_ref[...], antidiagonal(TAPS, n, TAPS), preferred_element_type=F32)
    conv_ref[...] = filtered(rows, window)
    turned_ref[...] = jnp.dot(antidiagonal(n, n, n - 1), window, preferred_element_type=F32).astype(BF16)


def mixed_grad_kernel(filters_ref, grad_ref, after_ref, key_ref, value_ref, key_grad_ref, value_grad_ref):
    window = jnp.concatenate([grad_ref[...], after_ref[...]], 0)
    taps = filters_ref[...].astype(F32)
    mixed_grad = filtered(jnp.concatenate([taps, jnp.zeros(taps.shape, F32)], 1), window)
    key_grad_ref[...] = (mixed_grad * value_ref[...].astype(F32)).astype(BF16)
    value_grad_ref[...] = (mixed_grad * key_ref[...].astype(F32)).astype(BF16)


def spread_kernel(cot_ref, out_ref):
    size = cot_ref.shape[1] // 8
    for x in range(4):
        for zh in range(2):
            out_ref[x, 0, :, zh * size : (zh + 1) * size] = cot_ref[:, (4 * zh + x) * size : (4 * zh + x + 1) * size]


def sum_kernel(parts_ref, out_ref):
    total = jnp.sum(parts_ref[...], axis=0)
    for i in range(out_ref.shape[0]):
        out_ref[i] = total


def branch_kernel(terms_ref, conv_ref, query_ref, turned_ref, query_grad_ref, conv_grad_ref, lag_ref):
    branch_grad = terms_ref[0].astype(F32)
    for x in range(1, terms_ref.shape[0]):
        branch_grad = branch_grad + terms_ref[x].astype(F32)
    query_grad_ref[...] = (branch_grad * conv_ref[...]).astype(BF16)
    conv_grad = (branch_grad * query_ref[...].astype(F32)).astype(BF16)
    conv_grad_ref[...] = conv_grad
    owner = lane_group((TAPS, LANES))
    wide = conv_grad.astype(F32)
    for g in range(PER):
        part = jnp.where(owner == g, wide, 0.0).astype(BF16)
        outer = lax.dot_general(part, turned_ref[...], (((1,), (1,)), ((), ())), preferred_element_type=F32)
        sums = skewed_sum(outer)[:, TAPS:]
        for copy in range(lag_ref.shape[0]):
            lag_ref[copy, g : g + 1, :] = sums


def product_kernel(place_ref, own_ref, low_ref, high_ref, *refs):
    count = (len(refs) - 3) // 2
    weights_hbm, out_ref, total_ref, weights, sems = refs[:count], refs[count], refs[count + 1], refs[count + 2 : -1], refs[-1]
    copies = [pltpu.make_async_copy(weights_hbm[i], weights[i], sems.at[i]) for i in range(count)]
    for copy in copies:
        copy.start()
    z, core, odd = place_ref[0], place_ref[1], place_ref[2]
    depth = weights[0].shape[0]
    below, above = [lax.rem(z + 8 - i, 8) for i in range(4)], [lax.rem(z + i, 8) for i in range(4)]
    mine = [jnp.where(core == 0, b, a) for b, a in zip(below, above)]
    theirs = [jnp.where(core == 0, a, b) for b, a in zip(below, above)]
    pieces = [(0, 0, z), (1, 0, mine[1]), (2, 0, theirs[1]), (3, 0, lax.rem(z + 4, 8))]
    pieces += [(4, 0, mine[2]), (4, depth, mine[3]), (5, 0, theirs[2]), (5, depth, theirs[3])]
    half = own_ref.shape[0] // 2
    parts = ((own_ref, 0), (own_ref, half), (low_ref, 0), (high_ref, 0))
    for n, (i, offset, place) in enumerate(pieces):
        if offset == 0:
            copies[i].wait()
        weight = weights[i][offset : offset + depth, :]
        columns = pl.ds(pl.multiple_of(place * depth, LANES), depth)
        for j, (cot_ref, first) in enumerate(parts):
            term = jnp.dot(cot_ref[first : first + half, columns], weight, preferred_element_type=F32)
            if n:
                term = total_ref[j] + term
            if n < len(pieces) - 1:
                total_ref[j] = term
                continue
            term = term.astype(BF16).reshape(2, 4, 16, term.shape[1])
            for x in range(2):
                for pair in range(4):
                    out_ref[2 * (j % 2) + x, pair, odd if j < 2 else 1 - odd] = term[x, pair]


def lane_blocks(*lead):
    return pl.BlockSpec(lead + (LANES,), lambda l: (0,) * len(lead) + (l,))


FILTER_BLOCK = pl.BlockSpec((PER, TAPS), lambda l: (l, 0))


def spread(cotangent):
    rows, width = cotangent.shape
    return pl.pallas_call(
        spread_kernel,
        grid=(4,),
        in_specs=[pl.BlockSpec((rows, width), lambda i: (0, 0))],
        out_specs=pl.BlockSpec((4, 1, rows, width // 4), lambda i: (0, i, 0, 0)),
        out_shape=jax.ShapeDtypeStruct((4, 4, rows, width // 4), cotangent.dtype),
        compiler_params=VMEM,
        name="spread",
    )(cotangent)


def summed_copies(parts):
    return pl.pallas_call(
        sum_kernel,
        out_shape=jax.ShapeDtypeStruct(parts.shape, parts.dtype),
        compiler_params=VMEM,
        name="sums",
    )(parts)


def convolve(filters, before, mixed):
    width = mixed.shape[1]
    tile = lane_blocks(TAPS)
    return pl.pallas_call(
        conv_kernel,
        grid=(width // LANES,),
        in_specs=[FILTER_BLOCK, tile, tile],
        out_specs=[tile, lane_blocks(2 * TAPS)],
        out_shape=[jax.ShapeDtypeStruct((TAPS, width), F32), jax.ShapeDtypeStruct((2 * TAPS, width), BF16)],
        compiler_params=VMEM,
        name="conv",
    )(filters, before, mixed)


def mixed_gradient(filters, grad, after, keys, values):
    width = grad.shape[1]
    tile = lane_blocks(TAPS)
    return pl.pallas_call(
        mixed_grad_kernel,
        grid=(width // LANES,),
        in_specs=[FILTER_BLOCK, tile, tile, tile, tile],
        out_specs=[tile, tile],
        out_shape=[jax.ShapeDtypeStruct((TAPS, width), BF16)] * 2,
        compiler_params=VMEM,
        name="mixed_grad",
    )(filters, grad, after, keys, values)


def branch_gradients(terms, conv, query, turned):
    width = query.shape[1]
    tile = lane_blocks(TAPS)
    return pl.pallas_call(
        branch_kernel,
        grid=(width // LANES,),
        in_specs=[lane_blocks(terms.shape[0], TAPS), tile, tile, lane_blocks(2 * TAPS)],
        out_specs=[tile, tile, pl.BlockSpec((8, PER, TAPS), lambda l: (0, l, 0))],
        out_shape=[jax.ShapeDtypeStruct((TAPS, width), BF16)] * 2
        + [jax.ShapeDtypeStruct((8, width // GROUP, TAPS), F32)],
        compiler_params=VMEM,
        name="branch",
    )(terms, conv, query, turned)


def partial_products(parts, weights):
    width = weights[0].shape[1]
    place = jnp.stack([lax.axis_index(Z), lax.axis_index("co"), lax.axis_index("yp")]).astype(jnp.int32)
    whole = pl.BlockSpec(memory_space=pltpu.VMEM)
    out = pl.pallas_call(
        product_kernel,
        in_specs=[pl.BlockSpec(memory_space=pltpu.SMEM)]
        + [whole] * 3
        + [pl.BlockSpec(memory_space=pltpu.HBM)] * len(weights),
        out_specs=whole,
        out_shape=jax.ShapeDtypeStruct((4, 4, 2, 16, width), BF16),
        scratch_shapes=[pltpu.VMEM((4, TAPS, width), F32)]
        + [pltpu.VMEM(a.shape, a.dtype) for a in weights]
        + [pltpu.SemaphoreType.DMA((len(weights),))],
        compiler_params=VMEM,
        name="product",
    )(place, *parts, *weights)
    return out.reshape(4, TAPS, width)


def exchange(copies, axes):
    return lax.all_to_all(copies, axes, split_axis=0, concat_axis=0)


def ahead(block, axes, distance):
    n = lax.axis_size(axes)
    return lax.ppermute(block, axes, [((i + distance) % n, i) for i in range(n)])


def along_z(block, steps):
    n = lax.axis_size(Z)
    route = [(2 * i, 2 * ((i + steps) % n)) for i in range(n)]
    route += [(2 * i + 1, 2 * ((i - steps) % n) + 1) for i in range(n)]
    return lax.ppermute(block, Z + ("co",), route)


def weight_blocks(chip):
    one, four = along_z(chip, 1), along_z(chip, 4)
    pair = along_z(jnp.concatenate([chip, one], 0), 2)
    return [chip, one, swap(one, "co"), four, pair, swap(pair, "co")]


def local(query_branch, key_branch, value_branch, cotangent, out_weight, filters):
    query, keys, values = query_branch[0], key_branch[0], value_branch[0]
    tokens, width = query.shape
    chip = in_order(out_weight, swap(out_weight, "co"), "co").reshape(2 * out_weight.shape[0], width)
    weights = weight_blocks(chip)

    copies = spread(cotangent[0])
    rows, columns = copies.shape[2:]
    own = exchange(copies.reshape(16, rows, columns), ("x", "yq"))
    own, weights[2], weights[3] = lax.optimization_barrier((own, weights[2], weights[3]))
    low, high = ahead(own[:8], Y, -1), ahead(own[8:], Y, 1)
    parts = [part.reshape(-1, columns) for part in (own, low, high)]

    keys, values, own = lax.optimization_barrier((keys, values, own))
    mixed = (keys.astype(F32) * values.astype(F32)).astype(BF16)
    conv, turned = convolve(filters, from_behind(mixed, 1), mixed)
    parts, conv, turned = lax.optimization_barrier((parts, conv, turned))
    terms = exchange(partial_products(parts, weights), "x")
    query_grad, conv_grad, lags = branch_gradients(terms, conv, query, turned)
    lags = summed_copies(exchange(lags, ("x", "co")))
    after = from_behind(conv_grad, -1)
    lags, after = lax.optimization_barrier((lags, after))
    scale = 1.0 / math.sqrt(2 * lax.axis_size(CONTEXT) * tokens * GROUP)
    filter_grad = jnp.sum(exchange(lags, Z), axis=0) * scale
    key_grad, value_grad = mixed_gradient(filters, conv_grad, after, keys, values)
    return (query_grad[None], key_grad[None], value_grad[None], filter_grad)


def solution(mesh):
    fine = Mesh(mesh.devices.reshape(2, 4, 4, 2, 4, 2), ("zh", "x", "zl", "co", "yq", "yp"))
    branch = P("zh", CONTEXT, Y)
    return jax.shard_map(
        local,
        mesh=fine,
        in_specs=(
            branch,
            branch,
            branch,
            P("zh", CONTEXT + Y, None),
            P(("zh",) + CONTEXT, Y),
            P(Y, None),
        ),
        out_specs=(branch, branch, branch, P(Y, None)),
        check_vma=False,
    )
```

```python
import math

import jax
import jax.numpy as jnp
from jax import lax
from jax.experimental import pallas as pl
from jax.experimental.pallas import tpu as pltpu
from jax.sharding import Mesh, PartitionSpec as P

GROUP = 16
TAPS = 128
LANES = 128
PER = LANES // GROUP
F32 = jnp.float32
BF16 = jnp.bfloat16

Z = ("zh", "zl")
CONTEXT = ("x", "zl", "co")
Y = ("yq", "yp")
VMEM = pltpu.CompilerParams(vmem_limit_bytes=8 * 1024 * 1024)


def swap(block, axis):
    return lax.ppermute(block, axis, [(0, 1), (1, 0)])


def in_order(mine, theirs, axis):
    first = lax.axis_index(axis) == 0
    return jnp.stack([jnp.where(first, mine, theirs), jnp.where(first, theirs, mine)])


def from_behind(block, distance):
    n = lax.axis_size(CONTEXT)
    route = [(i - distance, i) for i in range(n) if 0 <= i - distance < n]
    return lax.ppermute(block, CONTEXT, route)


def shifted_rows(row):
    return pltpu.roll(jnp.broadcast_to(row, (TAPS, 2 * TAPS)), 0, 1, stride=1, stride_axis=0)


def skewed_sum(rows):
    return jnp.sum(pltpu.roll(rows, 1, 1, stride=1, stride_axis=0), axis=0, keepdims=True)


def lane_group(shape):
    return lax.broadcasted_iota(jnp.int32, shape, 1) >> 4


def filtered(rows, window):
    owner = lane_group((TAPS, LANES))
    total = jnp.zeros((TAPS, LANES), F32)
    for g in range(PER):
        table = shifted_rows(rows[g : g + 1, :]).astype(BF16)
        term = jnp.dot(table, window, preferred_element_type=F32)
        total = jnp.where(owner == g, term, total)
    return total


def antidiagonal(rows, columns, total):
    across = lax.broadcasted_iota(jnp.int32, (rows, columns), 0) + lax.broadcasted_iota(jnp.int32, (rows, columns), 1)
    return (across == total).astype(F32).astype(BF16)


def conv_kernel(filters_ref, before_ref, mixed_ref, conv_ref, turned_ref):
    window = jnp.concatenate([before_ref[...], mixed_ref[...]], 0)
    n = 2 * TAPS
    rows = jnp.dot(filters_ref[...], antidiagonal(TAPS, n, TAPS), preferred_element_type=F32)
    conv_ref[...] = filtered(rows, window)
    turned_ref[...] = jnp.dot(antidiagonal(n, n, n - 1), window, preferred_element_type=F32).astype(BF16)


def mixed_grad_kernel(filters_ref, grad_ref, after_ref, key_ref, value_ref, key_grad_ref, value_grad_ref):
    window = jnp.concatenate([grad_ref[...], after_ref[...]], 0)
    taps = filters_ref[...].astype(F32)
    mixed_grad = filtered(jnp.concatenate([taps, jnp.zeros(taps.shape, F32)], 1), window)
    key_grad_ref[...] = (mixed_grad * value_ref[...].astype(F32)).astype(BF16)
    value_grad_ref[...] = (mixed_grad * key_ref[...].astype(F32)).astype(BF16)


def spread_kernel(cot_ref, out_ref):
    size = cot_ref.shape[1] // 8
    for x in range(4):
        for zh in range(2):
            out_ref[x, 0, :, zh * size : (zh + 1) * size] = cot_ref[:, (4 * zh + x) * size : (4 * zh + x + 1) * size]


def sum_kernel(parts_ref, out_ref):
    total = jnp.sum(parts_ref[...], axis=0)
    for i in range(out_ref.shape[0]):
        out_ref[i] = total


def branch_kernel(terms_ref, conv_ref, query_ref, turned_ref, query_grad_ref, conv_grad_ref, lag_ref):
    branch_grad = terms_ref[0].astype(F32)
    for x in range(1, terms_ref.shape[0]):
        branch_grad = branch_grad + terms_ref[x].astype(F32)
    query_grad_ref[...] = (branch_grad * conv_ref[...]).astype(BF16)
    conv_grad = (branch_grad * query_ref[...].astype(F32)).astype(BF16)
    conv_grad_ref[...] = conv_grad
    owner = lane_group((TAPS, LANES))
    wide = conv_grad.astype(F32)
    for g in range(PER):
        part = jnp.where(owner == g, wide, 0.0).astype(BF16)
        outer = lax.dot_general(part, turned_ref[...], (((1,), (1,)), ((), ())), preferred_element_type=F32)
        sums = skewed_sum(outer)[:, TAPS:]
        for copy in range(lag_ref.shape[0]):
            lag_ref[copy, g : g + 1, :] = sums


def product_kernel(place_ref, own_ref, low_ref, high_ref, *refs):
    count = (len(refs) - 3) // 2
    weights_hbm, out_ref, total_ref, weights, sems = refs[:count], refs[count], refs[count + 1], refs[count + 2 : -1], refs[-1]
    copies = [pltpu.make_async_copy(weights_hbm[i], weights[i], sems.at[i]) for i in range(count)]
    for copy in copies:
        copy.start()
    z, core, odd = place_ref[0], place_ref[1], place_ref[2]
    depth = weights[0].shape[0]
    below, above = [lax.rem(z + 8 - i, 8) for i in range(4)], [lax.rem(z + i, 8) for i in range(4)]
    mine = [jnp.where(core == 0, b, a) for b, a in zip(below, above)]
    theirs = [jnp.where(core == 0, a, b) for b, a in zip(below, above)]
    pieces = [(0, 0, z), (1, 0, mine[1]), (2, 0, theirs[1]), (3, 0, lax.rem(z + 4, 8))]
    pieces += [(4, 0, mine[2]), (4, depth, mine[3]), (5, 0, theirs[2]), (5, depth, theirs[3])]
    half = own_ref.shape[0] // 2
    parts = ((own_ref, 0), (own_ref, half), (low_ref, 0), (high_ref, 0))
    for n, (i, offset, place) in enumerate(pieces):
        if offset == 0:
            copies[i].wait()
        weight = weights[i][offset : offset + depth, :]
        columns = pl.ds(pl.multiple_of(place * depth, LANES), depth)
        for j, (cot_ref, first) in enumerate(parts):
            term = jnp.dot(cot_ref[first : first + half, columns], weight, preferred_element_type=F32)
            if n:
                term = total_ref[j] + term
            if n < len(pieces) - 1:
                total_ref[j] = term
                continue
            term = term.astype(BF16).reshape(2, 4, 16, term.shape[1])
            for x in range(2):
                for pair in range(4):
                    out_ref[2 * (j % 2) + x, pair, odd if j < 2 else 1 - odd] = term[x, pair]


def lane_blocks(*lead):
    return pl.BlockSpec(lead + (LANES,), lambda l: (0,) * len(lead) + (l,))


FILTER_BLOCK = pl.BlockSpec((PER, TAPS), lambda l: (l, 0))


def spread(cotangent):
    rows, width = cotangent.shape
    return pl.pallas_call(
        spread_kernel,
        grid=(4,),
        in_specs=[pl.BlockSpec((rows, width), lambda i: (0, 0))],
        out_specs=pl.BlockSpec((4, 1, rows, width // 4), lambda i: (0, i, 0, 0)),
        out_shape=jax.ShapeDtypeStruct((4, 4, rows, width // 4), cotangent.dtype),
        compiler_params=VMEM,
        name="spread",
    )(cotangent)


def summed_copies(parts):
    return pl.pallas_call(
        sum_kernel,
        out_shape=jax.ShapeDtypeStruct(parts.shape, parts.dtype),
        compiler_params=VMEM,
        name="sums",
    )(parts)


def convolve(filters, before, mixed):
    width = mixed.shape[1]
    tile = lane_blocks(TAPS)
    return pl.pallas_call(
        conv_kernel,
        grid=(width // LANES,),
        in_specs=[FILTER_BLOCK, tile, tile],
        out_specs=[tile, lane_blocks(2 * TAPS)],
        out_shape=[jax.ShapeDtypeStruct((TAPS, width), F32), jax.ShapeDtypeStruct((2 * TAPS, width), BF16)],
        compiler_params=VMEM,
        name="conv",
    )(filters, before, mixed)


def mixed_gradient(filters, grad, after, keys, values):
    width = grad.shape[1]
    tile = lane_blocks(TAPS)
    return pl.pallas_call(
        mixed_grad_kernel,
        grid=(width // LANES,),
        in_specs=[FILTER_BLOCK, tile, tile, tile, tile],
        out_specs=[tile, tile],
        out_shape=[jax.ShapeDtypeStruct((TAPS, width), BF16)] * 2,
        compiler_params=VMEM,
        name="mixed_grad",
    )(filters, grad, after, keys, values)


def branch_gradients(terms, conv, query, turned):
    width = query.shape[1]
    tile = lane_blocks(TAPS)
    return pl.pallas_call(
        branch_kernel,
        grid=(width // LANES,),
        in_specs=[lane_blocks(terms.shape[0], TAPS), tile, tile, lane_blocks(2 * TAPS)],
        out_specs=[tile, tile, pl.BlockSpec((8, PER, TAPS), lambda l: (0, l, 0))],
        out_shape=[jax.ShapeDtypeStruct((TAPS, width), BF16)] * 2
        + [jax.ShapeDtypeStruct((8, width // GROUP, TAPS), F32)],
        compiler_params=VMEM,
        name="branch",
    )(terms, conv, query, turned)


def partial_products(parts, weights):
    width = weights[0].shape[1]
    place = jnp.stack([lax.axis_index(Z), lax.axis_index("co"), lax.axis_index("yp")]).astype(jnp.int32)
    whole = pl.BlockSpec(memory_space=pltpu.VMEM)
    out = pl.pallas_call(
        product_kernel,
        in_specs=[pl.BlockSpec(memory_space=pltpu.SMEM)]
        + [whole] * 3
        + [pl.BlockSpec(memory_space=pltpu.HBM)] * len(weights),
        out_specs=whole,
        out_shape=jax.ShapeDtypeStruct((4, 4, 2, 16, width), BF16),
        scratch_shapes=[pltpu.VMEM((4, TAPS, width), F32)]
        + [pltpu.VMEM(a.shape, a.dtype) for a in weights]
        + [pltpu.SemaphoreType.DMA((len(weights),))],
        compiler_params=VMEM,
        name="product",
    )(place, *parts, *weights)
    return out.reshape(4, TAPS, width)


def exchange(copies, axes):
    return lax.all_to_all(copies, axes, split_axis=0, concat_axis=0)


def ahead(block, axes, distance):
    n = lax.axis_size(axes)
    return lax.ppermute(block, axes, [((i + distance) % n, i) for i in range(n)])


def along_z(block, steps):
    n = lax.axis_size(Z)
    route = [(2 * i, 2 * ((i + steps) % n)) for i in range(n)]
    route += [(2 * i + 1, 2 * ((i - steps) % n) + 1) for i in range(n)]
    return lax.ppermute(block, Z + ("co",), route)


def weight_blocks(chip):
    one, four = along_z(chip, 1), along_z(chip, 4)
    pair = along_z(jnp.concatenate([chip, one], 0), 2)
    return [chip, one, swap(one, "co"), four, pair, swap(pair, "co")]


def local(query_branch, key_branch, value_branch, cotangent, out_weight, filters):
    query, keys, values = query_branch[0], key_branch[0], value_branch[0]
    tokens, width = query.shape
    chip = in_order(out_weight, swap(out_weight, "co"), "co").reshape(2 * out_weight.shape[0], width)
    weights = weight_blocks(chip)

    copies = spread(cotangent[0])
    rows, columns = copies.shape[2:]
    own = exchange(copies.reshape(16, rows, columns), ("x", "yq"))
    own, weights[2], weights[3] = lax.optimization_barrier((own, weights[2], weights[3]))
    low, high = ahead(own[:8], Y, -1), ahead(own[8:], Y, 1)
    parts = [part.reshape(-1, columns) for part in (own, low, high)]

    keys, values, own = lax.optimization_barrier((keys, values, own))
    mixed = (keys.astype(F32) * values.astype(F32)).astype(BF16)
    parts, before = lax.optimization_barrier((parts, from_behind(mixed, 1)))
    terms = exchange(partial_products(parts, weights), "x")
    conv, turned = convolve(filters, before, mixed)
    query_grad, conv_grad, lags = branch_gradients(terms, conv, query, turned)
    lags = summed_copies(exchange(lags, ("x", "co")))
    after = from_behind(conv_grad, -1)
    lags, after = lax.optimization_barrier((lags, after))
    scale = 1.0 / math.sqrt(2 * lax.axis_size(CONTEXT) * tokens * GROUP)
    filter_grad = jnp.sum(exchange(lags, Z), axis=0) * scale
    key_grad, value_grad = mixed_gradient(filters, conv_grad, after, keys, values)
    return (query_grad[None], key_grad[None], value_grad[None], filter_grad)


def solution(mesh):
    fine = Mesh(mesh.devices.reshape(2, 4, 4, 2, 4, 2), ("zh", "x", "zl", "co", "yq", "yp"))
    branch = P("zh", CONTEXT, Y)
    return jax.shard_map(
        local,
        mesh=fine,
        in_specs=(
            branch,
            branch,
            branch,
            P("zh", CONTEXT + Y, None),
            P(("zh",) + CONTEXT, Y),
            P(Y, None),
        ),
        out_specs=(branch, branch, branch, P(Y, None)),
        check_vma=False,
    )
```

```python
import math

import jax
import jax.numpy as jnp
from jax import lax
from jax.experimental import pallas as pl
from jax.experimental.pallas import tpu as pltpu
from jax.sharding import Mesh, PartitionSpec as P

GROUP = 16
TAPS = 128
LANES = 128
PER = LANES // GROUP
F32 = jnp.float32
BF16 = jnp.bfloat16

Z = ("zh", "zl")
CONTEXT = ("x", "zl", "co")
Y = ("yq", "yp")
VMEM = pltpu.CompilerParams(vmem_limit_bytes=8 * 1024 * 1024)


def swap(block, axis):
    return lax.ppermute(block, axis, [(0, 1), (1, 0)])


def in_order(mine, theirs, axis):
    first = lax.axis_index(axis) == 0
    return jnp.stack([jnp.where(first, mine, theirs), jnp.where(first, theirs, mine)])


def from_behind(block, distance):
    n = lax.axis_size(CONTEXT)
    route = [(i - distance, i) for i in range(n) if 0 <= i - distance < n]
    return lax.ppermute(block, CONTEXT, route)


def shifted_rows(row):
    return pltpu.roll(jnp.broadcast_to(row, (TAPS, 2 * TAPS)), 0, 1, stride=1, stride_axis=0)


def skewed_sum(rows):
    return jnp.sum(pltpu.roll(rows, 1, 1, stride=1, stride_axis=0), axis=0, keepdims=True)


def lane_group(shape):
    return lax.broadcasted_iota(jnp.int32, shape, 1) >> 4


def filtered(rows, window):
    owner = lane_group((TAPS, LANES))
    total = jnp.zeros((TAPS, LANES), F32)
    for g in range(PER):
        table = shifted_rows(rows[g : g + 1, :]).astype(BF16)
        term = jnp.dot(table, window, preferred_element_type=F32)
        total = jnp.where(owner == g, term, total)
    return total


def antidiagonal(rows, columns, total):
    across = lax.broadcasted_iota(jnp.int32, (rows, columns), 0) + lax.broadcasted_iota(jnp.int32, (rows, columns), 1)
    return (across == total).astype(F32).astype(BF16)


def conv_kernel(filters_ref, before_ref, mixed_ref, conv_ref, turned_ref):
    window = jnp.concatenate([before_ref[...], mixed_ref[...]], 0)
    n = 2 * TAPS
    rows = jnp.dot(filters_ref[...], antidiagonal(TAPS, n, TAPS), preferred_element_type=F32)
    conv_ref[...] = filtered(rows, window)
    turned_ref[...] = jnp.dot(antidiagonal(n, n, n - 1), window, preferred_element_type=F32).astype(BF16)


def mixed_grad_kernel(filters_ref, grad_ref, after_ref, key_ref, value_ref, key_grad_ref, value_grad_ref):
    window = jnp.concatenate([grad_ref[...], after_ref[...]], 0)
    taps = filters_ref[...].astype(F32)
    mixed_grad = filtered(jnp.concatenate([taps, jnp.zeros(taps.shape, F32)], 1), window)
    key_grad_ref[...] = (mixed_grad * value_ref[...].astype(F32)).astype(BF16)
    value_grad_ref[...] = (mixed_grad * key_ref[...].astype(F32)).astype(BF16)


def spread_kernel(cot_ref, out_ref):
    size = cot_ref.shape[1] // 8
    for x in range(4):
        for zh in range(2):
            out_ref[x, 0, :, zh * size : (zh + 1) * size] = cot_ref[:, (4 * zh + x) * size : (4 * zh + x + 1) * size]


def sum_kernel(parts_ref, out_ref):
    total = jnp.sum(parts_ref[...], axis=0)
    for i in range(out_ref.shape[0]):
        out_ref[i] = total


def branch_kernel(terms_ref, conv_ref, query_ref, turned_ref, query_grad_ref, conv_grad_ref, lag_ref):
    branch_grad = terms_ref[0].astype(F32)
    for x in range(1, terms_ref.shape[0]):
        branch_grad = branch_grad + terms_ref[x].astype(F32)
    query_grad_ref[...] = (branch_grad * conv_ref[...]).astype(BF16)
    conv_grad = (branch_grad * query_ref[...].astype(F32)).astype(BF16)
    conv_grad_ref[...] = conv_grad
    owner = lane_group((TAPS, LANES))
    wide = conv_grad.astype(F32)
    for g in range(PER):
        part = jnp.where(owner == g, wide, 0.0).astype(BF16)
        outer = lax.dot_general(part, turned_ref[...], (((1,), (1,)), ((), ())), preferred_element_type=F32)
        sums = skewed_sum(outer)[:, TAPS:]
        for copy in range(lag_ref.shape[0]):
            lag_ref[copy, g : g + 1, :] = sums


def product_kernel(place_ref, own_ref, *refs):
    count = (len(refs) - 3) // 2
    fetched, out_ref, total_ref, here, sems = refs[:count], refs[count], refs[count + 1], refs[count + 2 : -1], refs[-1]
    copies = [pltpu.make_async_copy(fetched[i], here[i], sems.at[i]) for i in range(count)]
    for copy in copies:
        copy.start()
    weights, (low_ref, high_ref) = here[:-2], here[-2:]
    z, core, odd = place_ref[0], place_ref[1], place_ref[2]
    depth = weights[0].shape[0]
    below, above = [lax.rem(z + 8 - i, 8) for i in range(4)], [lax.rem(z + i, 8) for i in range(4)]
    mine = [jnp.where(core == 0, b, a) for b, a in zip(below, above)]
    theirs = [jnp.where(core == 0, a, b) for b, a in zip(below, above)]
    pieces = [(0, 0, z), (1, 0, mine[1]), (2, 0, theirs[1]), (3, 0, lax.rem(z + 4, 8))]
    pieces += [(4, 0, mine[2]), (4, depth, mine[3]), (5, 0, theirs[2]), (5, depth, theirs[3])]
    half = own_ref.shape[0] // 2
    for j, (cot_ref, first) in enumerate(((own_ref, 0), (own_ref, half), (low_ref, 0), (high_ref, 0))):
        if j >= 2:
            copies[count - 4 + j].wait()
        for n, (i, offset, place) in enumerate(pieces):
            if j == 0 and offset == 0:
                copies[i].wait()
            weight = weights[i][offset : offset + depth, :]
            columns = pl.ds(pl.multiple_of(place * depth, LANES), depth)
            term = jnp.dot(cot_ref[first : first + half, columns], weight, preferred_element_type=F32)
            if n:
                term = total_ref[j] + term
            if n < len(pieces) - 1:
                total_ref[j] = term
                continue
            term = term.astype(BF16).reshape(2, 4, 16, term.shape[1])
            for x in range(2):
                for pair in range(4):
                    out_ref[2 * (j % 2) + x, pair, odd if j < 2 else 1 - odd] = term[x, pair]


def lane_blocks(*lead):
    return pl.BlockSpec(lead + (LANES,), lambda l: (0,) * len(lead) + (l,))


FILTER_BLOCK = pl.BlockSpec((PER, TAPS), lambda l: (l, 0))


def spread(cotangent):
    rows, width = cotangent.shape
    return pl.pallas_call(
        spread_kernel,
        grid=(4,),
        in_specs=[pl.BlockSpec((rows, width), lambda i: (0, 0))],
        out_specs=pl.BlockSpec((4, 1, rows, width // 4), lambda i: (0, i, 0, 0)),
        out_shape=jax.ShapeDtypeStruct((4, 4, rows, width // 4), cotangent.dtype),
        compiler_params=VMEM,
        name="spread",
    )(cotangent)


def summed_copies(parts):
    return pl.pallas_call(
        sum_kernel,
        out_shape=jax.ShapeDtypeStruct(parts.shape, parts.dtype),
        compiler_params=VMEM,
        name="sums",
    )(parts)


def convolve(filters, before, mixed):
    width = mixed.shape[1]
    tile = lane_blocks(TAPS)
    return pl.pallas_call(
        conv_kernel,
        grid=(width // LANES,),
        in_specs=[FILTER_BLOCK, tile, tile],
        out_specs=[tile, lane_blocks(2 * TAPS)],
        out_shape=[jax.ShapeDtypeStruct((TAPS, width), F32), jax.ShapeDtypeStruct((2 * TAPS, width), BF16)],
        compiler_params=VMEM,
        name="conv",
    )(filters, before, mixed)


def mixed_gradient(filters, grad, after, keys, values):
    width = grad.shape[1]
    tile = lane_blocks(TAPS)
    return pl.pallas_call(
        mixed_grad_kernel,
        grid=(width // LANES,),
        in_specs=[FILTER_BLOCK, tile, tile, tile, tile],
        out_specs=[tile, tile],
        out_shape=[jax.ShapeDtypeStruct((TAPS, width), BF16)] * 2,
        compiler_params=VMEM,
        name="mixed_grad",
    )(filters, grad, after, keys, values)


def branch_gradients(terms, conv, query, turned):
    width = query.shape[1]
    tile = lane_blocks(TAPS)
    return pl.pallas_call(
        branch_kernel,
        grid=(width // LANES,),
        in_specs=[lane_blocks(terms.shape[0], TAPS), tile, tile, lane_blocks(2 * TAPS)],
        out_specs=[tile, tile, pl.BlockSpec((8, PER, TAPS), lambda l: (0, l, 0))],
        out_shape=[jax.ShapeDtypeStruct((TAPS, width), BF16)] * 2
        + [jax.ShapeDtypeStruct((8, width // GROUP, TAPS), F32)],
        compiler_params=VMEM,
        name="branch",
    )(terms, conv, query, turned)


def partial_products(parts, weights):
    width = weights[0].shape[1]
    place = jnp.stack([lax.axis_index(Z), lax.axis_index("co"), lax.axis_index("yp")]).astype(jnp.int32)
    whole = pl.BlockSpec(memory_space=pltpu.VMEM)
    out = pl.pallas_call(
        product_kernel,
        in_specs=[pl.BlockSpec(memory_space=pltpu.SMEM)]
        + [whole]
        + [pl.BlockSpec(memory_space=pltpu.HBM)] * (len(weights) + 2),
        out_specs=whole,
        out_shape=jax.ShapeDtypeStruct((4, 4, 2, 16, width), BF16),
        scratch_shapes=[pltpu.VMEM((4, TAPS, width), F32)]
        + [pltpu.VMEM(a.shape, a.dtype) for a in (*weights, *parts[1:])]
        + [pltpu.SemaphoreType.DMA((len(weights) + 2,))],
        compiler_params=VMEM,
        name="product",
    )(place, parts[0], *weights, *parts[1:])
    return out.reshape(4, TAPS, width)


def exchange(copies, axes):
    return lax.all_to_all(copies, axes, split_axis=0, concat_axis=0)


def ahead(block, axes, distance):
    n = lax.axis_size(axes)
    return lax.ppermute(block, axes, [((i + distance) % n, i) for i in range(n)])


def along_z(block, steps):
    n = lax.axis_size(Z)
    route = [(2 * i, 2 * ((i + steps) % n)) for i in range(n)]
    route += [(2 * i + 1, 2 * ((i - steps) % n) + 1) for i in range(n)]
    return lax.ppermute(block, Z + ("co",), route)


def weight_blocks(chip, beside):
    one, four = along_z(chip, 1), along_z(chip, 4)
    one, beside = lax.optimization_barrier((one, beside))
    pair = along_z(jnp.concatenate([chip, one], 0), 2)
    return beside, [chip, one, swap(one, "co"), four, pair, swap(pair, "co")]


def local(query_branch, key_branch, value_branch, cotangent, out_weight, filters):
    query, keys, values = query_branch[0], key_branch[0], value_branch[0]
    tokens, width = query.shape
    chip = in_order(out_weight, swap(out_weight, "co"), "co").reshape(2 * out_weight.shape[0], width)
    keys, values, chip = lax.optimization_barrier((keys, values, chip))
    mixed = (keys.astype(F32) * values.astype(F32)).astype(BF16)
    before, weights = weight_blocks(chip, from_behind(mixed, 1))

    copies = spread(cotangent[0])
    rows, columns = copies.shape[2:]
    own = exchange(copies.reshape(16, rows, columns), ("x", "yq"))
    own, weights[2], weights[3] = lax.optimization_barrier((own, weights[2], weights[3]))
    low, high = ahead(own[:8], Y, -1), ahead(own[8:], Y, 1)
    parts = [part.reshape(-1, columns) for part in (own, low, high)]

    terms = exchange(partial_products(parts, weights), "x")
    conv, turned = convolve(filters, before, mixed)
    query_grad, conv_grad, lags = branch_gradients(terms, conv, query, turned)
    lags = summed_copies(exchange(lags, ("x", "co")))
    after = from_behind(conv_grad, -1)
    lags, after = lax.optimization_barrier((lags, after))
    scale = 1.0 / math.sqrt(2 * lax.axis_size(CONTEXT) * tokens * GROUP)
    filter_grad = jnp.sum(exchange(lags, Z), axis=0) * scale
    key_grad, value_grad = mixed_gradient(filters, conv_grad, after, keys, values)
    return (query_grad[None], key_grad[None], value_grad[None], filter_grad)


def solution(mesh):
    fine = Mesh(mesh.devices.reshape(2, 4, 4, 2, 4, 2), ("zh", "x", "zl", "co", "yq", "yp"))
    branch = P("zh", CONTEXT, Y)
    return jax.shard_map(
        local,
        mesh=fine,
        in_specs=(
            branch,
            branch,
            branch,
            P("zh", CONTEXT + Y, None),
            P(("zh",) + CONTEXT, Y),
            P(Y, None),
        ),
        out_specs=(branch, branch, branch, P(Y, None)),
        check_vma=False,
    )
```

```python
import math

import jax
import jax.numpy as jnp
from jax import lax
from jax.experimental import pallas as pl
from jax.experimental.pallas import tpu as pltpu
from jax.sharding import Mesh, PartitionSpec as P

GROUP = 16
TAPS = 128
LANES = 128
PER = LANES // GROUP
F32 = jnp.float32
BF16 = jnp.bfloat16

Z = ("zh", "zl")
CONTEXT = ("x", "zl", "co")
Y = ("yq", "yp")
VMEM = pltpu.CompilerParams(vmem_limit_bytes=8 * 1024 * 1024)


def swap(block, axis):
    return lax.ppermute(block, axis, [(0, 1), (1, 0)])


def in_order(mine, theirs, axis):
    first = lax.axis_index(axis) == 0
    return jnp.stack([jnp.where(first, mine, theirs), jnp.where(first, theirs, mine)])


def from_behind(block, distance):
    n = lax.axis_size(CONTEXT)
    route = [(i - distance, i) for i in range(n) if 0 <= i - distance < n]
    return lax.ppermute(block, CONTEXT, route)


def shifted_rows(row):
    return pltpu.roll(jnp.broadcast_to(row, (TAPS, 2 * TAPS)), 0, 1, stride=1, stride_axis=0)


def skewed_sum(rows):
    return jnp.sum(pltpu.roll(rows, 1, 1, stride=1, stride_axis=0), axis=0, keepdims=True)


def lane_group(shape):
    return lax.broadcasted_iota(jnp.int32, shape, 1) >> 4


def filtered(rows, window):
    owner = lane_group((TAPS, LANES))
    total = jnp.zeros((TAPS, LANES), F32)
    for g in range(PER):
        table = shifted_rows(rows[g : g + 1, :]).astype(BF16)
        term = jnp.dot(table, window, preferred_element_type=F32)
        total = jnp.where(owner == g, term, total)
    return total


def antidiagonal(rows, columns, total):
    across = lax.broadcasted_iota(jnp.int32, (rows, columns), 0) + lax.broadcasted_iota(jnp.int32, (rows, columns), 1)
    return (across == total).astype(F32).astype(BF16)


def conv_kernel(filters_ref, before_ref, mixed_ref, conv_ref, turned_ref):
    window = jnp.concatenate([before_ref[...], mixed_ref[...]], 0)
    n = 2 * TAPS
    rows = jnp.dot(filters_ref[...], antidiagonal(TAPS, n, TAPS), preferred_element_type=F32)
    conv_ref[...] = filtered(rows, window)
    turned_ref[...] = jnp.dot(antidiagonal(n, n, n - 1), window, preferred_element_type=F32).astype(BF16)


def mixed_grad_kernel(filters_ref, grad_ref, after_ref, key_ref, value_ref, key_grad_ref, value_grad_ref):
    window = jnp.concatenate([grad_ref[...], after_ref[...]], 0)
    taps = filters_ref[...].astype(F32)
    mixed_grad = filtered(jnp.concatenate([taps, jnp.zeros(taps.shape, F32)], 1), window)
    key_grad_ref[...] = (mixed_grad * value_ref[...].astype(F32)).astype(BF16)
    value_grad_ref[...] = (mixed_grad * key_ref[...].astype(F32)).astype(BF16)


def spread_kernel(cot_ref, out_ref):
    size = cot_ref.shape[1] // 8
    for x in range(4):
        for zh in range(2):
            out_ref[x, 0, :, zh * size : (zh + 1) * size] = cot_ref[:, (4 * zh + x) * size : (4 * zh + x + 1) * size]


def sum_kernel(parts_ref, out_ref):
    total = jnp.sum(parts_ref[...], axis=0)
    for i in range(out_ref.shape[0]):
        out_ref[i] = total


def branch_kernel(terms_ref, conv_ref, query_ref, turned_ref, query_grad_ref, conv_grad_ref, lag_ref):
    branch_grad = terms_ref[0].astype(F32)
    for x in range(1, terms_ref.shape[0]):
        branch_grad = branch_grad + terms_ref[x].astype(F32)
    query_grad_ref[...] = (branch_grad * conv_ref[...]).astype(BF16)
    conv_grad = (branch_grad * query_ref[...].astype(F32)).astype(BF16)
    conv_grad_ref[...] = conv_grad
    owner = lane_group((TAPS, LANES))
    wide = conv_grad.astype(F32)
    for g in range(PER):
        part = jnp.where(owner == g, wide, 0.0).astype(BF16)
        outer = lax.dot_general(part, turned_ref[...], (((1,), (1,)), ((), ())), preferred_element_type=F32)
        sums = skewed_sum(outer)[:, TAPS:]
        for copy in range(lag_ref.shape[0]):
            lag_ref[copy, g : g + 1, :] = sums


def product_kernel(place_ref, own_ref, low_ref, high_ref, *refs):
    count = (len(refs) - 3) // 2
    weights_hbm, out_ref, total_ref, weights, sems = refs[:count], refs[count], refs[count + 1], refs[count + 2 : -1], refs[-1]
    copies = [pltpu.make_async_copy(weights_hbm[i], weights[i], sems.at[i]) for i in range(count)]
    for copy in copies:
        copy.start()
    z, core, odd = place_ref[0], place_ref[1], place_ref[2]
    depth = weights[0].shape[0]
    below, above = [lax.rem(z + 8 - i, 8) for i in range(4)], [lax.rem(z + i, 8) for i in range(4)]
    mine = [jnp.where(core == 0, b, a) for b, a in zip(below, above)]
    theirs = [jnp.where(core == 0, a, b) for b, a in zip(below, above)]
    pieces = [(0, 0, z), (1, 0, mine[1]), (2, 0, theirs[1]), (3, 0, lax.rem(z + 4, 8))]
    pieces += [(4, 0, mine[2]), (4, depth, mine[3]), (5, 0, theirs[2]), (5, depth, theirs[3])]
    half = own_ref.shape[0] // 2
    parts = ((own_ref, 0), (own_ref, half), (low_ref, 0), (high_ref, 0))
    for n, (i, offset, place) in enumerate(pieces):
        if offset == 0:
            copies[i].wait()
        weight = weights[i][offset : offset + depth, :]
        columns = pl.ds(pl.multiple_of(place * depth, LANES), depth)
        for j, (cot_ref, first) in enumerate(parts):
            term = jnp.dot(cot_ref[first : first + half, columns], weight, preferred_element_type=F32)
            if n:
                term = total_ref[j] + term
            if n < len(pieces) - 1:
                total_ref[j] = term
                continue
            term = term.astype(BF16).reshape(2, 4, 16, term.shape[1])
            for x in range(2):
                for pair in range(4):
                    out_ref[2 * (j % 2) + x, pair, odd if j < 2 else 1 - odd] = term[x, pair]


def lane_blocks(*lead):
    return pl.BlockSpec(lead + (LANES,), lambda l: (0,) * len(lead) + (l,))


FILTER_BLOCK = pl.BlockSpec((PER, TAPS), lambda l: (l, 0))


def spread(cotangent):
    rows, width = cotangent.shape
    return pl.pallas_call(
        spread_kernel,
        grid=(4,),
        in_specs=[pl.BlockSpec((rows, width), lambda i: (0, 0))],
        out_specs=pl.BlockSpec((4, 1, rows, width // 4), lambda i: (0, i, 0, 0)),
        out_shape=jax.ShapeDtypeStruct((4, 4, rows, width // 4), cotangent.dtype),
        compiler_params=VMEM,
        name="spread",
    )(cotangent)


def summed_copies(parts):
    return pl.pallas_call(
        sum_kernel,
        out_shape=jax.ShapeDtypeStruct(parts.shape, parts.dtype),
        compiler_params=VMEM,
        name="sums",
    )(parts)


def convolve(filters, before, mixed):
    width = mixed.shape[1]
    tile = lane_blocks(TAPS)
    return pl.pallas_call(
        conv_kernel,
        grid=(width // LANES,),
        in_specs=[FILTER_BLOCK, tile, tile],
        out_specs=[tile, lane_blocks(2 * TAPS)],
        out_shape=[jax.ShapeDtypeStruct((TAPS, width), F32), jax.ShapeDtypeStruct((2 * TAPS, width), BF16)],
        compiler_params=VMEM,
        name="conv",
    )(filters, before, mixed)


def mixed_gradient(filters, grad, after, keys, values):
    width = grad.shape[1]
    tile = lane_blocks(TAPS)
    return pl.pallas_call(
        mixed_grad_kernel,
        grid=(width // LANES,),
        in_specs=[FILTER_BLOCK, tile, tile, tile, tile],
        out_specs=[tile, tile],
        out_shape=[jax.ShapeDtypeStruct((TAPS, width), BF16)] * 2,
        compiler_params=VMEM,
        name="mixed_grad",
    )(filters, grad, after, keys, values)


def branch_gradients(terms, conv, query, turned):
    width = query.shape[1]
    tile = lane_blocks(TAPS)
    return pl.pallas_call(
        branch_kernel,
        grid=(width // LANES,),
        in_specs=[lane_blocks(terms.shape[0], TAPS), tile, tile, lane_blocks(2 * TAPS)],
        out_specs=[tile, tile, pl.BlockSpec((8, PER, TAPS), lambda l: (0, l, 0))],
        out_shape=[jax.ShapeDtypeStruct((TAPS, width), BF16)] * 2
        + [jax.ShapeDtypeStruct((8, width // GROUP, TAPS), F32)],
        compiler_params=VMEM,
        name="branch",
    )(terms, conv, query, turned)


def partial_products(parts, weights):
    width = weights[0].shape[1]
    place = jnp.stack([lax.axis_index(Z), lax.axis_index("co"), lax.axis_index("yp")]).astype(jnp.int32)
    whole = pl.BlockSpec(memory_space=pltpu.VMEM)
    out = pl.pallas_call(
        product_kernel,
        in_specs=[pl.BlockSpec(memory_space=pltpu.SMEM)]
        + [whole] * 3
        + [pl.BlockSpec(memory_space=pltpu.HBM)] * len(weights),
        out_specs=whole,
        out_shape=jax.ShapeDtypeStruct((4, 4, 2, 16, width), BF16),
        scratch_shapes=[pltpu.VMEM((4, TAPS, width), F32)]
        + [pltpu.VMEM(a.shape, a.dtype) for a in weights]
        + [pltpu.SemaphoreType.DMA((len(weights),))],
        compiler_params=VMEM,
        name="product",
    )(place, *parts, *weights)
    return out.reshape(4, TAPS, width)


def exchange(copies, axes):
    return lax.all_to_all(copies, axes, split_axis=0, concat_axis=0)


def ahead(block, axes, distance):
    n = lax.axis_size(axes)
    return lax.ppermute(block, axes, [((i + distance) % n, i) for i in range(n)])


def along_z(block, steps):
    n = lax.axis_size(Z)
    route = [(2 * i, 2 * ((i + steps) % n)) for i in range(n)]
    route += [(2 * i + 1, 2 * ((i - steps) % n) + 1) for i in range(n)]
    return lax.ppermute(block, Z + ("co",), route)


def weight_blocks(chip):
    one, four = along_z(chip, 1), along_z(chip, 4)
    pair = along_z(jnp.concatenate([chip, one], 0), 2)
    return [chip, one, swap(one, "co"), four, pair, swap(pair, "co")]


def local(query_branch, key_branch, value_branch, cotangent, out_weight, filters):
    query, keys, values = query_branch[0], key_branch[0], value_branch[0]
    tokens, width = query.shape
    chip = in_order(out_weight, swap(out_weight, "co"), "co").reshape(2 * out_weight.shape[0], width)
    weights = weight_blocks(chip)

    copies = spread(cotangent[0])
    rows, columns = copies.shape[2:]
    own = exchange(copies.reshape(16, rows, columns), ("x", "yq"))
    own, weights[2], weights[3] = lax.optimization_barrier((own, weights[2], weights[3]))
    low, high = ahead(own[:8], Y, -1), ahead(own[8:], Y, 1)
    parts = [part.reshape(-1, columns) for part in (own, low, high)]

    partial = partial_products(parts, weights)
    terms = exchange(partial, "x")
    keys, values, partial = lax.optimization_barrier((keys, values, partial))
    mixed = (keys.astype(F32) * values.astype(F32)).astype(BF16)
    conv, turned = convolve(filters, from_behind(mixed, 1), mixed)
    query_grad, conv_grad, lags = branch_gradients(terms, conv, query, turned)
    lags = summed_copies(exchange(lags, ("x", "co")))
    after = from_behind(conv_grad, -1)
    lags, after = lax.optimization_barrier((lags, after))
    scale = 1.0 / math.sqrt(2 * lax.axis_size(CONTEXT) * tokens * GROUP)
    filter_grad = jnp.sum(exchange(lags, Z), axis=0) * scale
    key_grad, value_grad = mixed_gradient(filters, conv_grad, after, keys, values)
    return (query_grad[None], key_grad[None], value_grad[None], filter_grad)


def solution(mesh):
    fine = Mesh(mesh.devices.reshape(2, 4, 4, 2, 4, 2), ("zh", "x", "zl", "co", "yq", "yp"))
    branch = P("zh", CONTEXT, Y)
    return jax.shard_map(
        local,
        mesh=fine,
        in_specs=(
            branch,
            branch,
            branch,
            P("zh", CONTEXT + Y, None),
            P(("zh",) + CONTEXT, Y),
            P(Y, None),
        ),
        out_specs=(branch, branch, branch, P(Y, None)),
        check_vma=False,
    )
```

```python
import math

import jax
import jax.numpy as jnp
from jax import lax
from jax.experimental import pallas as pl
from jax.experimental.pallas import tpu as pltpu
from jax.sharding import Mesh, PartitionSpec as P

GROUP = 16
TAPS = 128
LANES = 128
PER = LANES // GROUP
F32 = jnp.float32
BF16 = jnp.bfloat16

Z = ("zh", "zl")
CONTEXT = ("x", "zl", "co")
Y = ("yq", "yp")
VMEM = pltpu.CompilerParams(vmem_limit_bytes=8 * 1024 * 1024)


def swap(block, axis):
    return lax.ppermute(block, axis, [(0, 1), (1, 0)])


def in_order(mine, theirs, axis):
    first = lax.axis_index(axis) == 0
    return jnp.stack([jnp.where(first, mine, theirs), jnp.where(first, theirs, mine)])


def from_behind(block, distance):
    n = lax.axis_size(CONTEXT)
    route = [(i - distance, i) for i in range(n) if 0 <= i - distance < n]
    return lax.ppermute(block, CONTEXT, route)


def shifted_rows(row):
    return pltpu.roll(jnp.broadcast_to(row, (TAPS, 2 * TAPS)), 0, 1, stride=1, stride_axis=0)


def skewed_sum(rows):
    return jnp.sum(pltpu.roll(rows, 1, 1, stride=1, stride_axis=0), axis=0, keepdims=True)


def lane_group(shape):
    return lax.broadcasted_iota(jnp.int32, shape, 1) >> 4


def filtered(rows, window):
    owner = lane_group((TAPS, LANES))
    total = jnp.zeros((TAPS, LANES), F32)
    for g in range(PER):
        table = shifted_rows(rows[g : g + 1, :]).astype(BF16)
        term = jnp.dot(table, window, preferred_element_type=F32)
        total = jnp.where(owner == g, term, total)
    return total


def antidiagonal(rows, columns, total):
    across = lax.broadcasted_iota(jnp.int32, (rows, columns), 0) + lax.broadcasted_iota(jnp.int32, (rows, columns), 1)
    return (across == total).astype(F32).astype(BF16)


def conv_kernel(filters_ref, before_ref, mixed_ref, conv_ref, turned_ref):
    window = jnp.concatenate([before_ref[...], mixed_ref[...]], 0)
    n = 2 * TAPS
    rows = jnp.dot(filters_ref[...], antidiagonal(TAPS, n, TAPS), preferred_element_type=F32)
    conv_ref[...] = filtered(rows, window)
    turned_ref[...] = jnp.dot(antidiagonal(n, n, n - 1), window, preferred_element_type=F32).astype(BF16)


def mixed_grad_kernel(filters_ref, grad_ref, after_ref, key_ref, value_ref, key_grad_ref, value_grad_ref):
    window = jnp.concatenate([grad_ref[...], after_ref[...]], 0)
    taps = filters_ref[...].astype(F32)
    mixed_grad = filtered(jnp.concatenate([taps, jnp.zeros(taps.shape, F32)], 1), window)
    key_grad_ref[...] = (mixed_grad * value_ref[...].astype(F32)).astype(BF16)
    value_grad_ref[...] = (mixed_grad * key_ref[...].astype(F32)).astype(BF16)


def spread_kernel(cot_ref, out_ref):
    size = cot_ref.shape[1] // 8
    for x in range(4):
        for zh in range(2):
            out_ref[x, 0, :, zh * size : (zh + 1) * size] = cot_ref[:, (4 * zh + x) * size : (4 * zh + x + 1) * size]


def sum_kernel(parts_ref, out_ref):
    total = jnp.sum(parts_ref[...], axis=0)
    for i in range(out_ref.shape[0]):
        out_ref[i] = total


def branch_kernel(terms_ref, conv_ref, query_ref, turned_ref, query_grad_ref, conv_grad_ref, lag_ref):
    branch_grad = terms_ref[0].astype(F32)
    for x in range(1, terms_ref.shape[0]):
        branch_grad = branch_grad + terms_ref[x].astype(F32)
    query_grad_ref[...] = (branch_grad * conv_ref[...]).astype(BF16)
    conv_grad = (branch_grad * query_ref[...].astype(F32)).astype(BF16)
    conv_grad_ref[...] = conv_grad
    owner = lane_group((TAPS, LANES))
    wide = conv_grad.astype(F32)
    for g in range(PER):
        part = jnp.where(owner == g, wide, 0.0).astype(BF16)
        outer = lax.dot_general(part, turned_ref[...], (((1,), (1,)), ((), ())), preferred_element_type=F32)
        sums = skewed_sum(outer)[:, TAPS:]
        for copy in range(lag_ref.shape[0]):
            lag_ref[copy, g : g + 1, :] = sums


def product_kernel(place_ref, own_ref, low_ref, high_ref, *refs):
    count = (len(refs) - 3) // 2
    weights_hbm, out_ref, total_ref, weights, sems = refs[:count], refs[count], refs[count + 1], refs[count + 2 : -1], refs[-1]
    copies = [pltpu.make_async_copy(weights_hbm[i], weights[i], sems.at[i]) for i in range(count)]
    for copy in copies:
        copy.start()
    z, core, odd = place_ref[0], place_ref[1], place_ref[2]
    depth = weights[0].shape[0]
    below, above = [lax.rem(z + 8 - i, 8) for i in range(4)], [lax.rem(z + i, 8) for i in range(4)]
    mine = [jnp.where(core == 0, b, a) for b, a in zip(below, above)]
    theirs = [jnp.where(core == 0, a, b) for b, a in zip(below, above)]
    pieces = [(0, 0, z), (1, 0, mine[1]), (2, 0, theirs[1]), (3, 0, lax.rem(z + 4, 8))]
    pieces += [(4, 0, mine[2]), (4, depth, mine[3]), (5, 0, theirs[2]), (5, depth, theirs[3])]
    half = own_ref.shape[0] // 2
    parts = ((own_ref, 0), (own_ref, half), (low_ref, 0), (high_ref, 0))
    for n, (i, offset, place) in enumerate(pieces):
        if offset == 0:
            copies[i].wait()
        weight = weights[i][offset : offset + depth, :]
        columns = pl.ds(pl.multiple_of(place * depth, LANES), depth)
        for j, (cot_ref, first) in enumerate(parts):
            term = jnp.dot(cot_ref[first : first + half, columns], weight, preferred_element_type=F32)
            if n:
                term = total_ref[j] + term
            if n < len(pieces) - 1:
                total_ref[j] = term
                continue
            term = term.astype(BF16).reshape(2, 4, 16, term.shape[1])
            for x in range(2):
                for pair in range(4):
                    out_ref[2 * (j % 2) + x, pair, odd if j < 2 else 1 - odd] = term[x, pair]


def lane_blocks(*lead):
    return pl.BlockSpec(lead + (LANES,), lambda l: (0,) * len(lead) + (l,))


FILTER_BLOCK = pl.BlockSpec((PER, TAPS), lambda l: (l, 0))


def spread(cotangent):
    rows, width = cotangent.shape
    return pl.pallas_call(
        spread_kernel,
        grid=(4,),
        in_specs=[pl.BlockSpec((rows, width), lambda i: (0, 0))],
        out_specs=pl.BlockSpec((4, 1, rows, width // 4), lambda i: (0, i, 0, 0)),
        out_shape=jax.ShapeDtypeStruct((4, 4, rows, width // 4), cotangent.dtype),
        compiler_params=VMEM,
        name="spread",
    )(cotangent)


def summed_copies(parts):
    return pl.pallas_call(
        sum_kernel,
        out_shape=jax.ShapeDtypeStruct(parts.shape, parts.dtype),
        compiler_params=VMEM,
        name="sums",
    )(parts)


def convolve(filters, before, mixed):
    width = mixed.shape[1]
    tile = lane_blocks(TAPS)
    return pl.pallas_call(
        conv_kernel,
        grid=(width // LANES,),
        in_specs=[FILTER_BLOCK, tile, tile],
        out_specs=[tile, lane_blocks(2 * TAPS)],
        out_shape=[jax.ShapeDtypeStruct((TAPS, width), F32), jax.ShapeDtypeStruct((2 * TAPS, width), BF16)],
        compiler_params=VMEM,
        name="conv",
    )(filters, before, mixed)


def mixed_gradient(filters, grad, after, keys, values):
    width = grad.shape[1]
    tile = lane_blocks(TAPS)
    return pl.pallas_call(
        mixed_grad_kernel,
        grid=(width // LANES,),
        in_specs=[FILTER_BLOCK, tile, tile, tile, tile],
        out_specs=[tile, tile],
        out_shape=[jax.ShapeDtypeStruct((TAPS, width), BF16)] * 2,
        compiler_params=VMEM,
        name="mixed_grad",
    )(filters, grad, after, keys, values)


def branch_gradients(terms, conv, query, turned):
    width = query.shape[1]
    tile = lane_blocks(TAPS)
    return pl.pallas_call(
        branch_kernel,
        grid=(width // LANES,),
        in_specs=[lane_blocks(terms.shape[0], TAPS), tile, tile, lane_blocks(2 * TAPS)],
        out_specs=[tile, tile, pl.BlockSpec((8, PER, TAPS), lambda l: (0, l, 0))],
        out_shape=[jax.ShapeDtypeStruct((TAPS, width), BF16)] * 2
        + [jax.ShapeDtypeStruct((8, width // GROUP, TAPS), F32)],
        compiler_params=VMEM,
        name="branch",
    )(terms, conv, query, turned)


def partial_products(parts, weights):
    width = weights[0].shape[1]
    place = jnp.stack([lax.axis_index(Z), lax.axis_index("co"), lax.axis_index("yp")]).astype(jnp.int32)
    whole = pl.BlockSpec(memory_space=pltpu.VMEM)
    out = pl.pallas_call(
        product_kernel,
        in_specs=[pl.BlockSpec(memory_space=pltpu.SMEM)]
        + [whole] * 3
        + [pl.BlockSpec(memory_space=pltpu.HBM)] * len(weights),
        out_specs=whole,
        out_shape=jax.ShapeDtypeStruct((4, 4, 2, 16, width), BF16),
        scratch_shapes=[pltpu.VMEM((4, TAPS, width), F32)]
        + [pltpu.VMEM(a.shape, a.dtype) for a in weights]
        + [pltpu.SemaphoreType.DMA((len(weights),))],
        compiler_params=VMEM,
        name="product",
    )(place, *parts, *weights)
    return out.reshape(4, TAPS, width)


def exchange(copies, axes):
    return lax.all_to_all(copies, axes, split_axis=0, concat_axis=0)


def ahead(block, axes, distance):
    n = lax.axis_size(axes)
    return lax.ppermute(block, axes, [((i + distance) % n, i) for i in range(n)])


def along_z(block, steps):
    n = lax.axis_size(Z)
    route = [(2 * i, 2 * ((i + steps) % n)) for i in range(n)]
    route += [(2 * i + 1, 2 * ((i - steps) % n) + 1) for i in range(n)]
    return lax.ppermute(block, Z + ("co",), route)


def after_these(value, *others):
    return lax.optimization_barrier((value,) + others)[0]


def local(query_branch, key_branch, value_branch, cotangent, out_weight, filters):
    query, keys, values = query_branch[0], key_branch[0], value_branch[0]
    tokens, width = query.shape
    chip = in_order(out_weight, swap(out_weight, "co"), "co").reshape(2 * out_weight.shape[0], width)
    copies = spread(cotangent[0])
    rows, columns = copies.shape[2:]
    own = exchange(copies.reshape(16, rows, columns), ("x", "yq"))

    one, four = along_z(chip, 1), along_z(chip, 4)
    keys = after_these(keys, chip)
    mixed = (keys.astype(F32) * values.astype(F32)).astype(BF16)
    before = from_behind(mixed, 1)
    pair = after_these(jnp.concatenate([chip, one], 0), four, before)
    own = after_these(own, pair)
    low, high = ahead(own[:8], Y, -1), ahead(own[8:], Y, 1)
    pair = after_these(along_z(pair, 2), own)
    weights = [chip, one, swap(one, "co"), four, pair, swap(pair, "co")]
    parts = [part.reshape(-1, columns) for part in (own, low, high)]

    terms = exchange(partial_products(parts, weights), "x")
    conv, turned = convolve(filters, before, mixed)
    query_grad, conv_grad, lags = branch_gradients(terms, conv, query, turned)
    lags = summed_copies(exchange(lags, ("x", "co")))
    after = from_behind(conv_grad, -1)
    lags, after = lax.optimization_barrier((lags, after))
    scale = 1.0 / math.sqrt(2 * lax.axis_size(CONTEXT) * tokens * GROUP)
    filter_grad = jnp.sum(exchange(lags, Z), axis=0) * scale
    key_grad, value_grad = mixed_gradient(filters, conv_grad, after, keys, values)
    return (query_grad[None], key_grad[None], value_grad[None], filter_grad)


def solution(mesh):
    fine = Mesh(mesh.devices.reshape(2, 4, 4, 2, 4, 2), ("zh", "x", "zl", "co", "yq", "yp"))
    branch = P("zh", CONTEXT, Y)
    return jax.shard_map(
        local,
        mesh=fine,
        in_specs=(
            branch,
            branch,
            branch,
            P("zh", CONTEXT + Y, None),
            P(("zh",) + CONTEXT, Y),
            P(Y, None),
        ),
        out_specs=(branch, branch, branch, P(Y, None)),
        check_vma=False,
    )
```

```python
import math

import jax
import jax.numpy as jnp
from jax import lax
from jax.experimental import pallas as pl
from jax.experimental.pallas import tpu as pltpu
from jax.sharding import Mesh, PartitionSpec as P

GROUP = 16
TAPS = 128
LANES = 128
PER = LANES // GROUP
F32 = jnp.float32
BF16 = jnp.bfloat16

Z = ("zh", "zl")
CONTEXT = ("x", "zl", "co")
Y = ("yq", "yp")
VMEM = pltpu.CompilerParams(vmem_limit_bytes=8 * 1024 * 1024)


def swap(block, axis):
    return lax.ppermute(block, axis, [(0, 1), (1, 0)])


def in_order(mine, theirs, axis):
    first = lax.axis_index(axis) == 0
    return jnp.stack([jnp.where(first, mine, theirs), jnp.where(first, theirs, mine)])


def from_behind(block, distance):
    n = lax.axis_size(CONTEXT)
    route = [(i - distance, i) for i in range(n) if 0 <= i - distance < n]
    return lax.ppermute(block, CONTEXT, route)


def shifted_rows(row):
    return pltpu.roll(jnp.broadcast_to(row, (TAPS, 2 * TAPS)), 0, 1, stride=1, stride_axis=0)


def skewed_sum(rows):
    return jnp.sum(pltpu.roll(rows, 1, 1, stride=1, stride_axis=0), axis=0, keepdims=True)


def lane_group(shape):
    return lax.broadcasted_iota(jnp.int32, shape, 1) >> 4


def filtered(rows, window):
    owner = lane_group((TAPS, LANES))
    total = jnp.zeros((TAPS, LANES), F32)
    for g in range(PER):
        table = shifted_rows(rows[g : g + 1, :]).astype(BF16)
        term = jnp.dot(table, window, preferred_element_type=F32)
        total = jnp.where(owner == g, term, total)
    return total


def antidiagonal(rows, columns, total):
    across = lax.broadcasted_iota(jnp.int32, (rows, columns), 0) + lax.broadcasted_iota(jnp.int32, (rows, columns), 1)
    return (across == total).astype(F32).astype(BF16)


def conv_kernel(filters_ref, before_ref, mixed_ref, conv_ref, turned_ref):
    window = jnp.concatenate([before_ref[...], mixed_ref[...]], 0)
    n = 2 * TAPS
    rows = jnp.dot(filters_ref[...], antidiagonal(TAPS, n, TAPS), preferred_element_type=F32)
    conv_ref[...] = filtered(rows, window)
    turned_ref[...] = jnp.dot(antidiagonal(n, n, n - 1), window, preferred_element_type=F32).astype(BF16)


def mixed_grad_kernel(filters_ref, grad_ref, after_ref, key_ref, value_ref, key_grad_ref, value_grad_ref):
    window = jnp.concatenate([grad_ref[...], after_ref[...]], 0)
    taps = filters_ref[...].astype(F32)
    mixed_grad = filtered(jnp.concatenate([taps, jnp.zeros(taps.shape, F32)], 1), window)
    key_grad_ref[...] = (mixed_grad * value_ref[...].astype(F32)).astype(BF16)
    value_grad_ref[...] = (mixed_grad * key_ref[...].astype(F32)).astype(BF16)


def spread_kernel(cot_ref, out_ref):
    size = cot_ref.shape[1] // 8
    for x in range(4):
        for zh in range(2):
            out_ref[x, 0, :, zh * size : (zh + 1) * size] = cot_ref[:, (4 * zh + x) * size : (4 * zh + x + 1) * size]


def sum_kernel(parts_ref, out_ref):
    total = jnp.sum(parts_ref[...], axis=0)
    for i in range(out_ref.shape[0]):
        out_ref[i] = total


def branch_kernel(terms_ref, conv_ref, query_ref, turned_ref, query_grad_ref, conv_grad_ref, lag_ref):
    branch_grad = terms_ref[0].astype(F32)
    for x in range(1, terms_ref.shape[0]):
        branch_grad = branch_grad + terms_ref[x].astype(F32)
    query_grad_ref[...] = (branch_grad * conv_ref[...]).astype(BF16)
    conv_grad = (branch_grad * query_ref[...].astype(F32)).astype(BF16)
    conv_grad_ref[...] = conv_grad
    owner = lane_group((TAPS, LANES))
    wide = conv_grad.astype(F32)
    for g in range(PER):
        part = jnp.where(owner == g, wide, 0.0).astype(BF16)
        outer = lax.dot_general(part, turned_ref[...], (((1,), (1,)), ((), ())), preferred_element_type=F32)
        sums = skewed_sum(outer)[:, TAPS:]
        for copy in range(lag_ref.shape[0]):
            lag_ref[copy, g : g + 1, :] = sums


def product_kernel(place_ref, cot_ref, *refs):
    count = (len(refs) - 3) // 2
    weights_hbm, out_ref, total_ref, weights, sems = refs[:count], refs[count], refs[count + 1], refs[count + 2 : -1], refs[-1]
    copies = [pltpu.make_async_copy(weights_hbm[i], weights[i], sems.at[i]) for i in range(count)]
    for copy in copies:
        copy.start()
    z, core = place_ref[0], place_ref[1]
    depth = weights[0].shape[0]
    below, above = [lax.rem(z + 8 - i, 8) for i in range(4)], [lax.rem(z + i, 8) for i in range(4)]
    mine = [jnp.where(core == 0, b, a) for b, a in zip(below, above)]
    theirs = [jnp.where(core == 0, a, b) for b, a in zip(below, above)]
    pieces = [(0, 0, z), (1, 0, mine[1]), (2, 0, theirs[1]), (3, 0, lax.rem(z + 4, 8))]
    pieces += [(4, 0, mine[2]), (4, depth, mine[3]), (5, 0, theirs[2]), (5, depth, theirs[3])]
    for n, (i, offset, place) in enumerate(pieces):
        if offset == 0:
            copies[i].wait()
        weight = weights[i][offset : offset + depth, :]
        columns = pl.ds(pl.multiple_of(place * depth, LANES), depth)
        for x in range(4):
            term = jnp.dot(cot_ref[x * TAPS : (x + 1) * TAPS, columns], weight, preferred_element_type=F32)
            if n:
                term = total_ref[x] + term
            if n < len(pieces) - 1:
                total_ref[x] = term
            else:
                out_ref[x] = term.astype(BF16)


def lane_blocks(*lead):
    return pl.BlockSpec(lead + (LANES,), lambda l: (0,) * len(lead) + (l,))


FILTER_BLOCK = pl.BlockSpec((PER, TAPS), lambda l: (l, 0))


def spread(cotangent):
    rows, width = cotangent.shape
    return pl.pallas_call(
        spread_kernel,
        grid=(8,),
        in_specs=[pl.BlockSpec((rows, width), lambda i: (0, 0))],
        out_specs=pl.BlockSpec((4, 1, rows, width // 4), lambda i: (0, i, 0, 0)),
        out_shape=jax.ShapeDtypeStruct((4, 8, rows, width // 4), cotangent.dtype),
        compiler_params=VMEM,
        name="spread",
    )(cotangent)


def summed_copies(parts):
    return pl.pallas_call(
        sum_kernel,
        out_shape=jax.ShapeDtypeStruct(parts.shape, parts.dtype),
        compiler_params=VMEM,
        name="sums",
    )(parts)


def convolve(filters, before, mixed):
    width = mixed.shape[1]
    tile = lane_blocks(TAPS)
    return pl.pallas_call(
        conv_kernel,
        grid=(width // LANES,),
        in_specs=[FILTER_BLOCK, tile, tile],
        out_specs=[tile, lane_blocks(2 * TAPS)],
        out_shape=[jax.ShapeDtypeStruct((TAPS, width), F32), jax.ShapeDtypeStruct((2 * TAPS, width), BF16)],
        compiler_params=VMEM,
        name="conv",
    )(filters, before, mixed)


def mixed_gradient(filters, grad, after, keys, values):
    width = grad.shape[1]
    tile = lane_blocks(TAPS)
    return pl.pallas_call(
        mixed_grad_kernel,
        grid=(width // LANES,),
        in_specs=[FILTER_BLOCK, tile, tile, tile, tile],
        out_specs=[tile, tile],
        out_shape=[jax.ShapeDtypeStruct((TAPS, width), BF16)] * 2,
        compiler_params=VMEM,
        name="mixed_grad",
    )(filters, grad, after, keys, values)


def branch_gradients(terms, conv, query, turned):
    width = query.shape[1]
    tile = lane_blocks(TAPS)
    return pl.pallas_call(
        branch_kernel,
        grid=(width // LANES,),
        in_specs=[lane_blocks(terms.shape[0], TAPS), tile, tile, lane_blocks(2 * TAPS)],
        out_specs=[tile, tile, pl.BlockSpec((8, PER, TAPS), lambda l: (0, l, 0))],
        out_shape=[jax.ShapeDtypeStruct((TAPS, width), BF16)] * 2
        + [jax.ShapeDtypeStruct((8, width // GROUP, TAPS), F32)],
        compiler_params=VMEM,
        name="branch",
    )(terms, conv, query, turned)


def partial_products(cotangent, weights):
    width = weights[0].shape[1]
    place = jnp.stack([lax.axis_index(Z), lax.axis_index("co")]).astype(jnp.int32)
    whole = pl.BlockSpec(memory_space=pltpu.VMEM)
    return pl.pallas_call(
        product_kernel,
        in_specs=[pl.BlockSpec(memory_space=pltpu.SMEM), whole]
        + [pl.BlockSpec(memory_space=pltpu.HBM)] * len(weights),
        out_specs=whole,
        out_shape=jax.ShapeDtypeStruct((4, TAPS, width), BF16),
        scratch_shapes=[pltpu.VMEM((4, TAPS, width), F32)]
        + [pltpu.VMEM(a.shape, a.dtype) for a in weights]
        + [pltpu.SemaphoreType.DMA((len(weights),))],
        compiler_params=VMEM,
        name="product",
    )(place, cotangent, *weights)


def exchange(copies, axes):
    return lax.all_to_all(copies, axes, split_axis=0, concat_axis=0)


def after_these(value, *others):
    return lax.optimization_barrier((value,) + others)[0]


def along_z(block, steps):
    n = lax.axis_size(Z)
    route = [(2 * i, 2 * ((i + steps) % n)) for i in range(n)]
    route += [(2 * i + 1, 2 * ((i - steps) % n) + 1) for i in range(n)]
    return lax.ppermute(block, Z + ("co",), route)


def weight_blocks(chip):
    one, four = along_z(chip, 1), along_z(chip, 4)
    pair = along_z(jnp.concatenate([chip, one], 0), 2)
    return [chip, one, swap(one, "co"), four, pair, swap(pair, "co")]


def local(query_branch, key_branch, value_branch, cotangent, out_weight, filters):
    query, keys, values = query_branch[0], key_branch[0], value_branch[0]
    tokens, width = query.shape
    chip = in_order(out_weight, swap(out_weight, "co"), "co").reshape(2 * out_weight.shape[0], width)
    copies = spread(cotangent[0])
    gathered = exchange(copies.reshape((32,) + copies.shape[2:]), ("x",) + Y).reshape(4 * TAPS, -1)

    keys = after_these(keys, chip)
    mixed = (keys.astype(F32) * values.astype(F32)).astype(BF16)
    conv, turned = convolve(filters, from_behind(mixed, 1), mixed)
    weights = weight_blocks(chip)
    gathered = after_these(gathered, conv, *weights)
    terms = exchange(partial_products(gathered, weights), "x")
    query_grad, conv_grad, lags = branch_gradients(terms, conv, query, turned)
    lags = summed_copies(exchange(lags, ("x", "co")))
    after = from_behind(conv_grad, -1)
    lags, after = lax.optimization_barrier((lags, after))
    scale = 1.0 / math.sqrt(2 * lax.axis_size(CONTEXT) * tokens * GROUP)
    filter_grad = jnp.sum(exchange(lags, Z), axis=0) * scale
    key_grad, value_grad = mixed_gradient(filters, conv_grad, after, keys, values)
    return (query_grad[None], key_grad[None], value_grad[None], filter_grad)


def solution(mesh):
    fine = Mesh(mesh.devices.reshape(2, 4, 4, 2, 4, 2), ("zh", "x", "zl", "co", "yq", "yp"))
    branch = P("zh", CONTEXT, Y)
    return jax.shard_map(
        local,
        mesh=fine,
        in_specs=(
            branch,
            branch,
            branch,
            P("zh", CONTEXT + Y, None),
            P(("zh",) + CONTEXT, Y),
            P(Y, None),
        ),
        out_specs=(branch, branch, branch, P(Y, None)),
        check_vma=False,
    )
```

```python
import math

import jax
import jax.numpy as jnp
from jax import lax
from jax.experimental import pallas as pl
from jax.experimental.pallas import tpu as pltpu
from jax.sharding import Mesh, PartitionSpec as P

GROUP = 16
TAPS = 128
LANES = 128
PER = LANES // GROUP
F32 = jnp.float32
BF16 = jnp.bfloat16

Z = ("zh", "zl")
CONTEXT = ("x", "zl", "co")
Y = ("yq", "yp")
VMEM = pltpu.CompilerParams(vmem_limit_bytes=8 * 1024 * 1024)


def swap(block, axis):
    return lax.ppermute(block, axis, [(0, 1), (1, 0)])


def in_order(mine, theirs, axis):
    first = lax.axis_index(axis) == 0
    return jnp.stack([jnp.where(first, mine, theirs), jnp.where(first, theirs, mine)])


def from_behind(block, distance):
    n = lax.axis_size(CONTEXT)
    route = [(i - distance, i) for i in range(n) if 0 <= i - distance < n]
    return lax.ppermute(block, CONTEXT, route)


def shifted_rows(row):
    return pltpu.roll(jnp.broadcast_to(row, (TAPS, 2 * TAPS)), 0, 1, stride=1, stride_axis=0)


def skewed_sum(rows):
    return jnp.sum(pltpu.roll(rows, 1, 1, stride=1, stride_axis=0), axis=0, keepdims=True)


def lane_group(shape):
    return lax.broadcasted_iota(jnp.int32, shape, 1) >> 4


def filtered(rows, window):
    owner = lane_group((TAPS, LANES))
    total = jnp.zeros((TAPS, LANES), F32)
    for g in range(PER):
        table = shifted_rows(rows[g : g + 1, :]).astype(BF16)
        term = jnp.dot(table, window, preferred_element_type=F32)
        total = jnp.where(owner == g, term, total)
    return total


def antidiagonal(rows, columns, total):
    across = lax.broadcasted_iota(jnp.int32, (rows, columns), 0) + lax.broadcasted_iota(jnp.int32, (rows, columns), 1)
    return (across == total).astype(F32).astype(BF16)


def conv_kernel(filters_ref, before_ref, mixed_ref, conv_ref, turned_ref):
    window = jnp.concatenate([before_ref[...], mixed_ref[...]], 0)
    n = 2 * TAPS
    rows = jnp.dot(filters_ref[...], antidiagonal(TAPS, n, TAPS), preferred_element_type=F32)
    conv_ref[...] = filtered(rows, window)
    turned_ref[...] = jnp.dot(antidiagonal(n, n, n - 1), window, preferred_element_type=F32).astype(BF16)


def mixed_grad_kernel(filters_ref, grad_ref, after_ref, key_ref, value_ref, key_grad_ref, value_grad_ref):
    window = jnp.concatenate([grad_ref[...], after_ref[...]], 0)
    taps = filters_ref[...].astype(F32)
    mixed_grad = filtered(jnp.concatenate([taps, jnp.zeros(taps.shape, F32)], 1), window)
    key_grad_ref[...] = (mixed_grad * value_ref[...].astype(F32)).astype(BF16)
    value_grad_ref[...] = (mixed_grad * key_ref[...].astype(F32)).astype(BF16)


def spread_kernel(cot_ref, out_ref):
    size = cot_ref.shape[1] // 8
    for x in range(4):
        for zh in range(2):
            out_ref[x, 0, :, zh * size : (zh + 1) * size] = cot_ref[:, (4 * zh + x) * size : (4 * zh + x + 1) * size]


def sum_kernel(parts_ref, out_ref):
    total = jnp.sum(parts_ref[...], axis=0)
    for i in range(out_ref.shape[0]):
        out_ref[i] = total


def branch_kernel(terms_ref, conv_ref, query_ref, turned_ref, query_grad_ref, conv_grad_ref, lag_ref):
    branch_grad = terms_ref[0].astype(F32)
    for x in range(1, terms_ref.shape[0]):
        branch_grad = branch_grad + terms_ref[x].astype(F32)
    query_grad_ref[...] = (branch_grad * conv_ref[...]).astype(BF16)
    conv_grad = (branch_grad * query_ref[...].astype(F32)).astype(BF16)
    conv_grad_ref[...] = conv_grad
    owner = lane_group((TAPS, LANES))
    wide = conv_grad.astype(F32)
    for g in range(PER):
        part = jnp.where(owner == g, wide, 0.0).astype(BF16)
        outer = lax.dot_general(part, turned_ref[...], (((1,), (1,)), ((), ())), preferred_element_type=F32)
        sums = skewed_sum(outer)[:, TAPS:]
        for copy in range(lag_ref.shape[0]):
            lag_ref[copy, g : g + 1, :] = sums


def product_kernel(place_ref, cot_ref, *refs):
    count = (len(refs) - 3) // 2
    weights_hbm, out_ref, total_ref, weights, sems = refs[:count], refs[count], refs[count + 1], refs[count + 2 : -1], refs[-1]
    copies = [pltpu.make_async_copy(weights_hbm[i], weights[i], sems.at[i]) for i in range(count)]
    for copy in copies:
        copy.start()
    z, core = place_ref[0], place_ref[1]
    depth = weights[0].shape[0]
    below, above = [lax.rem(z + 8 - i, 8) for i in range(4)], [lax.rem(z + i, 8) for i in range(4)]
    mine = [jnp.where(core == 0, b, a) for b, a in zip(below, above)]
    theirs = [jnp.where(core == 0, a, b) for b, a in zip(below, above)]
    pieces = [(0, 0, z), (1, 0, mine[1]), (2, 0, theirs[1]), (3, 0, lax.rem(z + 4, 8))]
    pieces += [(4, 0, mine[2]), (4, depth, mine[3]), (5, 0, theirs[2]), (5, depth, theirs[3])]
    for n, (i, offset, place) in enumerate(pieces):
        if offset == 0:
            copies[i].wait()
        weight = weights[i][offset : offset + depth, :]
        columns = pl.ds(pl.multiple_of(place * depth, LANES), depth)
        for x in range(4):
            term = jnp.dot(cot_ref[x * TAPS : (x + 1) * TAPS, columns], weight, preferred_element_type=F32)
            if n:
                term = total_ref[x] + term
            if n < len(pieces) - 1:
                total_ref[x] = term
            else:
                out_ref[x] = term.astype(BF16)


def lane_blocks(*lead):
    return pl.BlockSpec(lead + (LANES,), lambda l: (0,) * len(lead) + (l,))


FILTER_BLOCK = pl.BlockSpec((PER, TAPS), lambda l: (l, 0))


def spread(cotangent):
    rows, width = cotangent.shape
    return pl.pallas_call(
        spread_kernel,
        grid=(8,),
        in_specs=[pl.BlockSpec((rows, width), lambda i: (0, 0))],
        out_specs=pl.BlockSpec((4, 1, rows, width // 4), lambda i: (0, i, 0, 0)),
        out_shape=jax.ShapeDtypeStruct((4, 8, rows, width // 4), cotangent.dtype),
        compiler_params=VMEM,
        name="spread",
    )(cotangent)


def summed_copies(parts):
    return pl.pallas_call(
        sum_kernel,
        out_shape=jax.ShapeDtypeStruct(parts.shape, parts.dtype),
        compiler_params=VMEM,
        name="sums",
    )(parts)


def convolve(filters, before, mixed):
    width = mixed.shape[1]
    tile = lane_blocks(TAPS)
    return pl.pallas_call(
        conv_kernel,
        grid=(width // LANES,),
        in_specs=[FILTER_BLOCK, tile, tile],
        out_specs=[tile, lane_blocks(2 * TAPS)],
        out_shape=[jax.ShapeDtypeStruct((TAPS, width), F32), jax.ShapeDtypeStruct((2 * TAPS, width), BF16)],
        compiler_params=VMEM,
        name="conv",
    )(filters, before, mixed)


def mixed_gradient(filters, grad, after, keys, values):
    width = grad.shape[1]
    tile = lane_blocks(TAPS)
    return pl.pallas_call(
        mixed_grad_kernel,
        grid=(width // LANES,),
        in_specs=[FILTER_BLOCK, tile, tile, tile, tile],
        out_specs=[tile, tile],
        out_shape=[jax.ShapeDtypeStruct((TAPS, width), BF16)] * 2,
        compiler_params=VMEM,
        name="mixed_grad",
    )(filters, grad, after, keys, values)


def branch_gradients(terms, conv, query, turned):
    width = query.shape[1]
    tile = lane_blocks(TAPS)
    return pl.pallas_call(
        branch_kernel,
        grid=(width // LANES,),
        in_specs=[lane_blocks(terms.shape[0], TAPS), tile, tile, lane_blocks(2 * TAPS)],
        out_specs=[tile, tile, pl.BlockSpec((8, PER, TAPS), lambda l: (0, l, 0))],
        out_shape=[jax.ShapeDtypeStruct((TAPS, width), BF16)] * 2
        + [jax.ShapeDtypeStruct((8, width // GROUP, TAPS), F32)],
        compiler_params=VMEM,
        name="branch",
    )(terms, conv, query, turned)


def partial_products(cotangent, weights):
    width = weights[0].shape[1]
    place = jnp.stack([lax.axis_index(Z), lax.axis_index("co")]).astype(jnp.int32)
    whole = pl.BlockSpec(memory_space=pltpu.VMEM)
    return pl.pallas_call(
        product_kernel,
        in_specs=[pl.BlockSpec(memory_space=pltpu.SMEM), whole]
        + [pl.BlockSpec(memory_space=pltpu.HBM)] * len(weights),
        out_specs=whole,
        out_shape=jax.ShapeDtypeStruct((4, TAPS, width), BF16),
        scratch_shapes=[pltpu.VMEM((4, TAPS, width), F32)]
        + [pltpu.VMEM(a.shape, a.dtype) for a in weights]
        + [pltpu.SemaphoreType.DMA((len(weights),))],
        compiler_params=VMEM,
        name="product",
    )(place, cotangent, *weights)


def exchange(copies, axes):
    return lax.all_to_all(copies, axes, split_axis=0, concat_axis=0)


def after_these(value, *others):
    return lax.optimization_barrier((value,) + others)[0]


def along_z(block, steps):
    n = lax.axis_size(Z)
    route = [(2 * i, 2 * ((i + steps) % n)) for i in range(n)]
    route += [(2 * i + 1, 2 * ((i - steps) % n) + 1) for i in range(n)]
    return lax.ppermute(block, Z + ("co",), route)


def weight_blocks(chip, beside):
    one, four = along_z(chip, 1), along_z(chip, 4)
    pair = along_z(jnp.concatenate([chip, one], 0), 2)
    other = swap(one, "co")
    pair = after_these(pair, four, other, beside)
    return [chip, one, other, four, pair, swap(pair, "co")]


def local(query_branch, key_branch, value_branch, cotangent, out_weight, filters):
    query, keys, values = query_branch[0], key_branch[0], value_branch[0]
    tokens, width = query.shape
    chip = in_order(out_weight, swap(out_weight, "co"), "co").reshape(2 * out_weight.shape[0], width)
    copies = spread(cotangent[0])
    gathered = exchange(copies.reshape((32,) + copies.shape[2:]), ("x",) + Y).reshape(4 * TAPS, -1)

    keys = after_these(keys, chip)
    mixed = (keys.astype(F32) * values.astype(F32)).astype(BF16)
    conv, turned = convolve(filters, from_behind(mixed, 1), mixed)
    weights = weight_blocks(chip, conv)
    gathered = after_these(gathered, conv, *weights)
    terms = exchange(partial_products(gathered, weights), "x")
    query_grad, conv_grad, lags = branch_gradients(terms, conv, query, turned)
    lags = summed_copies(exchange(lags, ("x", "co")))
    after = from_behind(conv_grad, -1)
    lags, after = lax.optimization_barrier((lags, after))
    scale = 1.0 / math.sqrt(2 * lax.axis_size(CONTEXT) * tokens * GROUP)
    filter_grad = jnp.sum(exchange(lags, Z), axis=0) * scale
    key_grad, value_grad = mixed_gradient(filters, conv_grad, after, keys, values)
    return (query_grad[None], key_grad[None], value_grad[None], filter_grad)


def solution(mesh):
    fine = Mesh(mesh.devices.reshape(2, 4, 4, 2, 4, 2), ("zh", "x", "zl", "co", "yq", "yp"))
    branch = P("zh", CONTEXT, Y)
    return jax.shard_map(
        local,
        mesh=fine,
        in_specs=(
            branch,
            branch,
            branch,
            P("zh", CONTEXT + Y, None),
            P(("zh",) + CONTEXT, Y),
            P(Y, None),
        ),
        out_specs=(branch, branch, branch, P(Y, None)),
        check_vma=False,
    )
```

```python
import math

import jax
import jax.numpy as jnp
from jax import lax
from jax.experimental import pallas as pl
from jax.experimental.pallas import tpu as pltpu
from jax.sharding import Mesh, PartitionSpec as P

GROUP = 16
TAPS = 128
LANES = 128
PER = LANES // GROUP
F32 = jnp.float32
BF16 = jnp.bfloat16

Z = ("zh", "zl")
CONTEXT = ("x", "zl", "co")
Y = ("yq", "yp")
VMEM = pltpu.CompilerParams(vmem_limit_bytes=3 * 1024 * 1024)
PRODUCT_VMEM = pltpu.CompilerParams(vmem_limit_bytes=8 * 1024 * 1024)


def swap(block, axis):
    return lax.ppermute(block, axis, [(0, 1), (1, 0)])


def in_order(mine, theirs, axis):
    first = lax.axis_index(axis) == 0
    return jnp.stack([jnp.where(first, mine, theirs), jnp.where(first, theirs, mine)])


def from_behind(block, distance):
    n = lax.axis_size(CONTEXT)
    route = [(i - distance, i) for i in range(n) if 0 <= i - distance < n]
    return lax.ppermute(block, CONTEXT, route)


def shifted_rows(row):
    return pltpu.roll(jnp.broadcast_to(row, (TAPS, 2 * TAPS)), 0, 1, stride=1, stride_axis=0)


def skewed_sum(rows):
    return jnp.sum(pltpu.roll(rows, 1, 1, stride=1, stride_axis=0), axis=0, keepdims=True)


def lane_group(shape):
    return lax.broadcasted_iota(jnp.int32, shape, 1) >> 4


def filtered(rows, window):
    owner = lane_group((TAPS, LANES))
    total = jnp.zeros((TAPS, LANES), F32)
    for g in range(PER):
        table = shifted_rows(rows[g : g + 1, :]).astype(BF16)
        term = jnp.dot(table, window, preferred_element_type=F32)
        total = jnp.where(owner == g, term, total)
    return total


def antidiagonal(rows, columns, total):
    across = lax.broadcasted_iota(jnp.int32, (rows, columns), 0) + lax.broadcasted_iota(jnp.int32, (rows, columns), 1)
    return (across == total).astype(F32).astype(BF16)


def conv_kernel(filters_ref, before_ref, mixed_ref, conv_ref, turned_ref):
    window = jnp.concatenate([before_ref[...], mixed_ref[...]], 0)
    n = 2 * TAPS
    rows = jnp.dot(filters_ref[...], antidiagonal(TAPS, n, TAPS), preferred_element_type=F32)
    conv_ref[...] = filtered(rows, window)
    turned_ref[...] = jnp.dot(antidiagonal(n, n, n - 1), window, preferred_element_type=F32).astype(BF16)


def mixed_grad_kernel(filters_ref, grad_ref, after_ref, key_ref, value_ref, key_grad_ref, value_grad_ref):
    window = jnp.concatenate([grad_ref[...], after_ref[...]], 0)
    taps = filters_ref[...].astype(F32)
    mixed_grad = filtered(jnp.concatenate([taps, jnp.zeros(taps.shape, F32)], 1), window)
    key_grad_ref[...] = (mixed_grad * value_ref[...].astype(F32)).astype(BF16)
    value_grad_ref[...] = (mixed_grad * key_ref[...].astype(F32)).astype(BF16)


def spread_kernel(cot_ref, out_ref):
    size = cot_ref.shape[1] // 8
    for x in range(4):
        for zh in range(2):
            out_ref[x, 0, :, zh * size : (zh + 1) * size] = cot_ref[:, (4 * zh + x) * size : (4 * zh + x + 1) * size]


def sum_kernel(parts_ref, out_ref):
    total = jnp.sum(parts_ref[...], axis=0)
    for i in range(out_ref.shape[0]):
        out_ref[i] = total


def branch_kernel(terms_ref, conv_ref, query_ref, turned_ref, query_grad_ref, conv_grad_ref, lag_ref):
    branch_grad = terms_ref[0].astype(F32)
    for x in range(1, terms_ref.shape[0]):
        branch_grad = branch_grad + terms_ref[x].astype(F32)
    query_grad_ref[...] = (branch_grad * conv_ref[...]).astype(BF16)
    conv_grad = (branch_grad * query_ref[...].astype(F32)).astype(BF16)
    conv_grad_ref[...] = conv_grad
    owner = lane_group((TAPS, LANES))
    wide = conv_grad.astype(F32)
    for g in range(PER):
        part = jnp.where(owner == g, wide, 0.0).astype(BF16)
        outer = lax.dot_general(part, turned_ref[...], (((1,), (1,)), ((), ())), preferred_element_type=F32)
        sums = skewed_sum(outer)[:, TAPS:]
        for copy in range(lag_ref.shape[0]):
            lag_ref[copy, g : g + 1, :] = sums


def product_kernel(place_ref, cot_ref, *refs):
    count = (len(refs) - 3) // 2
    weights_hbm, out_ref, total_ref, weights, sems = refs[:count], refs[count], refs[count + 1], refs[count + 2 : -1], refs[-1]
    copies = [pltpu.make_async_copy(weights_hbm[i], weights[i], sems.at[i]) for i in range(count)]
    for copy in copies:
        copy.start()
    z, core = place_ref[0], place_ref[1]
    depth = weights[0].shape[0]
    below, above = [lax.rem(z + 8 - i, 8) for i in range(4)], [lax.rem(z + i, 8) for i in range(4)]
    mine = [jnp.where(core == 0, b, a) for b, a in zip(below, above)]
    theirs = [jnp.where(core == 0, a, b) for b, a in zip(below, above)]
    pieces = [(0, 0, z), (1, 0, mine[1]), (2, 0, theirs[1]), (3, 0, lax.rem(z + 4, 8))]
    pieces += [(4, 0, mine[2]), (4, depth, mine[3]), (5, 0, theirs[2]), (5, depth, theirs[3])]
    for n, (i, offset, place) in enumerate(pieces):
        if offset == 0:
            copies[i].wait()
        weight = weights[i][offset : offset + depth, :]
        columns = pl.ds(pl.multiple_of(place * depth, LANES), depth)
        for x in range(4):
            term = jnp.dot(cot_ref[x * TAPS : (x + 1) * TAPS, columns], weight, preferred_element_type=F32)
            if n:
                term = total_ref[x] + term
            if n < len(pieces) - 1:
                total_ref[x] = term
            else:
                out_ref[x] = term.astype(BF16)


def lane_blocks(*lead):
    return pl.BlockSpec(lead + (LANES,), lambda l: (0,) * len(lead) + (l,))


FILTER_BLOCK = pl.BlockSpec((PER, TAPS), lambda l: (l, 0))


def spread(cotangent):
    rows, width = cotangent.shape
    return pl.pallas_call(
        spread_kernel,
        grid=(8,),
        in_specs=[pl.BlockSpec((rows, width), lambda i: (0, 0))],
        out_specs=pl.BlockSpec((4, 1, rows, width // 4), lambda i: (0, i, 0, 0)),
        out_shape=jax.ShapeDtypeStruct((4, 8, rows, width // 4), cotangent.dtype),
        compiler_params=VMEM,
        name="spread",
    )(cotangent)


def summed_copies(parts):
    return pl.pallas_call(
        sum_kernel,
        out_shape=jax.ShapeDtypeStruct(parts.shape, parts.dtype),
        compiler_params=VMEM,
        name="sums",
    )(parts)


def convolve(filters, before, mixed):
    width = mixed.shape[1]
    tile = lane_blocks(TAPS)
    return pl.pallas_call(
        conv_kernel,
        grid=(width // LANES,),
        in_specs=[FILTER_BLOCK, tile, tile],
        out_specs=[tile, lane_blocks(2 * TAPS)],
        out_shape=[jax.ShapeDtypeStruct((TAPS, width), F32), jax.ShapeDtypeStruct((2 * TAPS, width), BF16)],
        compiler_params=VMEM,
        name="conv",
    )(filters, before, mixed)


def mixed_gradient(filters, grad, after, keys, values):
    width = grad.shape[1]
    tile = lane_blocks(TAPS)
    return pl.pallas_call(
        mixed_grad_kernel,
        grid=(width // LANES,),
        in_specs=[FILTER_BLOCK, tile, tile, tile, tile],
        out_specs=[tile, tile],
        out_shape=[jax.ShapeDtypeStruct((TAPS, width), BF16)] * 2,
        compiler_params=VMEM,
        name="mixed_grad",
    )(filters, grad, after, keys, values)


def branch_gradients(terms, conv, query, turned):
    width = query.shape[1]
    tile = lane_blocks(TAPS)
    return pl.pallas_call(
        branch_kernel,
        grid=(width // LANES,),
        in_specs=[lane_blocks(terms.shape[0], TAPS), tile, tile, lane_blocks(2 * TAPS)],
        out_specs=[tile, tile, pl.BlockSpec((8, PER, TAPS), lambda l: (0, l, 0))],
        out_shape=[jax.ShapeDtypeStruct((TAPS, width), BF16)] * 2
        + [jax.ShapeDtypeStruct((8, width // GROUP, TAPS), F32)],
        compiler_params=VMEM,
        name="branch",
    )(terms, conv, query, turned)


def partial_products(cotangent, weights):
    width = weights[0].shape[1]
    place = jnp.stack([lax.axis_index(Z), lax.axis_index("co")]).astype(jnp.int32)
    whole = pl.BlockSpec(memory_space=pltpu.VMEM)
    return pl.pallas_call(
        product_kernel,
        in_specs=[pl.BlockSpec(memory_space=pltpu.SMEM), whole]
        + [pl.BlockSpec(memory_space=pltpu.HBM)] * len(weights),
        out_specs=whole,
        out_shape=jax.ShapeDtypeStruct((4, TAPS, width), BF16),
        scratch_shapes=[pltpu.VMEM((4, TAPS, width), F32)]
        + [pltpu.VMEM(a.shape, a.dtype) for a in weights]
        + [pltpu.SemaphoreType.DMA((len(weights),))],
        compiler_params=PRODUCT_VMEM,
        name="product",
    )(place, cotangent, *weights)


def exchange(copies, axes):
    return lax.all_to_all(copies, axes, split_axis=0, concat_axis=0)


def after_these(value, *others):
    return lax.optimization_barrier((value,) + others)[0]


def along_z(block, steps):
    n = lax.axis_size(Z)
    route = [(2 * i, 2 * ((i + steps) % n)) for i in range(n)]
    route += [(2 * i + 1, 2 * ((i - steps) % n) + 1) for i in range(n)]
    return lax.ppermute(block, Z + ("co",), route)


def local(query_branch, key_branch, value_branch, cotangent, out_weight, filters):
    query, keys, values = query_branch[0], key_branch[0], value_branch[0]
    tokens, width = query.shape
    chip = in_order(out_weight, swap(out_weight, "co"), "co").reshape(2 * out_weight.shape[0], width)
    copies = spread(cotangent[0])
    gathered = exchange(copies.reshape((32,) + copies.shape[2:]), ("x",) + Y).reshape(4 * TAPS, -1)

    one, four = along_z(chip, 1), along_z(chip, 4)
    keys = after_these(keys, four)
    mixed = (keys.astype(F32) * values.astype(F32)).astype(BF16)
    conv, turned = convolve(filters, from_behind(mixed, 1), mixed)
    pair = along_z(jnp.concatenate([chip, one], 0), 2)
    other = swap(one, "co")
    pair = after_these(pair, other, conv)
    weights = [chip, one, other, four, pair, swap(pair, "co")]
    gathered = after_these(gathered, conv, *weights)
    terms = exchange(partial_products(gathered, weights), "x")
    query_grad, conv_grad, lags = branch_gradients(terms, conv, query, turned)
    lags = summed_copies(exchange(lags, ("x", "co")))
    after = from_behind(conv_grad, -1)
    lags, after = lax.optimization_barrier((lags, after))
    scale = 1.0 / math.sqrt(2 * lax.axis_size(CONTEXT) * tokens * GROUP)
    filter_grad = jnp.sum(exchange(lags, Z), axis=0) * scale
    key_grad, value_grad = mixed_gradient(filters, conv_grad, after, keys, values)
    return (query_grad[None], key_grad[None], value_grad[None], filter_grad)


def solution(mesh):
    fine = Mesh(mesh.devices.reshape(2, 4, 4, 2, 4, 2), ("zh", "x", "zl", "co", "yq", "yp"))
    branch = P("zh", CONTEXT, Y)
    return jax.shard_map(
        local,
        mesh=fine,
        in_specs=(
            branch,
            branch,
            branch,
            P("zh", CONTEXT + Y, None),
            P(("zh",) + CONTEXT, Y),
            P(Y, None),
        ),
        out_specs=(branch, branch, branch, P(Y, None)),
        check_vma=False,
    )
```

```python
import math

import jax
import jax.numpy as jnp
from jax import lax
from jax.experimental import pallas as pl
from jax.experimental.pallas import tpu as pltpu
from jax.sharding import Mesh, PartitionSpec as P

GROUP = 16
TAPS = 128
LANES = 128
PER = LANES // GROUP
F32 = jnp.float32
BF16 = jnp.bfloat16

Z = ("zh", "zl")
CONTEXT = ("x", "zl", "co")
Y = ("yq", "yp")
VMEM = pltpu.CompilerParams(vmem_limit_bytes=3 * 1024 * 1024)
PRODUCT_VMEM = pltpu.CompilerParams(vmem_limit_bytes=8 * 1024 * 1024)


def swap(block, axis):
    return lax.ppermute(block, axis, [(0, 1), (1, 0)])


def in_order(mine, theirs, axis):
    first = lax.axis_index(axis) == 0
    return jnp.stack([jnp.where(first, mine, theirs), jnp.where(first, theirs, mine)])


def from_behind(block, distance):
    n = lax.axis_size(CONTEXT)
    route = [(i - distance, i) for i in range(n) if 0 <= i - distance < n]
    return lax.ppermute(block, CONTEXT, route)


def shifted_rows(row):
    return pltpu.roll(jnp.broadcast_to(row, (TAPS, 2 * TAPS)), 0, 1, stride=1, stride_axis=0)


def skewed_sum(rows):
    return jnp.sum(pltpu.roll(rows, 1, 1, stride=1, stride_axis=0), axis=0, keepdims=True)


def lane_group(shape):
    return lax.broadcasted_iota(jnp.int32, shape, 1) >> 4


def filtered(rows, window):
    owner = lane_group((TAPS, LANES))
    total = jnp.zeros((TAPS, LANES), F32)
    for g in range(PER):
        table = shifted_rows(rows[g : g + 1, :]).astype(BF16)
        term = jnp.dot(table, window, preferred_element_type=F32)
        total = jnp.where(owner == g, term, total)
    return total


def antidiagonal(rows, columns, total):
    across = lax.broadcasted_iota(jnp.int32, (rows, columns), 0) + lax.broadcasted_iota(jnp.int32, (rows, columns), 1)
    return (across == total).astype(F32).astype(BF16)


def conv_kernel(filters_ref, before_ref, mixed_ref, conv_ref, turned_ref):
    window = jnp.concatenate([before_ref[...], mixed_ref[...]], 0)
    n = 2 * TAPS
    rows = jnp.dot(filters_ref[...], antidiagonal(TAPS, n, TAPS), preferred_element_type=F32)
    conv_ref[...] = filtered(rows, window)
    turned_ref[...] = jnp.dot(antidiagonal(n, n, n - 1), window, preferred_element_type=F32).astype(BF16)


def mixed_grad_kernel(filters_ref, grad_ref, after_ref, key_ref, value_ref, key_grad_ref, value_grad_ref):
    window = jnp.concatenate([grad_ref[...], after_ref[...]], 0)
    taps = filters_ref[...].astype(F32)
    mixed_grad = filtered(jnp.concatenate([taps, jnp.zeros(taps.shape, F32)], 1), window)
    key_grad_ref[...] = (mixed_grad * value_ref[...].astype(F32)).astype(BF16)
    value_grad_ref[...] = (mixed_grad * key_ref[...].astype(F32)).astype(BF16)


def spread_kernel(cot_ref, out_ref):
    size = cot_ref.shape[1] // 8
    for x in range(4):
        for zh in range(2):
            out_ref[x, 0, :, zh * size : (zh + 1) * size] = cot_ref[:, (4 * zh + x) * size : (4 * zh + x + 1) * size]


def sum_kernel(parts_ref, out_ref):
    total = jnp.sum(parts_ref[...], axis=0)
    for i in range(out_ref.shape[0]):
        out_ref[i] = total


def branch_kernel(terms_ref, conv_ref, query_ref, turned_ref, query_grad_ref, conv_grad_ref, lag_ref):
    branch_grad = terms_ref[0].astype(F32)
    for x in range(1, terms_ref.shape[0]):
        branch_grad = branch_grad + terms_ref[x].astype(F32)
    query_grad_ref[...] = (branch_grad * conv_ref[...]).astype(BF16)
    conv_grad = (branch_grad * query_ref[...].astype(F32)).astype(BF16)
    conv_grad_ref[...] = conv_grad
    owner = lane_group((TAPS, LANES))
    wide = conv_grad.astype(F32)
    for g in range(PER):
        part = jnp.where(owner == g, wide, 0.0).astype(BF16)
        outer = lax.dot_general(part, turned_ref[...], (((1,), (1,)), ((), ())), preferred_element_type=F32)
        sums = skewed_sum(outer)[:, TAPS:]
        for copy in range(lag_ref.shape[0]):
            lag_ref[copy, g : g + 1, :] = sums


def product_kernel(place_ref, cot_ref, *refs):
    count = (len(refs) - 3) // 2
    weights_hbm, out_ref, total_ref, weights, sems = refs[:count], refs[count], refs[count + 1], refs[count + 2 : -1], refs[-1]
    copies = [pltpu.make_async_copy(weights_hbm[i], weights[i], sems.at[i]) for i in range(count)]
    for copy in copies:
        copy.start()
    z, core = place_ref[0], place_ref[1]
    depth = weights[0].shape[0]
    below, above = [lax.rem(z + 8 - i, 8) for i in range(4)], [lax.rem(z + i, 8) for i in range(4)]
    mine = [jnp.where(core == 0, b, a) for b, a in zip(below, above)]
    theirs = [jnp.where(core == 0, a, b) for b, a in zip(below, above)]
    pieces = [(0, 0, z), (1, 0, mine[1]), (2, 0, theirs[1]), (3, 0, lax.rem(z + 4, 8))]
    pieces += [(4, 0, mine[2]), (4, depth, mine[3]), (5, 0, theirs[2]), (5, depth, theirs[3])]
    for n, (i, offset, place) in enumerate(pieces):
        if offset == 0:
            copies[i].wait()
        weight = weights[i][offset : offset + depth, :]
        columns = pl.ds(pl.multiple_of(place * depth, LANES), depth)
        for x in range(4):
            term = jnp.dot(cot_ref[x * TAPS : (x + 1) * TAPS, columns], weight, preferred_element_type=F32)
            if n:
                term = total_ref[x] + term
            if n < len(pieces) - 1:
                total_ref[x] = term
            else:
                out_ref[x] = term.astype(BF16)


def lane_blocks(*lead):
    return pl.BlockSpec(lead + (LANES,), lambda l: (0,) * len(lead) + (l,))


FILTER_BLOCK = pl.BlockSpec((PER, TAPS), lambda l: (l, 0))


def spread(cotangent):
    rows, width = cotangent.shape
    return pl.pallas_call(
        spread_kernel,
        grid=(8,),
        in_specs=[pl.BlockSpec((rows, width), lambda i: (0, 0))],
        out_specs=pl.BlockSpec((4, 1, rows, width // 4), lambda i: (0, i, 0, 0)),
        out_shape=jax.ShapeDtypeStruct((4, 8, rows, width // 4), cotangent.dtype),
        compiler_params=VMEM,
        name="spread",
    )(cotangent)


def summed_copies(parts):
    return pl.pallas_call(
        sum_kernel,
        out_shape=jax.ShapeDtypeStruct(parts.shape, parts.dtype),
        compiler_params=VMEM,
        name="sums",
    )(parts)


def convolve(filters, before, mixed):
    width = mixed.shape[1]
    tile = lane_blocks(TAPS)
    return pl.pallas_call(
        conv_kernel,
        grid=(width // LANES,),
        in_specs=[FILTER_BLOCK, tile, tile],
        out_specs=[tile, lane_blocks(2 * TAPS)],
        out_shape=[jax.ShapeDtypeStruct((TAPS, width), F32), jax.ShapeDtypeStruct((2 * TAPS, width), BF16)],
        compiler_params=VMEM,
        name="conv",
    )(filters, before, mixed)


def mixed_gradient(filters, grad, after, keys, values):
    width = grad.shape[1]
    tile = lane_blocks(TAPS)
    return pl.pallas_call(
        mixed_grad_kernel,
        grid=(width // LANES,),
        in_specs=[FILTER_BLOCK, tile, tile, tile, tile],
        out_specs=[tile, tile],
        out_shape=[jax.ShapeDtypeStruct((TAPS, width), BF16)] * 2,
        compiler_params=VMEM,
        name="mixed_grad",
    )(filters, grad, after, keys, values)


def branch_gradients(terms, conv, query, turned):
    width = query.shape[1]
    tile = lane_blocks(TAPS)
    return pl.pallas_call(
        branch_kernel,
        grid=(width // LANES,),
        in_specs=[lane_blocks(terms.shape[0], TAPS), tile, tile, lane_blocks(2 * TAPS)],
        out_specs=[tile, tile, pl.BlockSpec((8, PER, TAPS), lambda l: (0, l, 0))],
        out_shape=[jax.ShapeDtypeStruct((TAPS, width), BF16)] * 2
        + [jax.ShapeDtypeStruct((8, width // GROUP, TAPS), F32)],
        compiler_params=VMEM,
        name="branch",
    )(terms, conv, query, turned)


def partial_products(cotangent, weights):
    width = weights[0].shape[1]
    place = jnp.stack([lax.axis_index(Z), lax.axis_index("co")]).astype(jnp.int32)
    whole = pl.BlockSpec(memory_space=pltpu.VMEM)
    return pl.pallas_call(
        product_kernel,
        in_specs=[pl.BlockSpec(memory_space=pltpu.SMEM), whole]
        + [pl.BlockSpec(memory_space=pltpu.HBM)] * len(weights),
        out_specs=whole,
        out_shape=jax.ShapeDtypeStruct((4, TAPS, width), BF16),
        scratch_shapes=[pltpu.VMEM((4, TAPS, width), F32)]
        + [pltpu.VMEM(a.shape, a.dtype) for a in weights]
        + [pltpu.SemaphoreType.DMA((len(weights),))],
        compiler_params=PRODUCT_VMEM,
        name="product",
    )(place, cotangent, *weights)


def exchange(copies, axes):
    return lax.all_to_all(copies, axes, split_axis=0, concat_axis=0)


def after_these(value, *others):
    return lax.optimization_barrier((value,) + others)[0]


def along_z(block, steps):
    n = lax.axis_size(Z)
    route = [(2 * i, 2 * ((i + steps) % n)) for i in range(n)]
    route += [(2 * i + 1, 2 * ((i - steps) % n) + 1) for i in range(n)]
    return lax.ppermute(block, Z + ("co",), route)


def local(query_branch, key_branch, value_branch, cotangent, out_weight, filters):
    query, keys, values = query_branch[0], key_branch[0], value_branch[0]
    tokens, width = query.shape
    chip = in_order(out_weight, swap(out_weight, "co"), "co").reshape(2 * out_weight.shape[0], width)
    copies = spread(cotangent[0])
    gathered = exchange(copies.reshape((32,) + copies.shape[2:]), ("x",) + Y).reshape(4 * TAPS, -1)

    one, four = along_z(chip, 1), along_z(chip, 4)
    keys = after_these(keys, four)
    mixed = (keys.astype(F32) * values.astype(F32)).astype(BF16)
    before = from_behind(mixed, 1)
    pair = along_z(jnp.concatenate([chip, one], 0), 2)
    other = swap(one, "co")
    pair = after_these(pair, other)
    weights = [chip, one, other, four, pair, swap(pair, "co")]
    gathered = after_these(gathered, before, *weights)
    terms = exchange(partial_products(gathered, weights), "x")
    conv, turned = convolve(filters, before, mixed)
    query_grad, conv_grad, lags = branch_gradients(terms, conv, query, turned)
    lags = summed_copies(exchange(lags, ("x", "co")))
    after = from_behind(conv_grad, -1)
    lags, after = lax.optimization_barrier((lags, after))
    scale = 1.0 / math.sqrt(2 * lax.axis_size(CONTEXT) * tokens * GROUP)
    filter_grad = jnp.sum(exchange(lags, Z), axis=0) * scale
    key_grad, value_grad = mixed_gradient(filters, conv_grad, after, keys, values)
    return (query_grad[None], key_grad[None], value_grad[None], filter_grad)


def solution(mesh):
    fine = Mesh(mesh.devices.reshape(2, 4, 4, 2, 4, 2), ("zh", "x", "zl", "co", "yq", "yp"))
    branch = P("zh", CONTEXT, Y)
    return jax.shard_map(
        local,
        mesh=fine,
        in_specs=(
            branch,
            branch,
            branch,
            P("zh", CONTEXT + Y, None),
            P(("zh",) + CONTEXT, Y),
            P(Y, None),
        ),
        out_specs=(branch, branch, branch, P(Y, None)),
        check_vma=False,
    )
```

```python
import math

import jax
import jax.numpy as jnp
from jax import lax
from jax.experimental import pallas as pl
from jax.experimental.pallas import tpu as pltpu
from jax.sharding import Mesh, PartitionSpec as P

GROUP = 16
TAPS = 128
LANES = 128
PER = LANES // GROUP
F32 = jnp.float32
BF16 = jnp.bfloat16

Z = ("zh", "zl")
CONTEXT = ("x", "zl", "co")
Y = ("yq", "yp")
VMEM = pltpu.CompilerParams(vmem_limit_bytes=3 * 1024 * 1024)
PRODUCT_VMEM = pltpu.CompilerParams(vmem_limit_bytes=8 * 1024 * 1024)


def swap(block, axis):
    return lax.ppermute(block, axis, [(0, 1), (1, 0)])


def in_order(mine, theirs, axis):
    first = lax.axis_index(axis) == 0
    return jnp.stack([jnp.where(first, mine, theirs), jnp.where(first, theirs, mine)])


def from_behind(block, distance):
    n = lax.axis_size(CONTEXT)
    route = [(i - distance, i) for i in range(n) if 0 <= i - distance < n]
    return lax.ppermute(block, CONTEXT, route)


def shifted_rows(row):
    return pltpu.roll(jnp.broadcast_to(row, (TAPS, 2 * TAPS)), 0, 1, stride=1, stride_axis=0)


def skewed_sum(rows):
    return jnp.sum(pltpu.roll(rows, 1, 1, stride=1, stride_axis=0), axis=0, keepdims=True)


def lane_group(shape):
    return lax.broadcasted_iota(jnp.int32, shape, 1) >> 4


def filtered(rows, window):
    owner = lane_group((TAPS, LANES))
    total = jnp.zeros((TAPS, LANES), F32)
    for g in range(PER):
        table = shifted_rows(rows[g : g + 1, :]).astype(BF16)
        term = jnp.dot(table, window, preferred_element_type=F32)
        total = jnp.where(owner == g, term, total)
    return total


def antidiagonal(rows, columns, total):
    across = lax.broadcasted_iota(jnp.int32, (rows, columns), 0) + lax.broadcasted_iota(jnp.int32, (rows, columns), 1)
    return (across == total).astype(F32).astype(BF16)


def conv_kernel(filters_ref, before_ref, mixed_ref, conv_ref, turned_ref):
    window = jnp.concatenate([before_ref[...], mixed_ref[...]], 0)
    n = 2 * TAPS
    rows = jnp.dot(filters_ref[...], antidiagonal(TAPS, n, TAPS), preferred_element_type=F32)
    conv_ref[...] = filtered(rows, window)
    turned_ref[...] = jnp.dot(antidiagonal(n, n, n - 1), window, preferred_element_type=F32).astype(BF16)


def mixed_grad_kernel(filters_ref, grad_ref, after_ref, key_ref, value_ref, key_grad_ref, value_grad_ref):
    window = jnp.concatenate([grad_ref[...], after_ref[...]], 0)
    taps = filters_ref[...].astype(F32)
    mixed_grad = filtered(jnp.concatenate([taps, jnp.zeros(taps.shape, F32)], 1), window)
    key_grad_ref[...] = (mixed_grad * value_ref[...].astype(F32)).astype(BF16)
    value_grad_ref[...] = (mixed_grad * key_ref[...].astype(F32)).astype(BF16)


def spread_kernel(cot_ref, out_ref):
    size = cot_ref.shape[1] // 8
    for x in range(4):
        for zh in range(2):
            out_ref[x, 0, :, zh * size : (zh + 1) * size] = cot_ref[:, (4 * zh + x) * size : (4 * zh + x + 1) * size]


def sum_kernel(parts_ref, out_ref):
    total = jnp.sum(parts_ref[...], axis=0)
    for i in range(out_ref.shape[0]):
        out_ref[i] = total


def branch_kernel(terms_ref, conv_ref, query_ref, turned_ref, query_grad_ref, conv_grad_ref, lag_ref):
    branch_grad = terms_ref[0].astype(F32)
    for x in range(1, terms_ref.shape[0]):
        branch_grad = branch_grad + terms_ref[x].astype(F32)
    query_grad_ref[...] = (branch_grad * conv_ref[...]).astype(BF16)
    conv_grad = (branch_grad * query_ref[...].astype(F32)).astype(BF16)
    conv_grad_ref[...] = conv_grad
    owner = lane_group((TAPS, LANES))
    wide = conv_grad.astype(F32)
    for g in range(PER):
        part = jnp.where(owner == g, wide, 0.0).astype(BF16)
        outer = lax.dot_general(part, turned_ref[...], (((1,), (1,)), ((), ())), preferred_element_type=F32)
        sums = skewed_sum(outer)[:, TAPS:]
        for copy in range(lag_ref.shape[0]):
            lag_ref[copy, g : g + 1, :] = sums


def product_kernel(place_ref, cot_ref, *refs):
    count = (len(refs) - 3) // 2
    weights_hbm, out_ref, total_ref, weights, sems = refs[:count], refs[count], refs[count + 1], refs[count + 2 : -1], refs[-1]
    copies = [pltpu.make_async_copy(weights_hbm[i], weights[i], sems.at[i]) for i in range(count)]
    for copy in copies:
        copy.start()
    z, core = place_ref[0], place_ref[1]
    depth = weights[0].shape[0]
    below, above = [lax.rem(z + 8 - i, 8) for i in range(4)], [lax.rem(z + i, 8) for i in range(4)]
    mine = [jnp.where(core == 0, b, a) for b, a in zip(below, above)]
    theirs = [jnp.where(core == 0, a, b) for b, a in zip(below, above)]
    pieces = [(0, 0, z), (1, 0, mine[1]), (2, 0, theirs[1]), (3, 0, lax.rem(z + 4, 8))]
    pieces += [(4, 0, mine[2]), (4, depth, mine[3]), (5, 0, theirs[2]), (5, depth, theirs[3])]
    for n, (i, offset, place) in enumerate(pieces):
        if offset == 0:
            copies[i].wait()
        weight = weights[i][offset : offset + depth, :]
        columns = pl.ds(pl.multiple_of(place * depth, LANES), depth)
        for x in range(4):
            term = jnp.dot(cot_ref[x * TAPS : (x + 1) * TAPS, columns], weight, preferred_element_type=F32)
            if n:
                term = total_ref[x] + term
            if n < len(pieces) - 1:
                total_ref[x] = term
            else:
                out_ref[x] = term.astype(BF16)


def lane_blocks(*lead):
    return pl.BlockSpec(lead + (LANES,), lambda l: (0,) * len(lead) + (l,))


FILTER_BLOCK = pl.BlockSpec((PER, TAPS), lambda l: (l, 0))


def spread(cotangent):
    rows, width = cotangent.shape
    return pl.pallas_call(
        spread_kernel,
        grid=(8,),
        in_specs=[pl.BlockSpec((rows, width), lambda i: (0, 0))],
        out_specs=pl.BlockSpec((4, 1, rows, width // 4), lambda i: (0, i, 0, 0)),
        out_shape=jax.ShapeDtypeStruct((4, 8, rows, width // 4), cotangent.dtype),
        compiler_params=VMEM,
        name="spread",
    )(cotangent)


def summed_copies(parts):
    return pl.pallas_call(
        sum_kernel,
        out_shape=jax.ShapeDtypeStruct(parts.shape, parts.dtype),
        compiler_params=VMEM,
        name="sums",
    )(parts)


def convolve(filters, before, mixed):
    width = mixed.shape[1]
    tile = lane_blocks(TAPS)
    return pl.pallas_call(
        conv_kernel,
        grid=(width // LANES,),
        in_specs=[FILTER_BLOCK, tile, tile],
        out_specs=[tile, lane_blocks(2 * TAPS)],
        out_shape=[jax.ShapeDtypeStruct((TAPS, width), F32), jax.ShapeDtypeStruct((2 * TAPS, width), BF16)],
        compiler_params=VMEM,
        name="conv",
    )(filters, before, mixed)


def mixed_gradient(filters, grad, after, keys, values):
    width = grad.shape[1]
    tile = lane_blocks(TAPS)
    return pl.pallas_call(
        mixed_grad_kernel,
        grid=(width // LANES,),
        in_specs=[FILTER_BLOCK, tile, tile, tile, tile],
        out_specs=[tile, tile],
        out_shape=[jax.ShapeDtypeStruct((TAPS, width), BF16)] * 2,
        compiler_params=VMEM,
        name="mixed_grad",
    )(filters, grad, after, keys, values)


def branch_gradients(terms, conv, query, turned):
    width = query.shape[1]
    tile = lane_blocks(TAPS)
    return pl.pallas_call(
        branch_kernel,
        grid=(width // LANES,),
        in_specs=[lane_blocks(terms.shape[0], TAPS), tile, tile, lane_blocks(2 * TAPS)],
        out_specs=[tile, tile, pl.BlockSpec((8, PER, TAPS), lambda l: (0, l, 0))],
        out_shape=[jax.ShapeDtypeStruct((TAPS, width), BF16)] * 2
        + [jax.ShapeDtypeStruct((8, width // GROUP, TAPS), F32)],
        compiler_params=VMEM,
        name="branch",
    )(terms, conv, query, turned)


def partial_products(cotangent, weights):
    width = weights[0].shape[1]
    place = jnp.stack([lax.axis_index(Z), lax.axis_index("co")]).astype(jnp.int32)
    whole = pl.BlockSpec(memory_space=pltpu.VMEM)
    return pl.pallas_call(
        product_kernel,
        in_specs=[pl.BlockSpec(memory_space=pltpu.SMEM), whole]
        + [pl.BlockSpec(memory_space=pltpu.HBM)] * len(weights),
        out_specs=whole,
        out_shape=jax.ShapeDtypeStruct((4, TAPS, width), BF16),
        scratch_shapes=[pltpu.VMEM((4, TAPS, width), F32)]
        + [pltpu.VMEM(a.shape, a.dtype) for a in weights]
        + [pltpu.SemaphoreType.DMA((len(weights),))],
        compiler_params=PRODUCT_VMEM,
        name="product",
    )(place, cotangent, *weights)


def exchange(copies, axes):
    return lax.all_to_all(copies, axes, split_axis=0, concat_axis=0)


def after_these(value, *others):
    return lax.optimization_barrier((value,) + others)[0]


def along_z(block, steps):
    n = lax.axis_size(Z)
    route = [(2 * i, 2 * ((i + steps) % n)) for i in range(n)]
    route += [(2 * i + 1, 2 * ((i - steps) % n) + 1) for i in range(n)]
    return lax.ppermute(block, Z + ("co",), route)


def local(query_branch, key_branch, value_branch, cotangent, out_weight, filters):
    query, keys, values = query_branch[0], key_branch[0], value_branch[0]
    tokens, width = query.shape
    chip = in_order(out_weight, swap(out_weight, "co"), "co").reshape(2 * out_weight.shape[0], width)
    copies = spread(cotangent[0])
    gathered = exchange(copies.reshape((32,) + copies.shape[2:]), ("x",) + Y).reshape(4 * TAPS, -1)

    one, four = along_z(chip, 1), along_z(chip, 4)
    keys = after_these(keys, four)
    mixed = (keys.astype(F32) * values.astype(F32)).astype(BF16)
    before = from_behind(mixed, 1)
    pair = along_z(jnp.concatenate([chip, one], 0), 2)
    other = swap(one, "co")
    pair = after_these(pair, other, before)
    weights = [chip, one, other, four, pair, swap(pair, "co")]
    gathered = after_these(gathered, *weights)
    partial = partial_products(gathered, weights)
    terms = exchange(partial, "x")
    conv, turned = convolve(filters, after_these(before, partial), mixed)
    query_grad, conv_grad, lags = branch_gradients(terms, conv, query, turned)
    lags = summed_copies(exchange(lags, ("x", "co")))
    after = from_behind(conv_grad, -1)
    lags, after = lax.optimization_barrier((lags, after))
    scale = 1.0 / math.sqrt(2 * lax.axis_size(CONTEXT) * tokens * GROUP)
    filter_grad = jnp.sum(exchange(lags, Z), axis=0) * scale
    key_grad, value_grad = mixed_gradient(filters, conv_grad, after, keys, values)
    return (query_grad[None], key_grad[None], value_grad[None], filter_grad)


def solution(mesh):
    fine = Mesh(mesh.devices.reshape(2, 4, 4, 2, 4, 2), ("zh", "x", "zl", "co", "yq", "yp"))
    branch = P("zh", CONTEXT, Y)
    return jax.shard_map(
        local,
        mesh=fine,
        in_specs=(
            branch,
            branch,
            branch,
            P("zh", CONTEXT + Y, None),
            P(("zh",) + CONTEXT, Y),
            P(Y, None),
        ),
        out_specs=(branch, branch, branch, P(Y, None)),
        check_vma=False,
    )
```

```python
import math

import jax
import jax.numpy as jnp
from jax import lax
from jax.experimental import pallas as pl
from jax.experimental.pallas import tpu as pltpu
from jax.sharding import Mesh, PartitionSpec as P

GROUP = 16
TAPS = 128
LANES = 128
PER = LANES // GROUP
F32 = jnp.float32
BF16 = jnp.bfloat16

Z = ("zh", "zl")
CONTEXT = ("x", "zl", "co")
Y = ("yq", "yp")
VMEM = pltpu.CompilerParams(vmem_limit_bytes=3 * 1024 * 1024)
PRODUCT_VMEM = pltpu.CompilerParams(vmem_limit_bytes=8 * 1024 * 1024)


def swap(block, axis):
    return lax.ppermute(block, axis, [(0, 1), (1, 0)])


def in_order(mine, theirs, axis):
    first = lax.axis_index(axis) == 0
    return jnp.stack([jnp.where(first, mine, theirs), jnp.where(first, theirs, mine)])


def from_behind(block, distance):
    n = lax.axis_size(CONTEXT)
    route = [(i - distance, i) for i in range(n) if 0 <= i - distance < n]
    return lax.ppermute(block, CONTEXT, route)


def shifted_rows(row):
    return pltpu.roll(jnp.broadcast_to(row, (TAPS, 2 * TAPS)), 0, 1, stride=1, stride_axis=0)


def skewed_sum(rows):
    return jnp.sum(pltpu.roll(rows, 1, 1, stride=1, stride_axis=0), axis=0, keepdims=True)


def lane_group(shape):
    return lax.broadcasted_iota(jnp.int32, shape, 1) >> 4


def filtered(rows, window):
    owner = lane_group((TAPS, LANES))
    total = jnp.zeros((TAPS, LANES), F32)
    for g in range(PER):
        table = shifted_rows(rows[g : g + 1, :]).astype(BF16)
        term = jnp.dot(table, window, preferred_element_type=F32)
        total = jnp.where(owner == g, term, total)
    return total


def antidiagonal(rows, columns, total):
    across = lax.broadcasted_iota(jnp.int32, (rows, columns), 0) + lax.broadcasted_iota(jnp.int32, (rows, columns), 1)
    return (across == total).astype(F32).astype(BF16)


def conv_kernel(filters_ref, before_ref, mixed_ref, conv_ref, turned_ref):
    window = jnp.concatenate([before_ref[...], mixed_ref[...]], 0)
    n = 2 * TAPS
    rows = jnp.dot(filters_ref[...], antidiagonal(TAPS, n, TAPS), preferred_element_type=F32)
    conv_ref[...] = filtered(rows, window)
    turned_ref[...] = jnp.dot(antidiagonal(n, n, n - 1), window, preferred_element_type=F32).astype(BF16)


def mixed_grad_kernel(filters_ref, grad_ref, after_ref, key_ref, value_ref, key_grad_ref, value_grad_ref):
    window = jnp.concatenate([grad_ref[...], after_ref[...]], 0)
    taps = filters_ref[...].astype(F32)
    mixed_grad = filtered(jnp.concatenate([taps, jnp.zeros(taps.shape, F32)], 1), window)
    key_grad_ref[...] = (mixed_grad * value_ref[...].astype(F32)).astype(BF16)
    value_grad_ref[...] = (mixed_grad * key_ref[...].astype(F32)).astype(BF16)


def spread_kernel(cot_ref, out_ref):
    size = cot_ref.shape[1] // 8
    for x in range(4):
        for zh in range(2):
            out_ref[x, 0, :, zh * size : (zh + 1) * size] = cot_ref[:, (4 * zh + x) * size : (4 * zh + x + 1) * size]


def sum_kernel(parts_ref, out_ref):
    total = jnp.sum(parts_ref[...], axis=0)
    for i in range(out_ref.shape[0]):
        out_ref[i] = total


def branch_kernel(terms_ref, conv_ref, query_ref, turned_ref, query_grad_ref, conv_grad_ref, lag_ref):
    branch_grad = terms_ref[0].astype(F32)
    for x in range(1, terms_ref.shape[0]):
        branch_grad = branch_grad + terms_ref[x].astype(F32)
    query_grad_ref[...] = (branch_grad * conv_ref[...]).astype(BF16)
    conv_grad = (branch_grad * query_ref[...].astype(F32)).astype(BF16)
    conv_grad_ref[...] = conv_grad
    owner = lane_group((TAPS, LANES))
    wide = conv_grad.astype(F32)
    for g in range(PER):
        part = jnp.where(owner == g, wide, 0.0).astype(BF16)
        outer = lax.dot_general(part, turned_ref[...], (((1,), (1,)), ((), ())), preferred_element_type=F32)
        sums = skewed_sum(outer)[:, TAPS:]
        for copy in range(lag_ref.shape[0]):
            lag_ref[copy, g : g + 1, :] = sums


def product_kernel(place_ref, cot_ref, *refs):
    count = (len(refs) - 3) // 2
    weights_hbm, out_ref, total_ref, weights, sems = refs[:count], refs[count], refs[count + 1], refs[count + 2 : -1], refs[-1]
    copies = [pltpu.make_async_copy(weights_hbm[i], weights[i], sems.at[i]) for i in range(count)]
    for copy in copies:
        copy.start()
    z, core = place_ref[0], place_ref[1]
    depth = weights[0].shape[0]
    below, above = [lax.rem(z + 8 - i, 8) for i in range(4)], [lax.rem(z + i, 8) for i in range(4)]
    mine = [jnp.where(core == 0, b, a) for b, a in zip(below, above)]
    theirs = [jnp.where(core == 0, a, b) for b, a in zip(below, above)]
    pieces = [(0, 0, z), (1, 0, mine[1]), (2, 0, theirs[1]), (3, 0, lax.rem(z + 4, 8))]
    pieces += [(4, 0, mine[2]), (4, depth, mine[3]), (5, 0, theirs[2]), (5, depth, theirs[3])]
    for n, (i, offset, place) in enumerate(pieces):
        if offset == 0:
            copies[i].wait()
        weight = weights[i][offset : offset + depth, :]
        columns = pl.ds(pl.multiple_of(place * depth, LANES), depth)
        for x in range(4):
            term = jnp.dot(cot_ref[x * TAPS : (x + 1) * TAPS, columns], weight, preferred_element_type=F32)
            if n:
                term = total_ref[x] + term
            if n < len(pieces) - 1:
                total_ref[x] = term
            else:
                out_ref[x] = term.astype(BF16)


def lane_blocks(*lead):
    return pl.BlockSpec(lead + (LANES,), lambda l: (0,) * len(lead) + (l,))


FILTER_BLOCK = pl.BlockSpec((PER, TAPS), lambda l: (l, 0))


def spread(cotangent):
    rows, width = cotangent.shape
    return pl.pallas_call(
        spread_kernel,
        grid=(8,),
        in_specs=[pl.BlockSpec((rows, width), lambda i: (0, 0))],
        out_specs=pl.BlockSpec((4, 1, rows, width // 4), lambda i: (0, i, 0, 0)),
        out_shape=jax.ShapeDtypeStruct((4, 8, rows, width // 4), cotangent.dtype),
        compiler_params=VMEM,
        name="spread",
    )(cotangent)


def summed_copies(parts):
    return pl.pallas_call(
        sum_kernel,
        out_shape=jax.ShapeDtypeStruct(parts.shape, parts.dtype),
        compiler_params=VMEM,
        name="sums",
    )(parts)


def convolve(filters, before, mixed):
    width = mixed.shape[1]
    tile = lane_blocks(TAPS)
    return pl.pallas_call(
        conv_kernel,
        grid=(width // LANES,),
        in_specs=[FILTER_BLOCK, tile, tile],
        out_specs=[tile, lane_blocks(2 * TAPS)],
        out_shape=[jax.ShapeDtypeStruct((TAPS, width), F32), jax.ShapeDtypeStruct((2 * TAPS, width), BF16)],
        compiler_params=VMEM,
        name="conv",
    )(filters, before, mixed)


def mixed_gradient(filters, grad, after, keys, values):
    width = grad.shape[1]
    tile = lane_blocks(TAPS)
    return pl.pallas_call(
        mixed_grad_kernel,
        grid=(width // LANES,),
        in_specs=[FILTER_BLOCK, tile, tile, tile, tile],
        out_specs=[tile, tile],
        out_shape=[jax.ShapeDtypeStruct((TAPS, width), BF16)] * 2,
        compiler_params=VMEM,
        name="mixed_grad",
    )(filters, grad, after, keys, values)


def branch_gradients(terms, conv, query, turned):
    width = query.shape[1]
    tile = lane_blocks(TAPS)
    return pl.pallas_call(
        branch_kernel,
        grid=(width // LANES,),
        in_specs=[lane_blocks(terms.shape[0], TAPS), tile, tile, lane_blocks(2 * TAPS)],
        out_specs=[tile, tile, pl.BlockSpec((8, PER, TAPS), lambda l: (0, l, 0))],
        out_shape=[jax.ShapeDtypeStruct((TAPS, width), BF16)] * 2
        + [jax.ShapeDtypeStruct((8, width // GROUP, TAPS), F32)],
        compiler_params=VMEM,
        name="branch",
    )(terms, conv, query, turned)


def partial_products(cotangent, weights):
    width = weights[0].shape[1]
    place = jnp.stack([lax.axis_index(Z), lax.axis_index("co")]).astype(jnp.int32)
    whole = pl.BlockSpec(memory_space=pltpu.VMEM)
    return pl.pallas_call(
        product_kernel,
        in_specs=[pl.BlockSpec(memory_space=pltpu.SMEM), whole]
        + [pl.BlockSpec(memory_space=pltpu.HBM)] * len(weights),
        out_specs=whole,
        out_shape=jax.ShapeDtypeStruct((4, TAPS, width), BF16),
        scratch_shapes=[pltpu.VMEM((4, TAPS, width), F32)]
        + [pltpu.VMEM(a.shape, a.dtype) for a in weights]
        + [pltpu.SemaphoreType.DMA((len(weights),))],
        compiler_params=PRODUCT_VMEM,
        name="product",
    )(place, cotangent, *weights)


def exchange(copies, axes):
    return lax.all_to_all(copies, axes, split_axis=0, concat_axis=0)


def after_these(value, *others):
    return lax.optimization_barrier((value,) + others)[0]


def along_z(block, steps):
    n = lax.axis_size(Z)
    route = [(2 * i, 2 * ((i + steps) % n)) for i in range(n)]
    route += [(2 * i + 1, 2 * ((i - steps) % n) + 1) for i in range(n)]
    return lax.ppermute(block, Z + ("co",), route)


def local(query_branch, key_branch, value_branch, cotangent, out_weight, filters):
    query, keys, values = query_branch[0], key_branch[0], value_branch[0]
    tokens, width = query.shape
    chip = in_order(out_weight, swap(out_weight, "co"), "co").reshape(2 * out_weight.shape[0], width)
    copies = spread(cotangent[0])
    gathered = exchange(copies.reshape((32,) + copies.shape[2:]), ("x",) + Y).reshape(4 * TAPS, -1)

    one, four = along_z(chip, 1), along_z(chip, 4)
    keys = after_these(keys, four)
    mixed = (keys.astype(F32) * values.astype(F32)).astype(BF16)
    before = from_behind(mixed, 1)
    pair = along_z(jnp.concatenate([chip, one], 0), 2)
    other = swap(one, "co")
    pair = after_these(pair, other, before)
    weights = [chip, one, other, four, pair, swap(pair, "co")]
    gathered = after_these(gathered, *weights)
    partial = partial_products(gathered, weights)
    terms = exchange(partial, "x")
    conv, turned = convolve(filters, after_these(before, partial), mixed)
    query_grad, conv_grad, lags = branch_gradients(terms, conv, query, turned)
    lags = summed_copies(exchange(lags, ("x", "co")))
    after = from_behind(after_these(conv_grad, lags), -1)
    scale = 1.0 / math.sqrt(2 * lax.axis_size(CONTEXT) * tokens * GROUP)
    filter_grad = jnp.sum(exchange(lags, Z), axis=0) * scale
    key_grad, value_grad = mixed_gradient(filters, conv_grad, after, keys, values)
    return (query_grad[None], key_grad[None], value_grad[None], filter_grad)


def solution(mesh):
    fine = Mesh(mesh.devices.reshape(2, 4, 4, 2, 4, 2), ("zh", "x", "zl", "co", "yq", "yp"))
    branch = P("zh", CONTEXT, Y)
    return jax.shard_map(
        local,
        mesh=fine,
        in_specs=(
            branch,
            branch,
            branch,
            P("zh", CONTEXT + Y, None),
            P(("zh",) + CONTEXT, Y),
            P(Y, None),
        ),
        out_specs=(branch, branch, branch, P(Y, None)),
        check_vma=False,
    )
```

```python
import math

import jax
import jax.numpy as jnp
from jax import lax
from jax.experimental import pallas as pl
from jax.experimental.pallas import tpu as pltpu
from jax.sharding import Mesh, PartitionSpec as P

GROUP = 16
TAPS = 128
LANES = 128
PER = LANES // GROUP
F32 = jnp.float32
BF16 = jnp.bfloat16

Z = ("zh", "zl")
CONTEXT = ("x", "zl", "co")
Y = ("yq", "yp")
VMEM = pltpu.CompilerParams(vmem_limit_bytes=8 * 1024 * 1024)


def swap(block, axis):
    return lax.ppermute(block, axis, [(0, 1), (1, 0)])


def in_order(mine, theirs, axis):
    first = lax.axis_index(axis) == 0
    return jnp.stack([jnp.where(first, mine, theirs), jnp.where(first, theirs, mine)])


def from_behind(block, distance):
    n = lax.axis_size(CONTEXT)
    route = [(i - distance, i) for i in range(n) if 0 <= i - distance < n]
    return lax.ppermute(block, CONTEXT, route)


def shifted_rows(row):
    return pltpu.roll(jnp.broadcast_to(row, (TAPS, 2 * TAPS)), 0, 1, stride=1, stride_axis=0)


def skewed_sum(rows):
    return jnp.sum(pltpu.roll(rows, 1, 1, stride=1, stride_axis=0), axis=0, keepdims=True)


def lane_group(shape):
    return lax.broadcasted_iota(jnp.int32, shape, 1) >> 4


def filtered(rows, window):
    owner = lane_group((TAPS, LANES))
    total = jnp.zeros((TAPS, LANES), F32)
    for g in range(PER):
        table = shifted_rows(rows[g : g + 1, :]).astype(BF16)
        term = jnp.dot(table, window, preferred_element_type=F32)
        total = jnp.where(owner == g, term, total)
    return total


def antidiagonal(rows, columns, total):
    across = lax.broadcasted_iota(jnp.int32, (rows, columns), 0) + lax.broadcasted_iota(jnp.int32, (rows, columns), 1)
    return (across == total).astype(F32).astype(BF16)


def conv_kernel(filters_ref, before_ref, mixed_ref, conv_ref, turned_ref):
    window = jnp.concatenate([before_ref[...], mixed_ref[...]], 0)
    n = 2 * TAPS
    rows = jnp.dot(filters_ref[...], antidiagonal(TAPS, n, TAPS), preferred_element_type=F32)
    conv_ref[...] = filtered(rows, window)
    turned_ref[...] = jnp.dot(antidiagonal(n, n, n - 1), window, preferred_element_type=F32).astype(BF16)


def mixed_grad_kernel(filters_ref, grad_ref, after_ref, key_ref, value_ref, key_grad_ref, value_grad_ref):
    window = jnp.concatenate([grad_ref[...], after_ref[...]], 0)
    taps = filters_ref[...].astype(F32)
    mixed_grad = filtered(jnp.concatenate([taps, jnp.zeros(taps.shape, F32)], 1), window)
    key_grad_ref[...] = (mixed_grad * value_ref[...].astype(F32)).astype(BF16)
    value_grad_ref[...] = (mixed_grad * key_ref[...].astype(F32)).astype(BF16)


def spread_kernel(cot_ref, out_ref):
    size = cot_ref.shape[1] // 8
    for x in range(4):
        for zh in range(2):
            out_ref[x, 0, :, zh * size : (zh + 1) * size] = cot_ref[:, (4 * zh + x) * size : (4 * zh + x + 1) * size]


def sum_kernel(parts_ref, out_ref):
    total = jnp.sum(parts_ref[...], axis=0)
    for i in range(out_ref.shape[0]):
        out_ref[i] = total


def branch_kernel(terms_ref, conv_ref, query_ref, turned_ref, query_grad_ref, conv_grad_ref, lag_ref):
    branch_grad = terms_ref[0].astype(F32)
    for x in range(1, terms_ref.shape[0]):
        branch_grad = branch_grad + terms_ref[x].astype(F32)
    query_grad_ref[...] = (branch_grad * conv_ref[...]).astype(BF16)
    conv_grad = (branch_grad * query_ref[...].astype(F32)).astype(BF16)
    conv_grad_ref[...] = conv_grad
    owner = lane_group((TAPS, LANES))
    wide = conv_grad.astype(F32)
    for g in range(PER):
        part = jnp.where(owner == g, wide, 0.0).astype(BF16)
        outer = lax.dot_general(part, turned_ref[...], (((1,), (1,)), ((), ())), preferred_element_type=F32)
        sums = skewed_sum(outer)[:, TAPS:]
        for copy in range(lag_ref.shape[0]):
            lag_ref[copy, g : g + 1, :] = sums


def product_kernel(place_ref, own_ref, low_ref, high_ref, *refs):
    count = (len(refs) - 3) // 2
    weights_hbm, out_ref, total_ref, weights, sems = refs[:count], refs[count], refs[count + 1], refs[count + 2 : -1], refs[-1]
    copies = [pltpu.make_async_copy(weights_hbm[i], weights[i], sems.at[i]) for i in range(count)]
    for copy in copies:
        copy.start()
    z, core, odd = place_ref[0], place_ref[1], place_ref[2]
    depth = weights[0].shape[0]
    below, above = [lax.rem(z + 8 - i, 8) for i in range(4)], [lax.rem(z + i, 8) for i in range(4)]
    mine = [jnp.where(core == 0, b, a) for b, a in zip(below, above)]
    theirs = [jnp.where(core == 0, a, b) for b, a in zip(below, above)]
    pieces = [(0, 0, z), (1, 0, mine[1]), (2, 0, theirs[1]), (3, 0, lax.rem(z + 4, 8))]
    pieces += [(4, 0, mine[2]), (4, depth, mine[3]), (5, 0, theirs[2]), (5, depth, theirs[3])]
    half = own_ref.shape[0] // 2
    parts = ((own_ref, 0), (own_ref, half), (low_ref, 0), (high_ref, 0))
    for n, (i, offset, place) in enumerate(pieces):
        if offset == 0:
            copies[i].wait()
        weight = weights[i][offset : offset + depth, :]
        columns = pl.ds(pl.multiple_of(place * depth, LANES), depth)
        for j, (cot_ref, first) in enumerate(parts):
            term = jnp.dot(cot_ref[first : first + half, columns], weight, preferred_element_type=F32)
            if n:
                term = total_ref[j] + term
            if n < len(pieces) - 1:
                total_ref[j] = term
                continue
            term = term.astype(BF16).reshape(2, 4, 16, term.shape[1])
            for x in range(2):
                for pair in range(4):
                    out_ref[2 * (j % 2) + x, pair, odd if j < 2 else 1 - odd] = term[x, pair]


def lane_blocks(*lead):
    return pl.BlockSpec(lead + (LANES,), lambda l: (0,) * len(lead) + (l,))


FILTER_BLOCK = pl.BlockSpec((PER, TAPS), lambda l: (l, 0))


def spread(cotangent):
    rows, width = cotangent.shape
    return pl.pallas_call(
        spread_kernel,
        grid=(4,),
        in_specs=[pl.BlockSpec((rows, width), lambda i: (0, 0))],
        out_specs=pl.BlockSpec((4, 1, rows, width // 4), lambda i: (0, i, 0, 0)),
        out_shape=jax.ShapeDtypeStruct((4, 4, rows, width // 4), cotangent.dtype),
        compiler_params=VMEM,
        name="spread",
    )(cotangent)


def summed_copies(parts):
    return pl.pallas_call(
        sum_kernel,
        out_shape=jax.ShapeDtypeStruct(parts.shape, parts.dtype),
        compiler_params=VMEM,
        name="sums",
    )(parts)


def convolve(filters, before, mixed):
    width = mixed.shape[1]
    tile = lane_blocks(TAPS)
    return pl.pallas_call(
        conv_kernel,
        grid=(width // LANES,),
        in_specs=[FILTER_BLOCK, tile, tile],
        out_specs=[tile, lane_blocks(2 * TAPS)],
        out_shape=[jax.ShapeDtypeStruct((TAPS, width), F32), jax.ShapeDtypeStruct((2 * TAPS, width), BF16)],
        compiler_params=VMEM,
        name="conv",
    )(filters, before, mixed)


def mixed_gradient(filters, grad, after, keys, values):
    width = grad.shape[1]
    tile = lane_blocks(TAPS)
    return pl.pallas_call(
        mixed_grad_kernel,
        grid=(width // LANES,),
        in_specs=[FILTER_BLOCK, tile, tile, tile, tile],
        out_specs=[tile, tile],
        out_shape=[jax.ShapeDtypeStruct((TAPS, width), BF16)] * 2,
        compiler_params=VMEM,
        name="mixed_grad",
    )(filters, grad, after, keys, values)


def branch_gradients(terms, conv, query, turned):
    width = query.shape[1]
    tile = lane_blocks(TAPS)
    return pl.pallas_call(
        branch_kernel,
        grid=(width // LANES,),
        in_specs=[lane_blocks(terms.shape[0], TAPS), tile, tile, lane_blocks(2 * TAPS)],
        out_specs=[tile, tile, pl.BlockSpec((8, PER, TAPS), lambda l: (0, l, 0))],
        out_shape=[jax.ShapeDtypeStruct((TAPS, width), BF16)] * 2
        + [jax.ShapeDtypeStruct((8, width // GROUP, TAPS), F32)],
        compiler_params=VMEM,
        name="branch",
    )(terms, conv, query, turned)


def partial_products(parts, weights):
    width = weights[0].shape[1]
    place = jnp.stack([lax.axis_index(Z), lax.axis_index("co"), lax.axis_index("yp")]).astype(jnp.int32)
    whole = pl.BlockSpec(memory_space=pltpu.VMEM)
    out = pl.pallas_call(
        product_kernel,
        in_specs=[pl.BlockSpec(memory_space=pltpu.SMEM)]
        + [whole] * 3
        + [pl.BlockSpec(memory_space=pltpu.HBM)] * len(weights),
        out_specs=whole,
        out_shape=jax.ShapeDtypeStruct((4, 4, 2, 16, width), BF16),
        scratch_shapes=[pltpu.VMEM((4, TAPS, width), F32)]
        + [pltpu.VMEM(a.shape, a.dtype) for a in weights]
        + [pltpu.SemaphoreType.DMA((len(weights),))],
        compiler_params=VMEM,
        name="product",
    )(place, *parts, *weights)
    return out.reshape(4, TAPS, width)


def exchange(copies, axes):
    return lax.all_to_all(copies, axes, split_axis=0, concat_axis=0)


def ahead(block, axes, distance):
    n = lax.axis_size(axes)
    return lax.ppermute(block, axes, [((i + distance) % n, i) for i in range(n)])


def along_z(block, steps):
    n = lax.axis_size(Z)
    route = [(2 * i, 2 * ((i + steps) % n)) for i in range(n)]
    route += [(2 * i + 1, 2 * ((i - steps) % n) + 1) for i in range(n)]
    return lax.ppermute(block, Z + ("co",), route)


def weight_blocks(chip):
    one, four = along_z(chip, 1), along_z(chip, 4)
    pair = along_z(jnp.concatenate([chip, one], 0), 2)
    return [chip, one, swap(one, "co"), four, pair, swap(pair, "co")]


def local(query_branch, key_branch, value_branch, cotangent, out_weight, filters):
    query, keys, values = query_branch[0], key_branch[0], value_branch[0]
    tokens, width = query.shape
    chip = in_order(out_weight, swap(out_weight, "co"), "co").reshape(2 * out_weight.shape[0], width)
    weights = weight_blocks(chip)

    copies = spread(cotangent[0])
    rows, columns = copies.shape[2:]
    own = exchange(copies.reshape(16, rows, columns), ("x", "yq"))
    own, weights[2], weights[3] = lax.optimization_barrier((own, weights[2], weights[3]))
    low, high = ahead(own[:8], Y, -1), ahead(own[8:], Y, 1)
    parts = [part.reshape(-1, columns) for part in (own, low, high)]

    keys, values, own = lax.optimization_barrier((keys, values, own))
    mixed = (keys.astype(F32) * values.astype(F32)).astype(BF16)
    parts, before = lax.optimization_barrier((parts, from_behind(mixed, 1)))
    terms = exchange(partial_products(parts, weights), "x")
    conv, turned = convolve(filters, before, mixed)
    query_grad, conv_grad, lags = branch_gradients(terms, conv, query, turned)
    lags = summed_copies(exchange(lags, ("x", "co")))
    tied_grad, _ = lax.optimization_barrier((conv_grad, lags))
    after = from_behind(tied_grad, -1)
    scale = 1.0 / math.sqrt(2 * lax.axis_size(CONTEXT) * tokens * GROUP)
    filter_grad = jnp.sum(exchange(lags, Z), axis=0) * scale
    key_grad, value_grad = mixed_gradient(filters, conv_grad, after, keys, values)
    return (query_grad[None], key_grad[None], value_grad[None], filter_grad)


def solution(mesh):
    fine = Mesh(mesh.devices.reshape(2, 4, 4, 2, 4, 2), ("zh", "x", "zl", "co", "yq", "yp"))
    branch = P("zh", CONTEXT, Y)
    return jax.shard_map(
        local,
        mesh=fine,
        in_specs=(
            branch,
            branch,
            branch,
            P("zh", CONTEXT + Y, None),
            P(("zh",) + CONTEXT, Y),
            P(Y, None),
        ),
        out_specs=(branch, branch, branch, P(Y, None)),
        check_vma=False,
    )
```
